128 devices in a mesh: ctx: 32 (over y, x_hi, z), tp: 4 (over x_lo, core).
Axes of the slice: x: 4 (x_hi: 2, x_lo: 2; x = x_hi * 2 + x_lo), y: 4, z: 4, core: 2. Of those that a mesh axis runs over, the one named last changes fastest.
Arguments:
- layer_input: bfloat16 [1, 4096, 768], P(None, 'ctx'), may hold values from -6 to 6
- attention_gain: bfloat16 [2, 768], replicated, may hold values from 0.5 to 1.5
- attention_shift: bfloat16 [2, 768], replicated, may hold values from -3 to 3
- feedforward_gain: bfloat16 [2, 768], replicated, may hold values from 0.5 to 1.5
- feedforward_shift: bfloat16 [2, 768], replicated, may hold values from -3 to 3
- query_key_value_weight: bfloat16 [2, 768, 3, 768], P(None, None, None, 'tp'), may hold values from -0.21875 to 0.21875
- query_key_value_bias: bfloat16 [2, 3, 768], P(None, None, 'tp'), may hold values from -2 to 2
- attention_out_weight: bfloat16 [2, 768, 768], P(None, 'tp'), may hold values from -1.75 to 1.75
- dense_bias: bfloat16 [2, 768], replicated, may hold values from -3 to 3
- expand_weight: bfloat16 [2, 768, 3072], P(None, None, 'tp'), may hold values from -0.21875 to 0.21875
- expand_bias: bfloat16 [2, 3072], P(None, 'tp'), may hold values from -3 to 3
- down_weight: bfloat16 [2, 3072, 768], P(None, 'tp'), may hold values from -0.109375 to 0.109375
- down_bias: bfloat16 [2, 768], replicated, may hold values from -3 to 3
- output_grad: bfloat16 [1, 4096, 768], P(None, 'ctx'), may hold values from -6 to 6
Outputs:
- output: bfloat16 [1, 4096, 768], P(None, 'ctx')
- input_grad: float32 [1, 4096, 768], P(None, 'ctx')
- attention_gain_grad: float32 [2, 768], replicated
- attention_shift_grad: float32 [2, 768], replicated
- feedforward_gain_grad: float32 [2, 768], replicated
- feedforward_shift_grad: float32 [2, 768], replicated
- merged_weight_grad: float32 [2, 768, 3, 768], P(None, None, None, 'tp')
- merged_bias_grad: float32 [2, 3, 768], P(None, None, 'tp')
- dense_weight_grad: float32 [2, 768, 768], P(None, 'tp')
- dense_bias_grad: float32 [2, 768], replicated
- up_weight_grad: float32 [2, 768, 3072], P(None, None, 'tp')
- up_bias_grad: float32 [2, 3072], P(None, 'tp')
- down_weight_grad: float32 [2, 3072, 768], P(None, 'tp')
- down_bias_grad: float32 [2, 768], replicated
The draws below stay inside these ranges and needn't reach their ends.
All inputs are finite; a program needn't handle non-finite values.
Results may differ from the reference program's by a relative error of at most 0.025.
Values may be sent and summed in bfloat16 or wider, within the bound.
A program may use at most 128 MiB of HBM per device.

```python
import math
import jax
import jax.numpy as jnp
from jax import lax

D = 768
H = 12
HD = 64
FF = 3072
ROT = 16
LAYERS = 2
SEQS = 1
LENGTH = 4096


def strengthened(array, own_key, source, target, parts, factor):
    def block_of(axis_at):
        return (jnp.arange(array.shape[axis_at]) // (array.shape[axis_at] // parts)).reshape((-1,) + (1,) * (array.ndim - 1 - axis_at))

    one_side = jax.random.permutation(own_key, parts)[block_of(target)]
    other_side = (block_of(target) + parts // 2) % parts
    return jnp.where((block_of(source) == one_side) | (block_of(source) == other_side), factor * array, array)


def levels(rng, dims, shards, least, top_value):
    level = 1.0
    for axis_at, shards_of in shards:
        steps = jax.random.uniform(jax.random.fold_in(jax.random.fold_in(rng, 6), axis_at), (shards_of,), jnp.float32, least / len(shards), top_value / len(shards))
        level = level * jnp.repeat(jnp.exp(steps), dims[axis_at] // shards_of).reshape((-1,) + (1,) * (len(dims) - 1 - axis_at))
    return level


def scatter_about(key, dims, scale, reach, pieces=(), kind=jnp.bfloat16):
    entries = jax.random.normal(key, dims, jnp.float32) * scale
    if len(pieces) > 0:
        entries = levels(key, dims, pieces, -0.22, 0.18) * entries
    return jnp.clip(entries, min=-reach, max=reach).astype(kind)


def gaussian_with(stream_key, dims, deviation, limit, cuts, heavy, held_as=jnp.bfloat16):
    values = deviation * jax.random.normal(stream_key, dims, jnp.float32)
    if cuts:
        values = values * levels(stream_key, dims, cuts, -0.22, 0.18)
    return jnp.clip(strengthened(values, jax.random.fold_in(stream_key, 3), *heavy), -limit, limit).astype(held_as)


def setup_inputs(seed: int = 0) -> dict:
    key_list = jax.random.split(jax.random.key(seed), 15)
    layer_input = scatter_about(key_list[0], (SEQS, LENGTH, D), 1.0, 6.0, ((1, 32),))
    attention_gain = jnp.clip(1.0 + 0.1 * jax.random.normal(key_list[1], (LAYERS, D), jnp.float32), 0.5, 1.5).astype(jnp.bfloat16)
    attention_shift = scatter_about(key_list[2], (LAYERS, D), 0.5, 3.0)
    feedforward_gain = jnp.clip(1.0 + 0.1 * jax.random.normal(key_list[3], (LAYERS, D), jnp.float32), 0.5, 1.5).astype(jnp.bfloat16)
    feedforward_shift = scatter_about(key_list[4], (LAYERS, D), 0.5, 3.0)
    query_key_value_weight = scatter_about(key_list[5], (LAYERS, D, 3, D), D ** -0.5, 0.21875, ((3, 4),))
    query_key_value_bias = scatter_about(key_list[6], (LAYERS, 3, D), 0.3, 2.0, ((2, 4),))
    attention_out_weight = scatter_about(key_list[7], (LAYERS, D, D), (D // 64) ** -0.5, 1.75, ((1, 4),))
    dense_bias = scatter_about(key_list[8], (LAYERS, D), 0.5, 3.0)
    expand_weight = scatter_about(key_list[9], (LAYERS, D, FF), D ** -0.5, 0.21875, ((2, 4),))
    expand_bias = scatter_about(key_list[10], (LAYERS, FF), 0.5, 3.0, ((1, 4),))
    down_weight = scatter_about(key_list[11], (LAYERS, FF, D), FF ** -0.5, 0.109375, ((1, 4),))
    down_bias = scatter_about(key_list[12], (LAYERS, D), 0.5, 3.0)
    output_grad = gaussian_with(key_list[13], (SEQS, LENGTH, D), 1.0, 6.0, ((1, 32),), (1, 2, 32, 2.75))
    return dict(layer_input=layer_input, attention_gain=attention_gain, attention_shift=attention_shift, feedforward_gain=feedforward_gain, feedforward_shift=feedforward_shift, query_key_value_weight=query_key_value_weight, query_key_value_bias=query_key_value_bias, attention_out_weight=attention_out_weight, dense_bias=dense_bias, expand_weight=expand_weight, expand_bias=expand_bias, down_weight=down_weight, down_bias=down_bias, output_grad=output_grad)


NORM_EPSILON = 1e-05
MASKED_SCORE = -1e+30
MATMUL_EXACTNESS = lax.Precision.HIGHEST

@jax.custom_vjp
def low(v):
    return lax.optimization_barrier(v.astype(jnp.bfloat16)).astype(jnp.float32)

@jax.custom_vjp
def low_back(v):
    return v

def low_keep(v):
    return (low(v), None)

def low_pass(kept, grad):
    return (grad,)

def back_keep(v):
    return (v, None)

def back_low(kept, grad):
    return (low(grad),)
low.defvjp(low_keep, low_pass)
low_back.defvjp(back_keep, back_low)

def layer_norm(values, gain, shift):
    mean_value = lax.optimization_barrier(jnp.mean(values, axis=-1, keepdims=True))
    centred = values - mean_value
    variance = lax.optimization_barrier(jnp.mean(centred * centred, axis=-1, keepdims=True))
    return centred * lax.rsqrt(variance + NORM_EPSILON) * gain + shift

def rotary_tables(positions):
    halves = ROT // 2
    inverse = jnp.power(10000.0, -2.0 * jnp.arange(halves, dtype=jnp.float32) / ROT)
    angles = positions[:, None] * inverse[None, :]
    return (jnp.cos(angles), jnp.sin(angles))

def rotate(values, cosine, sine):
    halves = cosine.shape[-1]
    leading = values[..., :halves]
    trailing = values[..., halves:2 * halves]
    others = values[..., 2 * halves:]
    cos_wide = cosine[:, None, :]
    sin_wide = sine[:, None, :]
    return jnp.concatenate([leading * cos_wide - trailing * sin_wide, trailing * cos_wide + leading * sin_wide, others], axis=-1)

def attend(queries, keys, values):
    batch, length = (queries.shape[0], queries.shape[1])
    block = math.gcd(512, length)
    count = length // block
    scale = HD ** (-0.5)
    key_pos = jnp.arange(length, dtype=jnp.int32)
    grouped = queries.reshape(batch, count, block, H, HD).transpose(1, 0, 2, 3, 4)
    starts = jnp.arange(count, dtype=jnp.int32) * block

    def one_block(inputs):
        part, start = inputs
        scores = low_back(jnp.einsum('sqhd,skhd->shqk', part, keys, precision=MATMUL_EXACTNESS) * scale)
        query_pos = start + jnp.arange(block, dtype=jnp.int32)
        allowed = key_pos[None, :] <= query_pos[:, None]
        scores = jnp.where(allowed, scores, MASKED_SCORE)
        probs = low(jax.nn.softmax(scores, axis=-1))
        return jnp.einsum('shqk,skhd->sqhd', probs, values, precision=MATMUL_EXACTNESS)
    outputs = lax.map(jax.checkpoint(one_block), (grouped, starts))
    return outputs.transpose(1, 0, 2, 3, 4).reshape(batch, length, H, HD)

def layer_forward(residual, weights, cosine, sine):
    attention_gain, attention_shift, feedforward_gain, feedforward_shift, query_key_value_weight, query_key_value_bias, attention_out_weight, dense_bias, expand_weight, expand_bias, down_weight, down_bias = weights
    batch, length, width = residual.shape
    first_normalized = low(layer_norm(residual, attention_gain, attention_shift))
    merged_projection = low_back(jnp.einsum('zmu,uqx->zmqx', first_normalized, query_key_value_weight, precision=MATMUL_EXACTNESS) + query_key_value_bias)
    queries = low(rotate(merged_projection[:, :, 0].reshape(batch, length, H, HD), cosine, sine))
    keys = low(rotate(merged_projection[:, :, 1].reshape(batch, length, H, HD), cosine, sine))
    values = low(merged_projection[:, :, 2].reshape(batch, length, H, HD))
    attention_mixture = attend(queries, keys, values).reshape(batch, length, width)
    attention_mixture = low(low_back(attention_mixture))
    second_normalized = low(layer_norm(residual, feedforward_gain, feedforward_shift))
    hidden_before_gelu = low_back(jnp.einsum('zip,pg->zig', second_normalized, expand_weight, precision=MATMUL_EXACTNESS) + expand_bias)
    hidden = low(jax.nn.gelu(hidden_before_gelu, approximate=False))
    branch_output = jnp.einsum('koc,ca->koa', attention_mixture, attention_out_weight, precision=MATMUL_EXACTNESS)
    branch_output = low_back(branch_output + jnp.einsum('slf,fe->sle', hidden, down_weight, precision=MATMUL_EXACTNESS))
    return residual + branch_output + dense_bias + down_bias

def reference(layer_input, attention_gain, attention_shift, feedforward_gain, feedforward_shift, query_key_value_weight, query_key_value_bias, attention_out_weight, dense_bias, expand_weight, expand_bias, down_weight, down_bias, output_grad):
    weights = tuple((entry.astype(jnp.float32) for entry in (attention_gain, attention_shift, feedforward_gain, feedforward_shift, query_key_value_weight, query_key_value_bias, attention_out_weight, dense_bias, expand_weight, expand_bias, down_weight, down_bias)))
    positions = jnp.arange(LENGTH, dtype=jnp.int32).astype(jnp.float32)
    cosine, sine = rotary_tables(positions)

    def network(values, stacked):
        residual = values
        for layer_index in range(LAYERS):
            residual = layer_forward(residual, tuple((entry[layer_index] for entry in stacked)), cosine, sine)
        return residual
    result, backward = jax.vjp(network, layer_input.astype(jnp.float32), weights)
    input_grad, weight_grads = backward(output_grad.astype(jnp.float32))
    return (result.astype(jnp.bfloat16), input_grad, weight_grads[0], weight_grads[1], weight_grads[2], weight_grads[3], weight_grads[4], weight_grads[5], weight_grads[6], weight_grads[7], weight_grads[8], weight_grads[9], weight_grads[10], weight_grads[11])
```

```python
import functools
import math

import jax
import jax.numpy as jnp
from jax import lax
from jax.experimental import pallas as pl
from jax.experimental.pallas import tpu as pltpu
from jax.sharding import PartitionSpec as P

HD = 64
ROT = 16
LAYERS = 2
NORM_EPSILON = 1e-05
MASKED = -1e30
F32 = jnp.float32
BF16 = jnp.bfloat16
ROWS = 128
D = 768
HEADS = 3
CTX = 32
TP = 4
CHUNK = 512
PER = CHUNK // ROWS
QUARTER = ROWS // TP
SCALE = HD**-0.5
G1, S1, G2, S2, BUP, BOUT, BQKV = range(7)
QKV_ROWS, OUT_ROWS, UP_ROWS, DOWN_ROWS = 576, 192, 768, 768
GRAD_ROWS = QKV_ROWS + OUT_ROWS + UP_ROWS + DOWN_ROWS

NN = (((1,), (0,)), ((), ()))
NT = (((1,), (1,)), ((), ()))
TN = (((0,), (0,)), ((), ()))


def dot(a, b, dims=NN):
    return lax.dot_general(a, b, dims, preferred_element_type=F32)


def remote(src, dst, send, recv, ctx=None, tp=None):
    where = {}
    if ctx is not None:
        where["ctx"] = ctx
    if tp is not None:
        where["tp"] = tp
    return pltpu.make_async_remote_copy(
        src_ref=src,
        dst_ref=dst,
        send_sem=send,
        recv_sem=recv,
        device_id=where,
        device_id_type=pl.DeviceIdType.MESH,
    )


def greet(ctx_peers, tp_peers):
    barrier = pltpu.get_barrier_semaphore()
    for peer in ctx_peers:
        pl.semaphore_signal(
            barrier, inc=1, device_id={"ctx": peer}, device_id_type=pl.DeviceIdType.MESH
        )
    for peer in tp_peers:
        pl.semaphore_signal(
            barrier, inc=1, device_id={"tp": peer}, device_id_type=pl.DeviceIdType.MESH
        )
    return barrier, len(ctx_peers) + len(tp_peers)


def greet_all(me, my_tp):
    barrier = pltpu.get_barrier_semaphore()

    @pl.loop(1, CTX)
    def _(step):
        pl.semaphore_signal(
            barrier,
            inc=1,
            device_id={"ctx": lax.rem(me + step, CTX)},
            device_id_type=pl.DeviceIdType.MESH,
        )

    for step in range(1, TP):
        pl.semaphore_signal(
            barrier,
            inc=1,
            device_id={"tp": lax.rem(my_tp + step, TP)},
            device_id_type=pl.DeviceIdType.MESH,
        )
    return barrier


def centre(residual):
    mean_value = jnp.mean(residual, axis=-1, keepdims=True)
    centred = residual - mean_value
    variance = jnp.mean(centred * centred, axis=-1, keepdims=True)
    inverse = lax.rsqrt(variance + NORM_EPSILON)
    return centred * inverse, inverse


def turn(values, rot_ref, sign):
    width = values.shape[1]
    count = width // 128
    cosine = jnp.concatenate([rot_ref[0]] * count, axis=1)
    after = jnp.concatenate([rot_ref[1]] * count, axis=1)
    before = jnp.concatenate([rot_ref[2]] * count, axis=1)
    turned = pltpu.roll(values, 8, 1) * after + pltpu.roll(values, width - 8, 1) * before
    return values * cosine + sign * turned


def tp_sum(part, my_tp, buffers, sems):
    mine, out, slots, gathered = buffers
    send, recv = sems
    mine[...] = part
    out[...] = part.astype(BF16)
    own = pl.ds(pl.multiple_of(my_tp * QUARTER, QUARTER), QUARTER)
    copies = []
    for step in range(1, TP):
        peer = lax.rem(my_tp + step, TP)
        rows = pl.ds(pl.multiple_of(peer * QUARTER, QUARTER), QUARTER)
        copy = remote(
            out.at[rows], slots.at[step - 1], send.at[step - 1], recv.at[step - 1], tp=peer
        )
        copy.start()
        copies.append(copy)
    total = mine[own, :]
    for step in range(1, TP):
        copies[step - 1].wait_recv()
        total = total + slots[step - 1].astype(F32)
    gathered[own, :] = total.astype(BF16)
    for step in range(1, TP):
        peer = lax.rem(my_tp + step, TP)
        copy = remote(
            gathered.at[own],
            gathered.at[own],
            send.at[TP - 2 + step],
            recv.at[TP - 2 + step],
            tp=peer,
        )
        copy.start()
        copies.append(copy)
    for step in range(1, TP):
        source = lax.rem(my_tp + TP - step, TP)
        rows = pl.ds(pl.multiple_of(source * QUARTER, QUARTER), QUARTER)
        remote(
            gathered.at[rows],
            gathered.at[rows],
            send.at[TP - 2 + step],
            recv.at[TP - 2 + step],
            tp=source,
        ).wait_recv()
    for copy in copies:
        copy.wait_send()
    return gathered[...].astype(F32)


TP_BUFFERS = [
    pltpu.VMEM((ROWS, D), F32),
    pltpu.VMEM((ROWS, D), BF16),
    pltpu.VMEM((TP - 1, QUARTER, D), BF16),
    pltpu.VMEM((ROWS, D), BF16),
]
TP_SEMS = [pltpu.SemaphoreType.DMA((2 * TP - 2,)), pltpu.SemaphoreType.DMA((2 * TP - 2,))]


def forward_kernel(
    layer,
    resid_ref,
    vec_ref,
    rot_ref,
    wq_hbm,
    wo_hbm,
    wu_hbm,
    wd_hbm,
    next_ref,
    kv_ref,
    qp_ref,
    att_ref,
    lse_ref,
    pre_ref,
    hid_ref,
    wq,
    wo,
    wu,
    wd,
    acc,
    top,
    load_sem,
    kv_send,
    kv_recv,
    tp_mine,
    tp_out,
    tp_slots,
    tp_gathered,
    tp_send,
    tp_recv,
):
    me = lax.axis_index("ctx")
    my_tp = lax.axis_index("tp")
    loads = []
    for index, (src, dst) in enumerate(((wq_hbm, wq), (wu_hbm, wu), (wd_hbm, wd), (wo_hbm, wo))):
        load = pltpu.make_async_copy(src.at[layer], dst, load_sem.at[index])
        load.start()
        loads.append(load)
    barrier = greet_all(me, my_tp)

    residual = resid_ref[...]
    vec = vec_ref.at[layer]
    hat, _ = centre(residual)
    normed = (hat * vec[G1 : G1 + 1, :] + vec[S1 : S1 + 1, :]).astype(BF16)
    loads[0].wait()
    merged = dot(normed, wq[...]) + vec[BQKV : BQKV + 1, :]
    merged = turn(merged, rot_ref, 1.0).astype(BF16)
    own = pl.ds(pl.multiple_of(me * ROWS, ROWS), ROWS)
    kv_ref[own, :] = merged[:, :384]
    qp_ref[...] = merged[:, 384:]
    pl.semaphore_wait(barrier, CTX - 1 + TP - 1)

    @pl.loop(me + 1, CTX)
    def _(target):
        remote(
            kv_ref.at[own], kv_ref.at[own], kv_send.at[target], kv_recv.at[me], ctx=target
        ).start()

    @pl.loop(me + 1, (me // PER + 1) * PER)
    def _(block):
        kv_ref[pl.ds(pl.multiple_of(block * ROWS, ROWS), ROWS), :] = jnp.zeros((ROWS, 384), BF16)

    normed = (hat * vec[G2 : G2 + 1, :] + vec[S2 : S2 + 1, :]).astype(BF16)
    loads[1].wait()
    pre = dot(normed, wu[...]) + vec[BUP : BUP + 1, :]
    pre_ref[...] = pre
    hidden = (pre * (1.0 + lax.erf(pre * math.sqrt(0.5))) * 0.5).astype(BF16)
    hid_ref[...] = hidden
    loads[2].wait()
    branch = dot(hidden, wd[...])
    next_ref[...] = branch

    acc[...] = jnp.zeros_like(acc)
    top[...] = jnp.zeros_like(top)
    for head in range(HEADS):
        top[head : head + 1, :] = jnp.full((1, ROWS), MASKED, F32)

    @pl.loop(0, me // PER + 1)
    def _(chunk):
        @pl.loop(chunk * PER, jnp.minimum(chunk * PER + PER, me))
        def _(source):
            rows = pl.ds(pl.multiple_of(source * ROWS, ROWS), ROWS)
            remote(
                kv_ref.at[rows], kv_ref.at[rows], kv_send.at[source], kv_recv.at[source], ctx=source
            ).wait_recv()

        keys = pl.ds(pl.multiple_of(chunk * CHUNK, CHUNK), CHUNK)
        key_pos = chunk * CHUNK + lax.broadcasted_iota(jnp.int32, (CHUNK, ROWS), 0)
        query_pos = me * ROWS + lax.broadcasted_iota(jnp.int32, (CHUNK, ROWS), 1)
        allowed = key_pos <= query_pos
        for head in range(HEADS):
            lanes = slice(128 * head, 128 * head + 128)
            block = kv_ref[keys, lanes]
            scores = dot(block, qp_ref[:, lanes], NT) * SCALE
            scores = jnp.where(allowed, scores, MASKED)
            old = top[head : head + 1, :]
            new = jnp.maximum(old, jnp.max(scores, axis=0, keepdims=True))
            weights = jnp.exp(scores - new)
            shrink = jnp.exp(old - new)
            top[head : head + 1, :] = new
            top[4 + head : 5 + head, :] = top[4 + head : 5 + head, :] * shrink + jnp.sum(
                weights, axis=0, keepdims=True
            )
            acc[head] = acc[head] * shrink + dot(block, weights.astype(BF16), TN)

    for head in range(HEADS):
        total = top[4 + head : 5 + head, :]
        att_ref[64 * head : 64 * head + 64, :] = acc[head, 64:, :] / total
        lse_ref[head : head + 1, :] = top[head : head + 1, :] + jnp.log(total)
    lse_ref[HEADS:, :] = jnp.zeros((8 - HEADS, ROWS), F32)
    loads[3].wait()
    branch = next_ref[...] + dot(att_ref[...].astype(BF16), wo[...], TN)
    branch = tp_sum(
        branch, my_tp, (tp_mine, tp_out, tp_slots, tp_gathered), (tp_send, tp_recv)
    )
    next_ref[...] = resid_ref[...] + branch + vec[BOUT : BOUT + 1, :]

    @pl.loop(me + 1, CTX)
    def _(target):
        remote(
            kv_ref.at[own], kv_ref.at[own], kv_send.at[target], kv_recv.at[me], ctx=target
        ).wait_send()


def vmem(count):
    return [pl.BlockSpec(memory_space=pltpu.VMEM)] * count


def hbm(count):
    return [pl.BlockSpec(memory_space=pl.ANY)] * count


def forward(layer, residual, vec, rot, wq, wo, wu, wd):
    return pl.pallas_call(
        functools.partial(forward_kernel, layer),
        name=f"layer_forward_{layer}",
        out_shape=[
            jax.ShapeDtypeStruct((ROWS, D), F32),
            jax.ShapeDtypeStruct((CTX * ROWS, 384), BF16),
            jax.ShapeDtypeStruct((ROWS, 384), BF16),
            jax.ShapeDtypeStruct((192, ROWS), F32),
            jax.ShapeDtypeStruct((8, ROWS), F32),
            jax.ShapeDtypeStruct((ROWS, D), F32),
            jax.ShapeDtypeStruct((ROWS, D), BF16),
        ],
        in_specs=vmem(3) + hbm(4),
        out_specs=vmem(7),
        scratch_shapes=[
            pltpu.VMEM((D, D), BF16),
            pltpu.VMEM((192, D), BF16),
            pltpu.VMEM((D, D), BF16),
            pltpu.VMEM((D, D), BF16),
            pltpu.VMEM((HEADS, 128, ROWS), F32),
            pltpu.VMEM((8, ROWS), F32),
            pltpu.SemaphoreType.DMA((4,)),
            pltpu.SemaphoreType.DMA((CTX,)),
            pltpu.SemaphoreType.DMA((CTX,)),
            *TP_BUFFERS,
            *TP_SEMS,
        ],
        compiler_params=pltpu.CompilerParams(
            collective_id=layer, has_side_effects=True, vmem_limit_bytes=48 << 20
        ),
    )(residual, vec, rot, wq, wo, wu, wd)


def backward_kernel(
    layer,
    grad_ref,
    resid_ref,
    vec_ref,
    rot_ref,
    kv_ref,
    qp_ref,
    att_ref,
    lse_ref,
    pre_ref,
    hid_ref,
    wq_hbm,
    wp_hbm,
    wu_hbm,
    wd_hbm,
    out_ref,
    weight_ref,
    small_ref,
    wq,
    wp,
    wu,
    wd,
    terms,
    slots,
    left,
    right,
    query,
    delta,
    norm_part,
    load_sem,
    kv_send,
    kv_recv,
    tp_mine,
    tp_out,
    tp_slots,
    tp_gathered,
    tp_send,
    tp_recv,
):
    me = lax.axis_index("ctx")
    my_tp = lax.axis_index("tp")
    loads = []
    for index, (src, dst) in enumerate(((wp_hbm, wp), (wd_hbm, wd), (wu_hbm, wu), (wq_hbm, wq))):
        load = pltpu.make_async_copy(src.at[layer], dst, load_sem.at[index])
        load.start()
        loads.append(load)
    barrier = greet_all(me, my_tp)
    vec = vec_ref.at[layer]

    low = grad_ref[...].astype(BF16)
    loads[0].wait()
    mixed = dot(low, wp[...], NT).astype(BF16)
    turned = dot(wp[...], low, NT).astype(BF16).astype(F32)
    for head in range(HEADS):
        lanes = slice(128 * head, 128 * head + 128)
        left[head, :ROWS, :] = qp_ref[:, lanes]
        left[head, ROWS:, :] = mixed[:, lanes]
        right[head, :ROWS, :] = (qp_ref[:, lanes].astype(F32) * SCALE).astype(BF16)
        right[head, ROWS:, :] = mixed[:, lanes]
        delta[head : head + 1, :] = jnp.sum(
            turned[128 * head + 64 : 128 * head + 128, :] * att_ref[64 * head : 64 * head + 64, :],
            axis=0,
            keepdims=True,
        )
    query[...] = jnp.zeros_like(query)
    pl.semaphore_wait(barrier, CTX - 1 + TP - 1)

    def term_copy(target):
        rows = pl.ds(pl.multiple_of(target * ROWS, ROWS), ROWS)
        return remote(
            terms.at[rows], slots.at[me], kv_send.at[target], kv_recv.at[me], ctx=target
        )

    @pl.loop(0, me // PER + 1)
    def _(chunk):
        keys = pl.ds(pl.multiple_of(chunk * CHUNK, CHUNK), CHUNK)
        key_pos = chunk * CHUNK + lax.broadcasted_iota(jnp.int32, (CHUNK, ROWS), 0)
        query_pos = me * ROWS + lax.broadcasted_iota(jnp.int32, (CHUNK, ROWS), 1)
        allowed = key_pos <= query_pos
        for head in range(HEADS):
            lanes = slice(128 * head, 128 * head + 128)
            block = kv_ref[keys, lanes]
            both = dot(block, left[head], NT)
            probs = jnp.where(
                allowed, jnp.exp(both[:, :ROWS] * SCALE - lse_ref[head : head + 1, :]), 0.0
            )
            scores = (probs * (both[:, ROWS:] - delta[head : head + 1, :])).astype(BF16)
            terms[keys, lanes] = dot(
                jnp.concatenate([scores, probs.astype(BF16)], axis=1), right[head]
            ).astype(BF16)
            query[head] += dot(scores, block, TN)

        @pl.loop(chunk * PER, jnp.minimum(chunk * PER + PER, me))
        def _(target):
            term_copy(target).start()

    small_ref[...] = jnp.zeros_like(small_ref)
    small_ref[4:5, :] = jnp.sum(grad_ref[...], axis=0, keepdims=True)
    weight_ref[QKV_ROWS : QKV_ROWS + OUT_ROWS, :] = dot(att_ref[...].astype(BF16), low).astype(BF16)
    weight_ref[QKV_ROWS + OUT_ROWS + UP_ROWS :, :] = dot(hid_ref[...], low, TN).astype(BF16)
    loads[1].wait()
    hidden_grad = dot(low, wd[...], NT)
    pre = pre_ref[...]
    slope = 0.5 * (1.0 + lax.erf(pre * math.sqrt(0.5))) + pre * jnp.exp(
        -0.5 * pre * pre
    ) * (1.0 / math.sqrt(2.0 * math.pi))
    pre_grad = (hidden_grad * slope).astype(BF16)
    small_ref[6:7, :] = jnp.sum(pre_grad.astype(F32), axis=0, keepdims=True)
    hat, inverse = centre(resid_ref[...])
    gain_one, gain_two = vec[G1 : G1 + 1, :], vec[G2 : G2 + 1, :]
    normed_two = (hat * gain_two + vec[S2 : S2 + 1, :]).astype(BF16)
    weight_ref[QKV_ROWS + OUT_ROWS : QKV_ROWS + OUT_ROWS + UP_ROWS, :] = dot(
        normed_two, pre_grad, TN
    ).astype(BF16)
    loads[2].wait()
    grad_two = dot(pre_grad, wu[...], NT)
    small_ref[2:3, :] = jnp.sum(grad_two * hat, axis=0, keepdims=True)
    small_ref[3:4, :] = jnp.sum(grad_two, axis=0, keepdims=True)
    norm_part[...] = grad_two * gain_two

    own = pl.ds(pl.multiple_of(me * ROWS, ROWS), ROWS)
    out_ref[:, :384] = terms[own, :].astype(F32)

    @pl.loop(me + 1, CTX)
    def _(source):
        remote(
            terms.at[own], slots.at[source], kv_send.at[source], kv_recv.at[source], ctx=source
        ).wait_recv()
        out_ref[:, :384] += slots[source].astype(F32)

    lane = lax.broadcasted_iota(jnp.int32, (ROWS, 128), 1)
    for head in range(HEADS):
        out_ref[:, 384 + 128 * head : 512 + 128 * head] = jnp.where(
            lane < HD, query[head] * SCALE, 0.0
        )
    merged = turn(out_ref[...], rot_ref, -1.0).astype(BF16)
    hat, inverse = centre(resid_ref[...])
    normed_one = (hat * gain_one + vec[S1 : S1 + 1, :]).astype(BF16)
    weight_ref[:384, :] = dot(merged[:, :384], normed_one, TN).astype(BF16)
    queries_grad = dot(merged[:, 384:], normed_one, TN).astype(BF16)
    for head in range(HEADS):
        weight_ref[384 + 64 * head : 448 + 64 * head, :] = queries_grad[
            128 * head : 128 * head + 64, :
        ]
    small_ref[5:6, :] = jnp.sum(merged.astype(F32), axis=0, keepdims=True)
    loads[3].wait()
    grad_one = dot(merged, wq[...], NT)
    small_ref[0:1, :] = jnp.sum(grad_one * hat, axis=0, keepdims=True)
    small_ref[1:2, :] = jnp.sum(grad_one, axis=0, keepdims=True)
    total = tp_sum(
        norm_part[...] + grad_one * gain_one,
        my_tp,
        (tp_mine, tp_out, tp_slots, tp_gathered),
        (tp_send, tp_recv),
    )
    hat, inverse = centre(resid_ref[...])
    along = jnp.mean(total * hat, axis=-1, keepdims=True)
    level = jnp.mean(total, axis=-1, keepdims=True)
    out_ref[...] = grad_ref[...] + inverse * (total - level - hat * along)

    @pl.loop(0, me)
    def _(target):
        term_copy(target).wait_send()


def backward(layer, grad, residual, vec, rot, saved, wq, wp, wu, wd):
    return pl.pallas_call(
        functools.partial(backward_kernel, layer),
        name=f"layer_backward_{layer}",
        out_shape=[
            jax.ShapeDtypeStruct((ROWS, D), F32),
            jax.ShapeDtypeStruct((GRAD_ROWS, D), BF16),
            jax.ShapeDtypeStruct((8, D), F32),
        ],
        in_specs=vmem(10) + hbm(4),
        out_specs=vmem(3),
        scratch_shapes=[
            pltpu.VMEM((D, D), BF16),
            pltpu.VMEM((384, D), BF16),
            pltpu.VMEM((D, D), BF16),
            pltpu.VMEM((D, D), BF16),
            pltpu.VMEM((CTX * ROWS, 384), BF16),
            pltpu.VMEM((CTX, ROWS, 384), BF16),
            pltpu.VMEM((HEADS, 2 * ROWS, 128), BF16),
            pltpu.VMEM((HEADS, 2 * ROWS, 128), BF16),
            pltpu.VMEM((HEADS, ROWS, 128), F32),
            pltpu.VMEM((8, ROWS), F32),
            pltpu.VMEM((ROWS, D), F32),
            pltpu.SemaphoreType.DMA((4,)),
            pltpu.SemaphoreType.DMA((CTX,)),
            pltpu.SemaphoreType.DMA((CTX,)),
            *TP_BUFFERS,
            *TP_SEMS,
        ],
        compiler_params=pltpu.CompilerParams(
            collective_id=2 + layer, has_side_effects=True, vmem_limit_bytes=56 << 20
        ),
    )(grad, residual, vec, rot, *saved, wq, wp, wu, wd)


RING = 4
BIG = GRAD_ROWS // RING
SUB = BIG // RING
BIG_CUT, SUB_CUT = 288, 80
HALF = D // 2
RS_MESSAGES, AG_MESSAGES = 6, 6
FLOW_SEMS = 2 * RS_MESSAGES + 1 + 2 * AG_MESSAGES


def rows_at(start, count):
    return pl.ds(pl.multiple_of(start, 16), count)


class Axis:
    def __init__(self, place, of_place):
        self.place = place
        self.of_place = of_place
        self.right = of_place(lax.rem(place + 1, RING))
        self.left = of_place(lax.rem(place + 3, RING))

    def at(self, step):
        return lax.rem(self.place + step + RING, RING)


class ReduceScatter:
    def __init__(self, axis, src, size, cut, first, second, from_left, from_right, sems):
        self.axis, self.src, self.size, self.cut = axis, src, size, cut
        self.first, self.second = first, second
        self.from_left, self.from_right = from_left, from_right
        self.send, self.recv, self.base = sems

    def copy(self, index, src, dst, ctx):
        return remote(
            src, dst, self.send.at[self.base + index], self.recv.at[self.base + index], ctx=ctx
        )

    def copies(self):
        axis, size, cut = self.axis, self.size, self.cut
        rest = size - cut
        far, near_right, near_left = axis.at(2) * size, axis.at(1) * size, axis.at(3) * size
        return [
            self.copy(0, self.src(far, cut), self.first[0].at[pl.ds(0, cut)], axis.right),
            self.copy(1, self.src(far + cut, rest), self.second[0].at[pl.ds(0, rest)], axis.left),
            self.copy(
                2, self.src(near_right + cut, rest), self.from_left.at[pl.ds(cut, rest)], axis.right
            ),
            self.copy(3, self.src(near_left, cut), self.from_right.at[pl.ds(0, cut)], axis.left),
            self.copy(
                4, self.first[1].at[pl.ds(0, cut)], self.from_left.at[pl.ds(0, cut)], axis.right
            ),
            self.copy(
                5, self.second[1].at[pl.ds(0, rest)], self.from_right.at[pl.ds(cut, rest)], axis.left
            ),
        ]

    def start(self):
        for copy in self.copies()[:4]:
            copy.start()

    def middle(self):
        axis, size, cut = self.axis, self.size, self.cut
        rest = size - cut
        copies = self.copies()
        copies[0].wait_recv()
        self.first[1][0:cut, :] = (
            self.first[0][0:cut, :].astype(F32) + self.src(axis.at(1) * size, cut)[...].astype(F32)
        ).astype(BF16)
        copies[4].start()
        copies[1].wait_recv()
        self.second[1][0:rest, :] = (
            self.second[0][0:rest, :].astype(F32)
            + self.src(axis.at(3) * size + cut, rest)[...].astype(F32)
        ).astype(BF16)
        copies[5].start()

    def finish(self, out):
        for copy in self.copies()[2:]:
            copy.wait_recv()
        size = self.size
        out[0:size, :] = (
            self.src(self.axis.place * size, size)[...].astype(F32)
            + self.from_left[0:size, :].astype(F32)
            + self.from_right[0:size, :].astype(F32)
        ).astype(BF16)

    def drain(self):
        for copy in self.copies():
            copy.wait_send()


class AllGather:
    def __init__(self, axis, view, size, cut, sems):
        self.axis, self.view, self.size, self.cut = axis, view, size, cut
        self.send, self.recv, self.base = sems

    def copy(self, index, start, count, ctx):
        part = self.view(start, count)
        return remote(
            part, part, self.send.at[self.base + index], self.recv.at[self.base + index], ctx=ctx
        )

    def copies(self, shift):
        axis, size, cut = self.axis, self.size, self.cut
        rest = size - cut
        if shift == 0:
            own, from_left, from_right = axis.place * size, axis.at(3) * size, axis.at(1) * size
            return [
                self.copy(0, own, cut, axis.right),
                self.copy(1, own + cut, rest, axis.left),
                self.copy(2, own + cut, rest, axis.right),
                self.copy(3, own, cut, axis.left),
                self.copy(4, from_left, cut, axis.right),
                self.copy(5, from_right + cut, rest, axis.left),
            ]
        from_left, from_right, far = axis.at(3) * size, axis.at(1) * size, axis.at(2) * size
        return [
            self.copy(0, from_left, cut, axis.right),
            self.copy(1, from_right + cut, rest, axis.left),
            self.copy(2, from_left + cut, rest, axis.right),
            self.copy(3, from_right, cut, axis.left),
            self.copy(4, far, cut, axis.right),
            self.copy(5, far + cut, rest, axis.left),
        ]

    def start(self):
        for copy in self.copies(0)[:4]:
            copy.start()

    def middle(self):
        come, go = self.copies(1), self.copies(0)
        come[0].wait_recv()
        go[4].start()
        come[1].wait_recv()
        go[5].start()

    def finish(self):
        for copy in self.copies(1)[2:]:
            copy.wait_recv()

    def drain(self):
        for copy in self.copies(0):
            copy.wait_send()


FLOW_BUFFERS = [
    pltpu.VMEM((BIG_CUT, HALF), BF16),
    pltpu.VMEM((BIG_CUT, HALF), BF16),
    pltpu.VMEM((BIG - BIG_CUT, HALF), BF16),
    pltpu.VMEM((BIG - BIG_CUT, HALF), BF16),
    pltpu.VMEM((BIG, HALF), BF16),
    pltpu.VMEM((BIG, HALF), BF16),
    pltpu.VMEM((BIG, HALF), BF16),
    pltpu.VMEM((SUB_CUT, HALF), BF16),
    pltpu.VMEM((SUB_CUT, HALF), BF16),
    pltpu.VMEM((SUB - SUB_CUT, HALF), BF16),
    pltpu.VMEM((SUB - SUB_CUT, HALF), BF16),
    pltpu.VMEM((SUB, HALF), BF16),
    pltpu.VMEM((SUB, HALF), BF16),
    pltpu.VMEM((SUB, HALF), BF16),
    pltpu.VMEM((SUB, HALF), BF16),
    pltpu.SemaphoreType.DMA((FLOW_SEMS,)),
    pltpu.SemaphoreType.DMA((FLOW_SEMS,)),
]


class Flow:
    def __init__(self, axes, across, src_ref, out_ref, half, scratch):
        one, two = axes
        (a0, a1, b0, b1, left, right, self.big, c0, c1, d0, d1, left2, right2, self.sub, self.other) = (
            scratch[:15]
        )
        self.send, self.recv = scratch[15:]
        lanes = pl.ds(half * HALF, HALF)

        def src(start, count):
            return src_ref.at[rows_at(start, count), lanes]

        def middle_src(start, count):
            return self.big.at[rows_at(start, count)]

        def out(start, count):
            return out_ref.at[rows_at(start, count), lanes]

        corner = one.place * BIG

        def out_sub(start, count):
            return out_ref.at[rows_at(corner + start, count), lanes]

        self.out_piece = out_sub(two.place * SUB, SUB)
        self.across = across

        def sems(base):
            return (self.send, self.recv, base)

        self.one = ReduceScatter(one, src, BIG, BIG_CUT, (a0, a1), (b0, b1), left, right, sems(0))
        self.two = ReduceScatter(
            two, middle_src, SUB, SUB_CUT, (c0, c1), (d0, d1), left2, right2, sems(6)
        )
        self.three = AllGather(two, out_sub, SUB, SUB_CUT, sems(13))
        self.four = AllGather(one, out, BIG, BIG_CUT, sems(19))

    def swap(self):
        return remote(self.sub, self.other, self.send.at[12], self.recv.at[12], ctx=self.across)

    def step(self, number):
        if number == 0:
            self.one.start()
        elif number == 1:
            self.one.middle()
        elif number == 2:
            self.one.finish(self.big)
            self.two.start()
        elif number == 3:
            self.two.middle()
        elif number == 4:
            self.two.finish(self.sub)
            self.swap().start()
        elif number == 5:
            self.swap().wait_recv()
            self.out_piece[...] = (
                self.sub[...].astype(F32) + self.other[...].astype(F32)
            ).astype(BF16)
            self.three.start()
        elif number == 6:
            self.three.middle()
        elif number == 7:
            self.three.finish()
            self.four.start()
        elif number == 8:
            self.four.middle()
        elif number == 9:
            self.four.finish()

    def drain(self):
        self.one.drain()
        self.two.drain()
        self.swap().wait_send()
        self.three.drain()
        self.four.drain()


STEPS = 10


def reduce_kernel(w0, w1, s0, s1, o0, o1, small_out, small, small_slots, small_send, small_recv, *flow):
    me = lax.axis_index("ctx")
    my_tp = lax.axis_index("tp")
    z = lax.rem(me, 4)
    x = lax.rem(me // 4, 2)
    y = me // 8
    across = me + 4 - 8 * x
    z_axis = Axis(z, lambda place: me - z + place)
    y_axis = Axis(y, lambda place: me + (place - y) * 8)
    z_peers = [z_axis.of_place(z_axis.at(step)) for step in (1, 2, 3)]
    y_peers = [y_axis.of_place(y_axis.at(step)) for step in (1, 2, 3)]
    tp_peers = [lax.rem(my_tp + step, TP) for step in (1, 2, 3)]
    barrier, count = greet(z_peers + y_peers + [across], tp_peers)
    pl.semaphore_wait(barrier, count)

    flows = []
    per = len(FLOW_BUFFERS)
    for index, (src, out, half) in enumerate(((w1, o1, 0), (w1, o1, 1), (w0, o0, 0), (w0, o0, 1))):
        axes = (z_axis, y_axis) if half == 0 else (y_axis, z_axis)
        flows.append(Flow(axes, across, src, out, half, flow[per * index : per * index + per]))

    def small_copies(stage, place, peers, tp):
        return [
            remote(
                small.at[stage],
                small_slots.at[stage, place],
                small_send.at[stage, step],
                small_recv.at[stage, step],
                **({"tp": peer} if tp else {"ctx": peer}),
            )
            for step, peer in enumerate(peers)
        ]

    stages = [
        small_copies(0, z, z_peers, False),
        small_copies(1, y, y_peers, False),
        small_copies(2, x, [across], False),
        small_copies(3, my_tp, tp_peers, True),
    ]
    places = (z, y, x, my_tp)

    def small_total(stage):
        for copy in stages[stage]:
            copy.wait_recv()
        small_slots[stage, places[stage]] = small[stage]
        total = small_slots[stage, 0]
        for place in range(1, 2 if stage == 2 else 4):
            total = total + small_slots[stage, place]
        return total

    def small_step(number):
        if number == 0:
            small[0, 0:8, :] = s0[...]
            small[0, 8:16, :] = s1[...]
        elif number < 4:
            small[number] = small_total(number - 1)
        if number < 4:
            for copy in stages[number]:
                copy.start()
        elif number == 4:
            total = small_total(3)
            row = lax.rem(lax.broadcasted_iota(jnp.int32, (16, D), 0), 8)
            small_out[...] = jnp.where(row < 4, total, small[3])

    for number in range(STEPS):
        if number < 5:
            small_step(number)
        for one in flows:
            one.step(number)
    for one in flows:
        one.drain()
    for copies in stages:
        for copy in copies:
            copy.wait_send()


def reduce_all(w0, w1, s0, s1):
    return pl.pallas_call(
        reduce_kernel,
        name="weight_gradient_sum",
        out_shape=[
            jax.ShapeDtypeStruct((GRAD_ROWS, D), BF16),
            jax.ShapeDtypeStruct((GRAD_ROWS, D), BF16),
            jax.ShapeDtypeStruct((16, D), F32),
        ],
        in_specs=vmem(4),
        out_specs=vmem(3),
        scratch_shapes=[
            pltpu.VMEM((4, 16, D), F32),
            pltpu.VMEM((4, 4, 16, D), F32),
            pltpu.SemaphoreType.DMA((4, 3)),
            pltpu.SemaphoreType.DMA((4, 3)),
            *(FLOW_BUFFERS * 4),
        ],
        compiler_params=pltpu.CompilerParams(
            collective_id=4, has_side_effects=True, vmem_limit_bytes=56 << 20
        ),
    )(w0, w1, s0, s1)


def rotary_planes(positions):
    halves = ROT // 2
    inverse = jnp.power(10000.0, -2.0 * jnp.arange(halves, dtype=F32) / ROT)
    angles = positions[:, None] * inverse[None, :]
    cosine, sine = jnp.cos(angles), jnp.sin(angles)
    rows = positions.shape[0]
    rest = 128 - ROT
    return jnp.stack(
        [
            jnp.concatenate([cosine, cosine, jnp.ones((rows, rest), F32)], axis=1),
            jnp.concatenate(
                [jnp.zeros((rows, halves), F32), sine, jnp.zeros((rows, rest), F32)], axis=1
            ),
            jnp.concatenate([-sine, jnp.zeros((rows, halves + rest), F32)], axis=1),
        ]
    )


def packed_qkv(array):
    lead = array.shape[:-2]
    parts = array.reshape(*lead, 3, HEADS, HD)
    pairs = jnp.stack([parts[..., 1, :, :], parts[..., 2, :, :]], axis=-2)
    queries = jnp.stack([parts[..., 0, :, :], jnp.zeros_like(parts[..., 0, :, :])], axis=-2)
    return jnp.concatenate(
        [pairs.reshape(*lead, 2 * HEADS * HD), queries.reshape(*lead, 2 * HEADS * HD)], axis=-1
    )


def on_device(
    layer_input,
    attention_gain,
    attention_shift,
    feedforward_gain,
    feedforward_shift,
    query_key_value_weight,
    query_key_value_bias,
    attention_out_weight,
    dense_bias,
    expand_weight,
    expand_bias,
    down_weight,
    down_bias,
    output_grad,
):
    me = lax.axis_index("ctx")
    positions = (me * ROWS + jnp.arange(ROWS, dtype=jnp.int32)).astype(F32)
    rot = rotary_planes(positions)
    vec = jnp.stack(
        [
            attention_gain.astype(F32),
            attention_shift.astype(F32),
            feedforward_gain.astype(F32),
            feedforward_shift.astype(F32),
            expand_bias.astype(F32),
            dense_bias.astype(F32) + down_bias.astype(F32),
            packed_qkv(query_key_value_bias.astype(F32)),
            jnp.zeros((LAYERS, D), F32),
        ],
        axis=1,
    )
    wq = packed_qkv(query_key_value_weight)
    wp = jnp.pad(
        attention_out_weight.reshape(LAYERS, HEADS, HD, D), ((0, 0), (0, 0), (HD, 0), (0, 0))
    ).reshape(LAYERS, 2 * HEADS * HD, D)
    residual = layer_input[0].astype(F32)
    residuals, saved = [], []
    for layer in range(LAYERS):
        residuals.append(residual)
        residual, *kept = forward(
            layer, residual, vec, rot, wq, attention_out_weight, expand_weight, down_weight
        )
        saved.append(kept)
    output = residual.astype(BF16)
    grad = output_grad[0].astype(F32)
    weights, smalls = [None] * LAYERS, [None] * LAYERS
    for layer in reversed(range(LAYERS)):
        grad, weights[layer], smalls[layer] = backward(
            layer,
            grad,
            residuals[layer],
            vec,
            rot,
            saved[layer],
            wq,
            wp,
            expand_weight,
            down_weight,
        )
    total_0, total_1, small = reduce_all(weights[0], weights[1], smalls[0], smalls[1])
    small = small.reshape(LAYERS, 8, D)
    totals = (total_0, total_1)

    def qkv_grad(total):
        pairs = total[:384].reshape(HEADS, 2, HD, D)
        queries = total[384:QKV_ROWS].reshape(1, HEADS, HD, D)
        slots = jnp.concatenate([queries, pairs.transpose(1, 0, 2, 3)], axis=0)
        return slots.reshape(3 * HEADS * HD, D).T.reshape(D, 3, HEADS * HD)

    def part(start, count):
        return jnp.stack([total[start : start + count] for total in totals]).astype(F32)

    bias = small[:, 5]
    pairs = bias[:, :384].reshape(LAYERS, HEADS, 2, HD)
    queries = bias[:, 384:].reshape(LAYERS, HEADS, 2, HD)[:, :, 0]
    merged_bias_grad = jnp.stack([queries, pairs[:, :, 0], pairs[:, :, 1]], axis=1).reshape(
        LAYERS, 3, HEADS * HD
    )
    return (
        output[None],
        grad[None],
        small[:, 0],
        small[:, 1],
        small[:, 2],
        small[:, 3],
        jnp.stack([qkv_grad(total) for total in totals]).astype(F32),
        merged_bias_grad,
        part(QKV_ROWS, OUT_ROWS),
        small[:, 4],
        part(QKV_ROWS + OUT_ROWS, UP_ROWS),
        small[:, 6],
        part(QKV_ROWS + OUT_ROWS + UP_ROWS, DOWN_ROWS),
        small[:, 4],
    )


def solution(mesh):
    in_specs = (
        P(None, "ctx", None),
        P(),
        P(),
        P(),
        P(),
        P(None, None, None, "tp"),
        P(None, None, "tp"),
        P(None, "tp", None),
        P(),
        P(None, None, "tp"),
        P(None, "tp"),
        P(None, "tp", None),
        P(),
        P(None, "ctx", None),
    )
    out_specs = (
        P(None, "ctx", None),
        P(None, "ctx", None),
        P(),
        P(),
        P(),
        P(),
        P(None, None, None, "tp"),
        P(None, None, "tp"),
        P(None, "tp", None),
        P(),
        P(None, None, "tp"),
        P(None, "tp"),
        P(None, "tp", None),
        P(),
    )
    return jax.shard_map(
        on_device, mesh=mesh, in_specs=in_specs, out_specs=out_specs, check_vma=False
    )
```

```python
import functools
import math

import jax
import jax.numpy as jnp
from jax import lax
from jax.experimental import pallas as pl
from jax.experimental.pallas import tpu as pltpu
from jax.sharding import PartitionSpec as P

HD = 64
ROT = 16
LAYERS = 2
NORM_EPSILON = 1e-05
MASKED = -1e30
F32 = jnp.float32
BF16 = jnp.bfloat16
ROWS = 128
D = 768
HEADS = 3
CTX = 32
TP = 4
RING = 4
GROUPS = CTX // RING
KEYS = RING * ROWS
WIDE = HEADS * HD
QUARTER = ROWS // TP
SCALE = HD**-0.5
G1, S1, G2, S2, BUP, BOUT, BQKV = range(7)
QKV_ROWS, OUT_ROWS, UP_ROWS, DOWN_ROWS = 576, 192, 768, 768
GRAD_ROWS = QKV_ROWS + OUT_ROWS + UP_ROWS + DOWN_ROWS

NN = (((1,), (0,)), ((), ()))
NT = (((1,), (1,)), ((), ()))
TN = (((0,), (0,)), ((), ()))


def dot(a, b, dims=NN):
    return lax.dot_general(a, b, dims, preferred_element_type=F32)


def remote(src, dst, send, recv, ctx=None, tp=None):
    where = {}
    if ctx is not None:
        where["ctx"] = ctx
    if tp is not None:
        where["tp"] = tp
    return pltpu.make_async_remote_copy(
        src_ref=src,
        dst_ref=dst,
        send_sem=send,
        recv_sem=recv,
        device_id=where,
        device_id_type=pl.DeviceIdType.MESH,
    )


def greet(ctx_peers, tp_peers):
    barrier = pltpu.get_barrier_semaphore()
    for peer in ctx_peers:
        pl.semaphore_signal(
            barrier, inc=1, device_id={"ctx": peer}, device_id_type=pl.DeviceIdType.MESH
        )
    for peer in tp_peers:
        pl.semaphore_signal(
            barrier, inc=1, device_id={"tp": peer}, device_id_type=pl.DeviceIdType.MESH
        )
    return barrier, len(ctx_peers) + len(tp_peers)


def greet_layer(me, my_tp):
    z, group = lax.rem(me, RING), me // RING
    ring = [group * RING + lax.rem(z + step, RING) for step in range(1, RING)]
    column = [lax.rem(group + step, GROUPS) * RING + z for step in range(1, GROUPS)]
    return greet(ring + column, [lax.rem(my_tp + step, TP) for step in range(1, TP)])


def centre(residual):
    mean_value = jnp.mean(residual, axis=-1, keepdims=True)
    centred = residual - mean_value
    variance = jnp.mean(centred * centred, axis=-1, keepdims=True)
    inverse = lax.rsqrt(variance + NORM_EPSILON)
    return centred * inverse, inverse


def turn(values, rot_ref, sign):
    width = values.shape[1]
    count = width // 128
    cosine = jnp.concatenate([rot_ref[0]] * count, axis=1)
    after = jnp.concatenate([rot_ref[1]] * count, axis=1)
    before = jnp.concatenate([rot_ref[2]] * count, axis=1)
    turned = pltpu.roll(values, 8, 1) * after + pltpu.roll(values, width - 8, 1) * before
    return values * cosine + sign * turned


def tp_sum(part, my_tp, buffers, sems):
    mine, out, slots, gathered = buffers
    send, recv = sems
    mine[...] = part
    out[...] = part.astype(BF16)
    own = pl.ds(pl.multiple_of(my_tp * QUARTER, QUARTER), QUARTER)
    copies = []
    for step in range(1, TP):
        peer = lax.rem(my_tp + step, TP)
        rows = pl.ds(pl.multiple_of(peer * QUARTER, QUARTER), QUARTER)
        copy = remote(
            out.at[rows], slots.at[step - 1], send.at[step - 1], recv.at[step - 1], tp=peer
        )
        copy.start()
        copies.append(copy)
    total = mine[own, :]
    for step in range(1, TP):
        copies[step - 1].wait_recv()
        total = total + slots[step - 1].astype(F32)
    gathered[own, :] = total.astype(BF16)
    for step in range(1, TP):
        peer = lax.rem(my_tp + step, TP)
        copy = remote(
            gathered.at[own],
            gathered.at[own],
            send.at[TP - 2 + step],
            recv.at[TP - 2 + step],
            tp=peer,
        )
        copy.start()
        copies.append(copy)
    for step in range(1, TP):
        source = lax.rem(my_tp + TP - step, TP)
        rows = pl.ds(pl.multiple_of(source * QUARTER, QUARTER), QUARTER)
        remote(
            gathered.at[rows],
            gathered.at[rows],
            send.at[TP - 2 + step],
            recv.at[TP - 2 + step],
            tp=source,
        ).wait_recv()
    for copy in copies:
        copy.wait_send()
    return gathered[...].astype(F32)


TP_BUFFERS = [
    pltpu.VMEM((ROWS, D), F32),
    pltpu.VMEM((ROWS, D), BF16),
    pltpu.VMEM((TP - 1, QUARTER, D), BF16),
    pltpu.VMEM((ROWS, D), BF16),
]
TP_SEMS = [pltpu.SemaphoreType.DMA((2 * TP - 2,)), pltpu.SemaphoreType.DMA((2 * TP - 2,))]


def group_copies(buffer, stats, here, there, group, z, sems):
    send, recv, stat_send, stat_recv = sems
    target = group * RING + z
    main = remote(
        buffer[0].at[here], buffer[1].at[there], send.at[group], recv.at[there], ctx=target
    )
    side = remote(
        stats[0].at[here], stats[1].at[there], stat_send.at[group], stat_recv.at[there], ctx=target
    )
    return main, side


def allowed_pairs(group, of_query, z):
    key_pos = group * KEYS + lax.broadcasted_iota(jnp.int32, (KEYS, ROWS), 0)
    query_pos = of_query * KEYS + z * ROWS + lax.broadcasted_iota(jnp.int32, (KEYS, ROWS), 1)
    return key_pos <= query_pos


def forward_kernel(
    layer,
    resid_ref,
    vec_ref,
    rot_ref,
    wq_hbm,
    wo_hbm,
    wu_hbm,
    wd_hbm,
    next_ref,
    kv_ref,
    q_ref,
    att_ref,
    lse_ref,
    pre_ref,
    hid_ref,
    wq,
    wo,
    wu,
    wd,
    kv_t,
    part_out,
    part_in,
    lse_out,
    lse_in,
    load_sem,
    kv_send,
    kv_recv,
    q_send,
    q_recv,
    part_send,
    part_recv,
    lse_send,
    lse_recv,
    tp_mine,
    tp_out,
    tp_slots,
    tp_gathered,
    tp_send,
    tp_recv,
):
    me = lax.axis_index("ctx")
    my_tp = lax.axis_index("tp")
    z, group = lax.rem(me, RING), me // RING
    loads = []
    for index, (src, dst) in enumerate(((wq_hbm, wq), (wu_hbm, wu), (wd_hbm, wd), (wo_hbm, wo))):
        load = pltpu.make_async_copy(src.at[layer], dst, load_sem.at[index])
        load.start()
        loads.append(load)
    barrier, count = greet_layer(me, my_tp)

    residual = resid_ref[...]
    vec = vec_ref.at[layer]
    hat, _ = centre(residual)
    normed = (hat * vec[G1 : G1 + 1, :] + vec[S1 : S1 + 1, :]).astype(BF16)
    loads[0].wait()
    merged = dot(normed, wq[...]) + vec[BQKV : BQKV + 1, :]
    merged = turn(merged, rot_ref, 1.0)

    def ring_rows(step):
        place = lax.rem(z + step + RING, RING)
        return pl.ds(pl.multiple_of(place * ROWS, ROWS), ROWS)

    def kv_copy(step):
        own = ring_rows(0)
        return remote(
            kv_ref.at[own],
            kv_ref.at[own],
            kv_send.at[step - 1],
            kv_recv.at[step - 1],
            ctx=group * RING + lax.rem(z + step, RING),
        )

    def q_copy(target, source):
        return remote(
            q_ref.at[source],
            q_ref.at[source],
            q_send.at[target],
            q_recv.at[source],
            ctx=target * RING + z,
        )

    kv_ref[ring_rows(0), :] = merged[:, :384].astype(BF16)
    for head in range(HEADS):
        across = merged[:, 384 + 128 * head : 512 + 128 * head].T
        q_ref[group, HD * head : HD * head + HD, :] = across[:HD, :].astype(BF16)
    pl.semaphore_wait(barrier, count)
    for step in range(1, RING):
        kv_copy(step).start()

    @pl.loop(0, group)
    def _(target):
        q_copy(target, group).start()

    normed = (hat * vec[G2 : G2 + 1, :] + vec[S2 : S2 + 1, :]).astype(BF16)
    loads[1].wait()
    pre = dot(normed, wu[...]) + vec[BUP : BUP + 1, :]
    pre_ref[...] = pre
    hidden = (pre * (1.0 + lax.erf(pre * math.sqrt(0.5))) * 0.5).astype(BF16)
    hid_ref[...] = hidden
    loads[2].wait()
    next_ref[...] = dot(hidden, wd[...])

    for step in range(1, RING):
        rows = ring_rows(-step)
        remote(
            kv_ref.at[rows],
            kv_ref.at[rows],
            kv_send.at[step - 1],
            kv_recv.at[step - 1],
            ctx=group * RING + lax.rem(z + step, RING),
        ).wait_recv()
    kv_t[...] = kv_ref[...].T

    def attend(of_query, own):
        allowed = allowed_pairs(group, of_query, z)
        for head in range(HEADS):
            rows = slice(HD * head, HD * head + HD)
            scores = dot(kv_ref[:, 128 * head : 128 * head + HD], q_ref[of_query, rows, :]) * SCALE
            if own:
                scores = jnp.where(allowed, scores, MASKED)
            highest = jnp.max(scores, axis=0, keepdims=True)
            weights = jnp.exp(scores - highest)
            total = jnp.sum(weights, axis=0, keepdims=True)
            values_t = kv_t[128 * head + HD : 128 * head + 128, :]
            attended = dot(values_t, weights.astype(BF16)) / total
            log_total = highest + jnp.log(total)
            if own:
                att_ref[rows, :] = attended
                lse_ref[head : head + 1, :] = log_total
            else:
                part_out[of_query, rows, :] = attended.astype(BF16)
                lse_out[of_query, head : head + 1, :] = log_total

    def part_copies(here, there, target):
        return group_copies(
            (part_out, part_in),
            (lse_out, lse_in),
            here,
            there,
            target,
            z,
            (part_send, part_recv, lse_send, lse_recv),
        )

    lse_ref[...] = jnp.zeros_like(lse_ref)

    @pl.loop(group + 1, GROUPS)
    def _(of_query):
        q_copy(of_query, of_query).wait_recv()
        lse_out[of_query] = jnp.zeros((8, ROWS), F32)
        attend(of_query, False)
        for copy in part_copies(of_query, group, of_query):
            copy.start()

    attend(group, True)

    @pl.loop(0, group)
    def _(source):
        for copy in part_copies(source, source, source):
            copy.wait_recv()
        old, new = lse_ref[...], lse_in[source]
        highest = jnp.maximum(old, new)
        old_part, new_part = jnp.exp(old - highest), jnp.exp(new - highest)
        total = old_part + new_part
        lse_ref[...] = highest + jnp.log(total)
        old_part, new_part = old_part / total, new_part / total
        for head in range(HEADS):
            rows = slice(HD * head, HD * head + HD)
            att_ref[rows, :] = att_ref[rows, :] * old_part[head : head + 1, :] + (
                part_in[source, rows, :].astype(F32) * new_part[head : head + 1, :]
            )

    loads[3].wait()
    branch = next_ref[...] + dot(att_ref[...].astype(BF16), wo[...], TN)
    branch = tp_sum(
        branch, my_tp, (tp_mine, tp_out, tp_slots, tp_gathered), (tp_send, tp_recv)
    )
    next_ref[...] = resid_ref[...] + branch + vec[BOUT : BOUT + 1, :]

    for step in range(1, RING):
        kv_copy(step).wait_send()

    @pl.loop(0, group)
    def _(target):
        q_copy(target, group).wait_send()

    @pl.loop(group + 1, GROUPS)
    def _(of_query):
        for copy in part_copies(of_query, group, of_query):
            copy.wait_send()


def vmem(count):
    return [pl.BlockSpec(memory_space=pltpu.VMEM)] * count


def hbm(count):
    return [pl.BlockSpec(memory_space=pl.ANY)] * count


GROUP_BUFFERS = [
    pltpu.VMEM((GROUPS, WIDE, ROWS), BF16),
    pltpu.VMEM((GROUPS, WIDE, ROWS), BF16),
    pltpu.VMEM((GROUPS, 8, ROWS), F32),
    pltpu.VMEM((GROUPS, 8, ROWS), F32),
]


def dma_sems(*counts):
    return [pltpu.SemaphoreType.DMA((count,)) for count in counts]


def forward(layer, residual, vec, rot, wq, wo, wu, wd):
    return pl.pallas_call(
        functools.partial(forward_kernel, layer),
        name=f"layer_forward_{layer}",
        out_shape=[
            jax.ShapeDtypeStruct((ROWS, D), F32),
            jax.ShapeDtypeStruct((KEYS, 384), BF16),
            jax.ShapeDtypeStruct((GROUPS, WIDE, ROWS), BF16),
            jax.ShapeDtypeStruct((WIDE, ROWS), F32),
            jax.ShapeDtypeStruct((8, ROWS), F32),
            jax.ShapeDtypeStruct((ROWS, D), F32),
            jax.ShapeDtypeStruct((ROWS, D), BF16),
        ],
        in_specs=vmem(3) + hbm(4),
        out_specs=vmem(7),
        scratch_shapes=[
            pltpu.VMEM((D, D), BF16),
            pltpu.VMEM((WIDE, D), BF16),
            pltpu.VMEM((D, D), BF16),
            pltpu.VMEM((D, D), BF16),
            pltpu.VMEM((384, KEYS), BF16),
            *GROUP_BUFFERS,
            *dma_sems(4, 3, 3, *[GROUPS] * 6),
            *TP_BUFFERS,
            *TP_SEMS,
        ],
        compiler_params=pltpu.CompilerParams(
            collective_id=layer, has_side_effects=True, vmem_limit_bytes=40 << 20
        ),
    )(residual, vec, rot, wq, wo, wu, wd)


def backward_kernel(
    layer,
    grad_ref,
    resid_ref,
    vec_ref,
    rot_ref,
    kv_ref,
    q_ref,
    att_ref,
    lse_ref,
    pre_ref,
    hid_ref,
    wq_hbm,
    wo_hbm,
    wu_hbm,
    wd_hbm,
    out_ref,
    weight_ref,
    small_ref,
    wq,
    wo,
    wu,
    wd,
    kv_t,
    mixed,
    stats,
    query_out,
    query_in,
    pair,
    terms,
    low_terms,
    term_slots,
    query,
    norm_part,
    load_sem,
    kv_send,
    kv_recv,
    mixed_send,
    mixed_recv,
    stat_send,
    stat_recv,
    query_send,
    query_recv,
    tp_mine,
    tp_out,
    tp_slots,
    tp_gathered,
    tp_send,
    tp_recv,
):
    me = lax.axis_index("ctx")
    my_tp = lax.axis_index("tp")
    z, group = lax.rem(me, RING), me // RING
    loads = []
    for index, (src, dst) in enumerate(((wo_hbm, wo), (wd_hbm, wd), (wu_hbm, wu), (wq_hbm, wq))):
        load = pltpu.make_async_copy(src.at[layer], dst, load_sem.at[index])
        load.start()
        loads.append(load)
    barrier, count = greet_layer(me, my_tp)
    vec = vec_ref.at[layer]

    low = grad_ref[...].astype(BF16)
    loads[0].wait()
    own_mixed = dot(wo[...], low, NT).astype(BF16)
    mixed[group] = own_mixed
    own_stats = [lse_ref[head : head + 1, :] for head in range(HEADS)]
    for head in range(HEADS):
        rows = slice(HD * head, HD * head + HD)
        own_stats.append(
            jnp.sum(own_mixed[rows, :].astype(F32) * att_ref[rows, :], axis=0, keepdims=True)
        )
    for row, stat in enumerate(own_stats):
        stats[group, row : row + 1, :] = stat
    stats[group, 2 * HEADS :, :] = jnp.zeros((8 - 2 * HEADS, ROWS), F32)

    def mixed_copies(entry, target):
        return group_copies(
            (mixed, mixed),
            (stats, stats),
            entry,
            entry,
            target,
            z,
            (mixed_send, mixed_recv, stat_send, stat_recv),
        )

    def query_copy(here, there, target):
        return remote(
            query_out.at[here],
            query_in.at[there],
            query_send.at[target],
            query_recv.at[there],
            ctx=target * RING + z,
        )

    def ring_rows(step):
        place = lax.rem(z + step + RING, RING)
        return pl.ds(pl.multiple_of(place * ROWS, ROWS), ROWS)

    def term_copy(step):
        return remote(
            low_terms.at[ring_rows(step)],
            term_slots.at[step - 1],
            kv_send.at[step - 1],
            kv_recv.at[step - 1],
            ctx=group * RING + lax.rem(z + step, RING),
        )

    pl.semaphore_wait(barrier, count)

    @pl.loop(0, group)
    def _(target):
        for copy in mixed_copies(group, target):
            copy.start()

    kv_t[...] = kv_ref[...].T
    pair[...] = jnp.zeros_like(pair)
    terms[...] = jnp.zeros_like(terms)
    small_ref[...] = jnp.zeros_like(small_ref)
    small_ref[4:5, :] = jnp.sum(grad_ref[...], axis=0, keepdims=True)
    hat, inverse = centre(resid_ref[...])
    gain_one, gain_two = vec[G1 : G1 + 1, :], vec[G2 : G2 + 1, :]
    loads[1].wait()
    hidden_grad = dot(low, wd[...], NT)
    pre = pre_ref[...]
    slope = 0.5 * (1.0 + lax.erf(pre * math.sqrt(0.5))) + pre * jnp.exp(
        -0.5 * pre * pre
    ) * (1.0 / math.sqrt(2.0 * math.pi))
    pre_grad = (hidden_grad * slope).astype(BF16)
    tp_out[...] = pre_grad
    small_ref[6:7, :] = jnp.sum(pre_grad.astype(F32), axis=0, keepdims=True)
    loads[2].wait()
    grad_two = dot(pre_grad, wu[...], NT)
    small_ref[2:3, :] = jnp.sum(grad_two * hat, axis=0, keepdims=True)
    small_ref[3:4, :] = jnp.sum(grad_two, axis=0, keepdims=True)
    norm_part[...] = grad_two * gain_two

    def attend_back(of_query, own):
        allowed = allowed_pairs(group, of_query, z)
        for head in range(HEADS):
            rows = slice(HD * head, HD * head + HD)
            lanes = slice(128 * head, 128 * head + 128)
            pair[head, :HD, :ROWS] = q_ref[of_query, rows, :]
            pair[head, HD:, ROWS:] = mixed[of_query, rows, :]
            both = dot(kv_ref[:, lanes], pair[head])
            probs = jnp.exp(both[:, :ROWS] * SCALE - stats[of_query, head : head + 1, :])
            if own:
                probs = jnp.where(allowed, probs, 0.0)
            scores = probs * (both[:, ROWS:] - stats[of_query, HEADS + head : HEADS + head + 1, :])
            scores = (scores * SCALE).astype(BF16)
            terms[:, lanes] += dot(
                jnp.concatenate([scores, probs.astype(BF16)], axis=1), pair[head], NT
            )
            back = dot(kv_t[128 * head : 128 * head + HD, :], scores)
            if own:
                query[rows, :] = back
            else:
                query_out[of_query, rows, :] = back.astype(BF16)

    @pl.loop(group + 1, GROUPS)
    def _(of_query):
        for copy in mixed_copies(of_query, of_query):
            copy.wait_recv()
        attend_back(of_query, False)
        query_copy(of_query, group, of_query).start()

    attend_back(group, True)
    low_terms[...] = terms[...].astype(BF16)
    for step in range(1, RING):
        term_copy(step).start()

    low = grad_ref[...].astype(BF16)
    pre_grad = tp_out[...]
    weight_ref[QKV_ROWS : QKV_ROWS + OUT_ROWS, :] = dot(att_ref[...].astype(BF16), low).astype(BF16)
    weight_ref[QKV_ROWS + OUT_ROWS + UP_ROWS :, :] = dot(hid_ref[...], low, TN).astype(BF16)
    hat, inverse = centre(resid_ref[...])
    normed_two = (hat * gain_two + vec[S2 : S2 + 1, :]).astype(BF16)
    weight_ref[QKV_ROWS + OUT_ROWS : QKV_ROWS + OUT_ROWS + UP_ROWS, :] = dot(
        normed_two, pre_grad, TN
    ).astype(BF16)

    out_ref[:, :384] = terms[ring_rows(0), :]
    for step in range(1, RING):
        term_copy(step).wait_recv()
        out_ref[:, :384] += term_slots[step - 1].astype(F32)

    @pl.loop(0, group)
    def _(source):
        query_copy(source, source, source).wait_recv()
        query[...] += query_in[source].astype(F32)

    for head in range(HEADS):
        across = jnp.concatenate(
            [query[HD * head : HD * head + HD, :], jnp.zeros((HD, ROWS), F32)], axis=0
        )
        out_ref[:, 384 + 128 * head : 512 + 128 * head] = across.T
    merged = turn(out_ref[...], rot_ref, -1.0).astype(BF16)
    normed_one = (hat * gain_one + vec[S1 : S1 + 1, :]).astype(BF16)
    loads[3].wait()
    grad_one = dot(merged, wq[...], NT)
    small_ref[0:1, :] = jnp.sum(grad_one * hat, axis=0, keepdims=True)
    small_ref[1:2, :] = jnp.sum(grad_one, axis=0, keepdims=True)
    small_ref[5:6, :] = jnp.sum(merged.astype(F32), axis=0, keepdims=True)
    weight_ref[:384, :] = dot(merged[:, :384], normed_one, TN).astype(BF16)
    queries_grad = dot(merged[:, 384:], normed_one, TN).astype(BF16)
    for head in range(HEADS):
        weight_ref[384 + 64 * head : 448 + 64 * head, :] = queries_grad[
            128 * head : 128 * head + 64, :
        ]
    total = tp_sum(
        norm_part[...] + grad_one * gain_one,
        my_tp,
        (tp_mine, tp_out, tp_slots, tp_gathered),
        (tp_send, tp_recv),
    )
    hat, inverse = centre(resid_ref[...])
    along = jnp.mean(total * hat, axis=-1, keepdims=True)
    level = jnp.mean(total, axis=-1, keepdims=True)
    out_ref[...] = grad_ref[...] + inverse * (total - level - hat * along)

    for step in range(1, RING):
        term_copy(step).wait_send()

    @pl.loop(0, group)
    def _(target):
        for copy in mixed_copies(group, target):
            copy.wait_send()

    @pl.loop(group + 1, GROUPS)
    def _(of_query):
        query_copy(of_query, group, of_query).wait_send()


def backward(layer, grad, residual, vec, rot, saved, wq, wo, wu, wd):
    return pl.pallas_call(
        functools.partial(backward_kernel, layer),
        name=f"layer_backward_{layer}",
        out_shape=[
            jax.ShapeDtypeStruct((ROWS, D), F32),
            jax.ShapeDtypeStruct((GRAD_ROWS, D), BF16),
            jax.ShapeDtypeStruct((8, D), F32),
        ],
        in_specs=vmem(10) + hbm(4),
        out_specs=vmem(3),
        scratch_shapes=[
            pltpu.VMEM((D, D), BF16),
            pltpu.VMEM((WIDE, D), BF16),
            pltpu.VMEM((D, D), BF16),
            pltpu.VMEM((D, D), BF16),
            pltpu.VMEM((384, KEYS), BF16),
            pltpu.VMEM((GROUPS, WIDE, ROWS), BF16),
            pltpu.VMEM((GROUPS, 8, ROWS), F32),
            pltpu.VMEM((GROUPS, WIDE, ROWS), BF16),
            pltpu.VMEM((GROUPS, WIDE, ROWS), BF16),
            pltpu.VMEM((HEADS, 128, 2 * ROWS), BF16),
            pltpu.VMEM((KEYS, 384), F32),
            pltpu.VMEM((KEYS, 384), BF16),
            pltpu.VMEM((RING - 1, ROWS, 384), BF16),
            pltpu.VMEM((WIDE, ROWS), F32),
            pltpu.VMEM((ROWS, D), F32),
            *dma_sems(4, 3, 3, *[GROUPS] * 6),
            *TP_BUFFERS,
            *TP_SEMS,
        ],
        compiler_params=pltpu.CompilerParams(
            collective_id=2 + layer, has_side_effects=True, vmem_limit_bytes=48 << 20
        ),
    )(grad, residual, vec, rot, *saved, wq, wo, wu, wd)


BIG = GRAD_ROWS // RING
SUB = BIG // RING
BIG_CUT, SUB_CUT = 288, 80
HALF = D // 2
RS_MESSAGES, AG_MESSAGES = 6, 6
FLOW_SEMS = 2 * RS_MESSAGES + 1 + 2 * AG_MESSAGES


def rows_at(start, count):
    return pl.ds(pl.multiple_of(start, 16), count)


class Axis:
    def __init__(self, place, of_place):
        self.place = place
        self.of_place = of_place
        self.right = of_place(lax.rem(place + 1, RING))
        self.left = of_place(lax.rem(place + 3, RING))

    def at(self, step):
        return lax.rem(self.place + step + RING, RING)


class ReduceScatter:
    def __init__(self, axis, src, size, cut, first, second, from_left, from_right, sems):
        self.axis, self.src, self.size, self.cut = axis, src, size, cut
        self.first, self.second = first, second
        self.from_left, self.from_right = from_left, from_right
        self.send, self.recv, self.base = sems

    def copy(self, index, src, dst, ctx):
        return remote(
            src, dst, self.send.at[self.base + index], self.recv.at[self.base + index], ctx=ctx
        )

    def copies(self):
        axis, size, cut = self.axis, self.size, self.cut
        rest = size - cut
        far, near_right, near_left = axis.at(2) * size, axis.at(1) * size, axis.at(3) * size
        return [
            self.copy(0, self.src(far, cut), self.first[0].at[pl.ds(0, cut)], axis.right),
            self.copy(1, self.src(far + cut, rest), self.second[0].at[pl.ds(0, rest)], axis.left),
            self.copy(
                2, self.src(near_right + cut, rest), self.from_left.at[pl.ds(cut, rest)], axis.right
            ),
            self.copy(3, self.src(near_left, cut), self.from_right.at[pl.ds(0, cut)], axis.left),
            self.copy(
                4, self.first[1].at[pl.ds(0, cut)], self.from_left.at[pl.ds(0, cut)], axis.right
            ),
            self.copy(
                5, self.second[1].at[pl.ds(0, rest)], self.from_right.at[pl.ds(cut, rest)], axis.left
            ),
        ]

    def start(self):
        for copy in self.copies()[:4]:
            copy.start()

    def middle(self):
        axis, size, cut = self.axis, self.size, self.cut
        rest = size - cut
        copies = self.copies()
        copies[0].wait_recv()
        self.first[1][0:cut, :] = (
            self.first[0][0:cut, :].astype(F32) + self.src(axis.at(1) * size, cut)[...].astype(F32)
        ).astype(BF16)
        copies[4].start()
        copies[1].wait_recv()
        self.second[1][0:rest, :] = (
            self.second[0][0:rest, :].astype(F32)
            + self.src(axis.at(3) * size + cut, rest)[...].astype(F32)
        ).astype(BF16)
        copies[5].start()

    def finish(self, out):
        for copy in self.copies()[2:]:
            copy.wait_recv()
        size = self.size
        out[0:size, :] = (
            self.src(self.axis.place * size, size)[...].astype(F32)
            + self.from_left[0:size, :].astype(F32)
            + self.from_right[0:size, :].astype(F32)
        ).astype(BF16)

    def drain(self):
        for copy in self.copies():
            copy.wait_send()


class AllGather:
    def __init__(self, axis, view, size, cut, sems):
        self.axis, self.view, self.size, self.cut = axis, view, size, cut
        self.send, self.recv, self.base = sems

    def copy(self, index, start, count, ctx):
        part = self.view(start, count)
        return remote(
            part, part, self.send.at[self.base + index], self.recv.at[self.base + index], ctx=ctx
        )

    def copies(self, shift):
        axis, size, cut = self.axis, self.size, self.cut
        rest = size - cut
        if shift == 0:
            own, from_left, from_right = axis.place * size, axis.at(3) * size, axis.at(1) * size
            return [
                self.copy(0, own, cut, axis.right),
                self.copy(1, own + cut, rest, axis.left),
                self.copy(2, own + cut, rest, axis.right),
                self.copy(3, own, cut, axis.left),
                self.copy(4, from_left, cut, axis.right),
                self.copy(5, from_right + cut, rest, axis.left),
            ]
        from_left, from_right, far = axis.at(3) * size, axis.at(1) * size, axis.at(2) * size
        return [
            self.copy(0, from_left, cut, axis.right),
            self.copy(1, from_right + cut, rest, axis.left),
            self.copy(2, from_left + cut, rest, axis.right),
            self.copy(3, from_right, cut, axis.left),
            self.copy(4, far, cut, axis.right),
            self.copy(5, far + cut, rest, axis.left),
        ]

    def start(self):
        for copy in self.copies(0)[:4]:
            copy.start()

    def middle(self):
        come, go = self.copies(1), self.copies(0)
        come[0].wait_recv()
        go[4].start()
        come[1].wait_recv()
        go[5].start()

    def finish(self):
        for copy in self.copies(1)[2:]:
            copy.wait_recv()

    def drain(self):
        for copy in self.copies(0):
            copy.wait_send()


FLOW_BUFFERS = [
    pltpu.VMEM((BIG_CUT, HALF), BF16),
    pltpu.VMEM((BIG_CUT, HALF), BF16),
    pltpu.VMEM((BIG - BIG_CUT, HALF), BF16),
    pltpu.VMEM((BIG - BIG_CUT, HALF), BF16),
    pltpu.VMEM((BIG, HALF), BF16),
    pltpu.VMEM((BIG, HALF), BF16),
    pltpu.VMEM((BIG, HALF), BF16),
    pltpu.VMEM((SUB_CUT, HALF), BF16),
    pltpu.VMEM((SUB_CUT, HALF), BF16),
    pltpu.VMEM((SUB - SUB_CUT, HALF), BF16),
    pltpu.VMEM((SUB - SUB_CUT, HALF), BF16),
    pltpu.VMEM((SUB, HALF), BF16),
    pltpu.VMEM((SUB, HALF), BF16),
    pltpu.VMEM((SUB, HALF), BF16),
    pltpu.VMEM((SUB, HALF), BF16),
    pltpu.SemaphoreType.DMA((FLOW_SEMS,)),
    pltpu.SemaphoreType.DMA((FLOW_SEMS,)),
]


class Flow:
    def __init__(self, axes, across, src_ref, out_ref, half, scratch):
        one, two = axes
        (a0, a1, b0, b1, left, right, self.big, c0, c1, d0, d1, left2, right2, self.sub, self.other) = (
            scratch[:15]
        )
        self.send, self.recv = scratch[15:]
        lanes = pl.ds(half * HALF, HALF)

        def src(start, count):
            return src_ref.at[rows_at(start, count), lanes]

        def middle_src(start, count):
            return self.big.at[rows_at(start, count)]

        def out(start, count):
            return out_ref.at[rows_at(start, count), lanes]

        corner = one.place * BIG

        def out_sub(start, count):
            return out_ref.at[rows_at(corner + start, count), lanes]

        self.out_piece = out_sub(two.place * SUB, SUB)
        self.across = across

        def sems(base):
            return (self.send, self.recv, base)

        self.one = ReduceScatter(one, src, BIG, BIG_CUT, (a0, a1), (b0, b1), left, right, sems(0))
        self.two = ReduceScatter(
            two, middle_src, SUB, SUB_CUT, (c0, c1), (d0, d1), left2, right2, sems(6)
        )
        self.three = AllGather(two, out_sub, SUB, SUB_CUT, sems(13))
        self.four = AllGather(one, out, BIG, BIG_CUT, sems(19))

    def swap(self):
        return remote(self.sub, self.other, self.send.at[12], self.recv.at[12], ctx=self.across)

    def step(self, number):
        if number == 0:
            self.one.start()
        elif number == 1:
            self.one.middle()
        elif number == 2:
            self.one.finish(self.big)
            self.two.start()
        elif number == 3:
            self.two.middle()
        elif number == 4:
            self.two.finish(self.sub)
            self.swap().start()
        elif number == 5:
            self.swap().wait_recv()
            self.out_piece[...] = (
                self.sub[...].astype(F32) + self.other[...].astype(F32)
            ).astype(BF16)
            self.three.start()
        elif number == 6:
            self.three.middle()
        elif number == 7:
            self.three.finish()
            self.four.start()
        elif number == 8:
            self.four.middle()
        elif number == 9:
            self.four.finish()

    def drain(self):
        self.one.drain()
        self.two.drain()
        self.swap().wait_send()
        self.three.drain()
        self.four.drain()


STEPS = 10


def reduce_kernel(w0, w1, s0, s1, o0, o1, small_out, small, small_slots, small_send, small_recv, *flow):
    me = lax.axis_index("ctx")
    my_tp = lax.axis_index("tp")
    z = lax.rem(me, 4)
    x = lax.rem(me // 4, 2)
    y = me // 8
    across = me + 4 - 8 * x
    z_axis = Axis(z, lambda place: me - z + place)
    y_axis = Axis(y, lambda place: me + (place - y) * 8)
    z_peers = [z_axis.of_place(z_axis.at(step)) for step in (1, 2, 3)]
    y_peers = [y_axis.of_place(y_axis.at(step)) for step in (1, 2, 3)]
    tp_peers = [lax.rem(my_tp + step, TP) for step in (1, 2, 3)]
    barrier, count = greet(z_peers + y_peers + [across], tp_peers)
    pl.semaphore_wait(barrier, count)

    flows = []
    per = len(FLOW_BUFFERS)
    for index, (src, out, half) in enumerate(((w1, o1, 0), (w1, o1, 1), (w0, o0, 0), (w0, o0, 1))):
        axes = (z_axis, y_axis) if half == 0 else (y_axis, z_axis)
        flows.append(Flow(axes, across, src, out, half, flow[per * index : per * index + per]))

    def small_copies(stage, place, peers, tp):
        return [
            remote(
                small.at[stage],
                small_slots.at[stage, place],
                small_send.at[stage, step],
                small_recv.at[stage, step],
                **({"tp": peer} if tp else {"ctx": peer}),
            )
            for step, peer in enumerate(peers)
        ]

    stages = [
        small_copies(0, z, z_peers, False),
        small_copies(1, y, y_peers, False),
        small_copies(2, x, [across], False),
        small_copies(3, my_tp, tp_peers, True),
    ]
    places = (z, y, x, my_tp)

    def small_total(stage):
        for copy in stages[stage]:
            copy.wait_recv()
        small_slots[stage, places[stage]] = small[stage]
        total = small_slots[stage, 0]
        for place in range(1, 2 if stage == 2 else 4):
            total = total + small_slots[stage, place]
        return total

    def small_step(number):
        if number == 0:
            small[0, 0:8, :] = s0[...]
            small[0, 8:16, :] = s1[...]
        elif number < 4:
            small[number] = small_total(number - 1)
        if number < 4:
            for copy in stages[number]:
                copy.start()
        elif number == 4:
            total = small_total(3)
            row = lax.rem(lax.broadcasted_iota(jnp.int32, (16, D), 0), 8)
            small_out[...] = jnp.where(row < 4, total, small[3])

    for number in range(STEPS):
        if number < 5:
            small_step(number)
        for one in flows:
            one.step(number)
    for one in flows:
        one.drain()
    for copies in stages:
        for copy in copies:
            copy.wait_send()


def reduce_all(w0, w1, s0, s1):
    return pl.pallas_call(
        reduce_kernel,
        name="weight_gradient_sum",
        out_shape=[
            jax.ShapeDtypeStruct((GRAD_ROWS, D), BF16),
            jax.ShapeDtypeStruct((GRAD_ROWS, D), BF16),
            jax.ShapeDtypeStruct((16, D), F32),
        ],
        in_specs=vmem(4),
        out_specs=vmem(3),
        scratch_shapes=[
            pltpu.VMEM((4, 16, D), F32),
            pltpu.VMEM((4, 4, 16, D), F32),
            pltpu.SemaphoreType.DMA((4, 3)),
            pltpu.SemaphoreType.DMA((4, 3)),
            *(FLOW_BUFFERS * 4),
        ],
        compiler_params=pltpu.CompilerParams(
            collective_id=4, has_side_effects=True, vmem_limit_bytes=56 << 20
        ),
    )(w0, w1, s0, s1)


def rotary_planes(positions):
    halves = ROT // 2
    inverse = jnp.power(10000.0, -2.0 * jnp.arange(halves, dtype=F32) / ROT)
    angles = positions[:, None] * inverse[None, :]
    cosine, sine = jnp.cos(angles), jnp.sin(angles)
    rows = positions.shape[0]
    rest = 128 - ROT
    return jnp.stack(
        [
            jnp.concatenate([cosine, cosine, jnp.ones((rows, rest), F32)], axis=1),
            jnp.concatenate(
                [jnp.zeros((rows, halves), F32), sine, jnp.zeros((rows, rest), F32)], axis=1
            ),
            jnp.concatenate([-sine, jnp.zeros((rows, halves + rest), F32)], axis=1),
        ]
    )


def packed_qkv(array):
    lead = array.shape[:-2]
    parts = array.reshape(*lead, 3, HEADS, HD)
    pairs = jnp.stack([parts[..., 1, :, :], parts[..., 2, :, :]], axis=-2)
    queries = jnp.stack([parts[..., 0, :, :], jnp.zeros_like(parts[..., 0, :, :])], axis=-2)
    return jnp.concatenate(
        [pairs.reshape(*lead, 2 * HEADS * HD), queries.reshape(*lead, 2 * HEADS * HD)], axis=-1
    )


def on_device(
    layer_input,
    attention_gain,
    attention_shift,
    feedforward_gain,
    feedforward_shift,
    query_key_value_weight,
    query_key_value_bias,
    attention_out_weight,
    dense_bias,
    expand_weight,
    expand_bias,
    down_weight,
    down_bias,
    output_grad,
):
    me = lax.axis_index("ctx")
    positions = (me * ROWS + jnp.arange(ROWS, dtype=jnp.int32)).astype(F32)
    rot = rotary_planes(positions)
    vec = jnp.stack(
        [
            attention_gain.astype(F32),
            attention_shift.astype(F32),
            feedforward_gain.astype(F32),
            feedforward_shift.astype(F32),
            expand_bias.astype(F32),
            dense_bias.astype(F32) + down_bias.astype(F32),
            packed_qkv(query_key_value_bias.astype(F32)),
            jnp.zeros((LAYERS, D), F32),
        ],
        axis=1,
    )
    wq = packed_qkv(query_key_value_weight)
    residual = layer_input[0].astype(F32)
    residuals, saved = [], []
    for layer in range(LAYERS):
        residuals.append(residual)
        residual, *kept = forward(
            layer, residual, vec, rot, wq, attention_out_weight, expand_weight, down_weight
        )
        saved.append(kept)
    output = residual.astype(BF16)
    grad = output_grad[0].astype(F32)
    weights, smalls = [None] * LAYERS, [None] * LAYERS
    for layer in reversed(range(LAYERS)):
        grad, weights[layer], smalls[layer] = backward(
            layer,
            grad,
            residuals[layer],
            vec,
            rot,
            saved[layer],
            wq,
            attention_out_weight,
            expand_weight,
            down_weight,
        )
    total_0, total_1, small = reduce_all(weights[0], weights[1], smalls[0], smalls[1])
    small = small.reshape(LAYERS, 8, D)
    totals = (total_0, total_1)

    def qkv_grad(total):
        pairs = total[:384].reshape(HEADS, 2, HD, D)
        queries = total[384:QKV_ROWS].reshape(1, HEADS, HD, D)
        slots = jnp.concatenate([queries, pairs.transpose(1, 0, 2, 3)], axis=0)
        return slots.reshape(3 * HEADS * HD, D).T.reshape(D, 3, HEADS * HD)

    def part(start, count):
        return jnp.stack([total[start : start + count] for total in totals]).astype(F32)

    bias = small[:, 5]
    pairs = bias[:, :384].reshape(LAYERS, HEADS, 2, HD)
    queries = bias[:, 384:].reshape(LAYERS, HEADS, 2, HD)[:, :, 0]
    merged_bias_grad = jnp.stack([queries, pairs[:, :, 0], pairs[:, :, 1]], axis=1).reshape(
        LAYERS, 3, HEADS * HD
    )
    return (
        output[None],
        grad[None],
        small[:, 0],
        small[:, 1],
        small[:, 2],
        small[:, 3],
        jnp.stack([qkv_grad(total) for total in totals]).astype(F32),
        merged_bias_grad,
        part(QKV_ROWS, OUT_ROWS),
        small[:, 4],
        part(QKV_ROWS + OUT_ROWS, UP_ROWS),
        small[:, 6],
        part(QKV_ROWS + OUT_ROWS + UP_ROWS, DOWN_ROWS),
        small[:, 4],
    )


def solution(mesh):
    in_specs = (
        P(None, "ctx", None),
        P(),
        P(),
        P(),
        P(),
        P(None, None, None, "tp"),
        P(None, None, "tp"),
        P(None, "tp", None),
        P(),
        P(None, None, "tp"),
        P(None, "tp"),
        P(None, "tp", None),
        P(),
        P(None, "ctx", None),
    )
    out_specs = (
        P(None, "ctx", None),
        P(None, "ctx", None),
        P(),
        P(),
        P(),
        P(),
        P(None, None, None, "tp"),
        P(None, None, "tp"),
        P(None, "tp", None),
        P(),
        P(None, None, "tp"),
        P(None, "tp"),
        P(None, "tp", None),
        P(),
    )
    return jax.shard_map(
        on_device, mesh=mesh, in_specs=in_specs, out_specs=out_specs, check_vma=False
    )
```

```python
import functools
import math

import jax
import jax.numpy as jnp
from jax import lax
from jax.experimental import pallas as pl
from jax.experimental.pallas import tpu as pltpu
from jax.sharding import PartitionSpec as P

HD = 64
ROT = 16
LAYERS = 2
NORM_EPSILON = 1e-05
MASKED = -1e30
F32 = jnp.float32
BF16 = jnp.bfloat16
ROWS = 128
D = 768
HEADS = 3
CTX = 32
TP = 4
RING = 4
GROUPS = CTX // RING
KEYS = RING * ROWS
WIDE = HEADS * HD
QUARTER = ROWS // TP
SCALE = HD**-0.5
QKV = 3 * WIDE
HALF = D // 2
FF_ROWS, AT_ROWS = 2 * D, QKV + WIDE
PHASES = 2 * LAYERS

NN = (((1,), (0,)), ((), ()))
NT = (((1,), (1,)), ((), ()))
TN = (((0,), (0,)), ((), ()))


def dot(a, b, dims=NN):
    return lax.dot_general(a, b, dims, preferred_element_type=F32)


def remote(src, dst, send, recv, ctx=None, tp=None):
    where = {}
    if ctx is not None:
        where["ctx"] = ctx
    if tp is not None:
        where["tp"] = tp
    return pltpu.make_async_remote_copy(
        src_ref=src,
        dst_ref=dst,
        send_sem=send,
        recv_sem=recv,
        device_id=where,
        device_id_type=pl.DeviceIdType.MESH,
    )


def greet(ctx_peers, tp_peers):
    barrier = pltpu.get_barrier_semaphore()
    for peer in ctx_peers:
        pl.semaphore_signal(
            barrier, inc=1, device_id={"ctx": peer}, device_id_type=pl.DeviceIdType.MESH
        )
    for peer in tp_peers:
        pl.semaphore_signal(
            barrier, inc=1, device_id={"tp": peer}, device_id_type=pl.DeviceIdType.MESH
        )
    return barrier, len(ctx_peers) + len(tp_peers)


def centre(residual):
    mean_value = jnp.mean(residual, axis=-1, keepdims=True)
    centred = residual - mean_value
    variance = jnp.mean(centred * centred, axis=-1, keepdims=True)
    inverse = lax.rsqrt(variance + NORM_EPSILON)
    return centred * inverse, inverse


def tp_sum(part, my_tp, phase, s):
    s.tp_mine[...] = part
    s.tp_out[...] = part.astype(BF16)
    slots, gathered = s.tp_slots.at[phase], s.tp_gathered.at[phase]
    send, recv = s.tp_send.at[phase], s.tp_recv.at[phase]

    def quarter(place):
        return pl.ds(pl.multiple_of(place * QUARTER, QUARTER), QUARTER)

    def spread(step):
        peer = lax.rem(my_tp + step, TP)
        return remote(
            s.tp_out.at[quarter(peer)], slots.at[step - 1], send.at[step - 1], recv.at[step - 1], tp=peer
        )

    def collect(step, place):
        return remote(
            gathered.at[quarter(place)],
            gathered.at[quarter(place)],
            send.at[TP - 2 + step],
            recv.at[TP - 2 + step],
            tp=lax.rem(my_tp + step, TP),
        )

    for step in range(1, TP):
        spread(step).start()
    total = s.tp_mine[quarter(my_tp), :]
    for step in range(1, TP):
        spread(step).wait_recv()
        total = total + slots[step - 1].astype(F32)
    gathered[quarter(my_tp), :] = total.astype(BF16)
    for step in range(1, TP):
        collect(step, my_tp).start()
    for step in range(1, TP):
        collect(step, lax.rem(my_tp + TP - step, TP)).wait_recv()
    for step in range(1, TP):
        spread(step).wait_send()
        collect(step, my_tp).wait_send()
    return gathered[...].astype(F32)


RS_MESSAGES, AG_MESSAGES = 6, 6
FLOW_SEMS = 2 * RS_MESSAGES + 1 + 2 * AG_MESSAGES


def rows_at(start, count):
    return pl.ds(pl.multiple_of(start, 16), count)


class Axis:
    def __init__(self, place, of_place):
        self.place = place
        self.of_place = of_place
        self.right = of_place(lax.rem(place + 1, RING))
        self.left = of_place(lax.rem(place + 3, RING))

    def at(self, step):
        return lax.rem(self.place + step + RING, RING)


class ReduceScatter:
    def __init__(self, axis, src, size, cut, first, second, from_left, from_right, sems):
        self.axis, self.src, self.size, self.cut = axis, src, size, cut
        self.first, self.second = first, second
        self.from_left, self.from_right = from_left, from_right
        self.send, self.recv, self.base = sems

    def copy(self, index, src, dst, ctx):
        return remote(
            src, dst, self.send.at[self.base + index], self.recv.at[self.base + index], ctx=ctx
        )

    def copies(self):
        axis, size, cut = self.axis, self.size, self.cut
        rest = size - cut
        far, near_right, near_left = axis.at(2) * size, axis.at(1) * size, axis.at(3) * size
        return [
            self.copy(0, self.src(far, cut), self.first[0].at[pl.ds(0, cut)], axis.right),
            self.copy(1, self.src(far + cut, rest), self.second[0].at[pl.ds(0, rest)], axis.left),
            self.copy(
                2, self.src(near_right + cut, rest), self.from_left.at[pl.ds(cut, rest)], axis.right
            ),
            self.copy(3, self.src(near_left, cut), self.from_right.at[pl.ds(0, cut)], axis.left),
            self.copy(
                4, self.first[1].at[pl.ds(0, cut)], self.from_left.at[pl.ds(0, cut)], axis.right
            ),
            self.copy(
                5, self.second[1].at[pl.ds(0, rest)], self.from_right.at[pl.ds(cut, rest)], axis.left
            ),
        ]

    def start(self):
        for copy in self.copies()[:4]:
            copy.start()

    def middle(self):
        axis, size, cut = self.axis, self.size, self.cut
        rest = size - cut
        copies = self.copies()
        copies[0].wait_recv()
        self.first[1][0:cut, :] = (
            self.first[0][0:cut, :].astype(F32) + self.src(axis.at(1) * size, cut)[...].astype(F32)
        ).astype(BF16)
        copies[4].start()
        copies[1].wait_recv()
        self.second[1][0:rest, :] = (
            self.second[0][0:rest, :].astype(F32)
            + self.src(axis.at(3) * size + cut, rest)[...].astype(F32)
        ).astype(BF16)
        copies[5].start()

    def finish(self, out):
        for copy in self.copies()[2:]:
            copy.wait_recv()
        size = self.size
        out[0:size, :] = (
            self.src(self.axis.place * size, size)[...].astype(F32)
            + self.from_left[0:size, :].astype(F32)
            + self.from_right[0:size, :].astype(F32)
        ).astype(BF16)

    def drain(self):
        for copy in self.copies():
            copy.wait_send()


class AllGather:
    def __init__(self, axis, view, size, cut, sems):
        self.axis, self.view, self.size, self.cut = axis, view, size, cut
        self.send, self.recv, self.base = sems

    def copy(self, index, start, count, ctx):
        part = self.view(start, count)
        return remote(
            part, part, self.send.at[self.base + index], self.recv.at[self.base + index], ctx=ctx
        )

    def copies(self, shift):
        axis, size, cut = self.axis, self.size, self.cut
        rest = size - cut
        if shift == 0:
            own, from_left, from_right = axis.place * size, axis.at(3) * size, axis.at(1) * size
            return [
                self.copy(0, own, cut, axis.right),
                self.copy(1, own + cut, rest, axis.left),
                self.copy(2, own + cut, rest, axis.right),
                self.copy(3, own, cut, axis.left),
                self.copy(4, from_left, cut, axis.right),
                self.copy(5, from_right + cut, rest, axis.left),
            ]
        from_left, from_right, far = axis.at(3) * size, axis.at(1) * size, axis.at(2) * size
        return [
            self.copy(0, from_left, cut, axis.right),
            self.copy(1, from_right + cut, rest, axis.left),
            self.copy(2, from_left + cut, rest, axis.right),
            self.copy(3, from_right, cut, axis.left),
            self.copy(4, far, cut, axis.right),
            self.copy(5, far + cut, rest, axis.left),
        ]

    def start(self):
        for copy in self.copies(0)[:4]:
            copy.start()

    def middle(self):
        come, go = self.copies(1), self.copies(0)
        come[0].wait_recv()
        go[4].start()
        come[1].wait_recv()
        go[5].start()

    def finish(self):
        for copy in self.copies(1)[2:]:
            copy.wait_recv()

    def drain(self):
        for copy in self.copies(0):
            copy.wait_send()


STEPS = 10


def cuts(rows):
    big, sub = rows // RING, rows // RING // RING
    return big // 32 * 16, sub // 32 * 16


def flow_buffers(rows):
    big, sub = rows // RING, rows // RING // RING
    big_cut, sub_cut = cuts(rows)
    counts = [big_cut] * 2 + [big - big_cut] * 2 + [big] * 3
    counts += [sub_cut] * 2 + [sub - sub_cut] * 2 + [sub] * 4
    return [pltpu.VMEM((count, HALF), BF16) for count in counts] + dma_sems(FLOW_SEMS, FLOW_SEMS)


class Flow:
    def __init__(self, axes, across, src_ref, out_ref, half, scratch):
        self.at = 0
        rows = src_ref.shape[0]
        big, sub = rows // RING, rows // RING // RING
        big_cut, sub_cut = cuts(rows)
        one, two = axes
        (a0, a1, b0, b1, left, right, self.big, c0, c1, d0, d1, left2, right2, self.sub, self.other) = (
            scratch[:15]
        )
        self.send, self.recv = scratch[15:]
        lanes = pl.ds(half * HALF, HALF)

        def src(start, count):
            return src_ref.at[rows_at(start, count), lanes]

        def middle_src(start, count):
            return self.big.at[rows_at(start, count)]

        def out(start, count):
            return out_ref.at[rows_at(start, count), lanes]

        corner = one.place * big

        def out_sub(start, count):
            return out_ref.at[rows_at(corner + start, count), lanes]

        self.out_piece = out_sub(two.place * sub, sub)
        self.across = across

        def sems(base):
            return (self.send, self.recv, base)

        self.one = ReduceScatter(one, src, big, big_cut, (a0, a1), (b0, b1), left, right, sems(0))
        self.two = ReduceScatter(
            two, middle_src, sub, sub_cut, (c0, c1), (d0, d1), left2, right2, sems(6)
        )
        self.three = AllGather(two, out_sub, sub, sub_cut, sems(13))
        self.four = AllGather(one, out, big, big_cut, sems(19))

    def swap(self):
        return remote(self.sub, self.other, self.send.at[12], self.recv.at[12], ctx=self.across)

    def advance(self):
        if self.at < STEPS:
            self.step(self.at)
            self.at += 1

    def step(self, number):
        if number == 0:
            self.one.start()
        elif number == 1:
            self.one.middle()
        elif number == 2:
            self.one.finish(self.big)
            self.two.start()
        elif number == 3:
            self.two.middle()
        elif number == 4:
            self.two.finish(self.sub)
            self.swap().start()
        elif number == 5:
            self.swap().wait_recv()
            self.out_piece[...] = (
                self.sub[...].astype(F32) + self.other[...].astype(F32)
            ).astype(BF16)
            self.three.start()
        elif number == 6:
            self.three.middle()
        elif number == 7:
            self.three.finish()
            self.four.start()
        elif number == 8:
            self.four.middle()
        elif number == 9:
            self.four.finish()

    def drain(self):
        self.one.drain()
        self.two.drain()
        self.swap().wait_send()
        self.three.drain()
        self.four.drain()


def dma_sems(*counts):
    return [
        pltpu.SemaphoreType.DMA(count if isinstance(count, tuple) else (count,)) for count in counts
    ]


def scratch():
    sems = dma_sems
    named = dict(
        wq=pltpu.VMEM((LAYERS, QKV, D), BF16),
        wo=pltpu.VMEM((LAYERS, WIDE, D), BF16),
        wu=pltpu.VMEM((LAYERS, D, D), BF16),
        wd=pltpu.VMEM((LAYERS, D, D), BF16),
        resid=pltpu.VMEM((LAYERS, ROWS, D), F32),
        branch=pltpu.VMEM((ROWS, D), F32),
        grad=pltpu.VMEM((ROWS, D), F32),
        norm_part=pltpu.VMEM((ROWS, D), F32),
        pre=pltpu.VMEM((LAYERS, ROWS, D), F32),
        hid=pltpu.VMEM((LAYERS, ROWS, D), BF16),
        kv_t=pltpu.VMEM((LAYERS, 2 * WIDE, KEYS), BF16),
        kv=pltpu.VMEM((LAYERS, KEYS, 2 * WIDE), BF16),
        q=pltpu.VMEM((LAYERS, GROUPS, WIDE, ROWS), BF16),
        att=pltpu.VMEM((LAYERS, WIDE, ROWS), F32),
        lse=pltpu.VMEM((LAYERS, 8, ROWS), F32),
        part_out=pltpu.VMEM((LAYERS, GROUPS, WIDE, ROWS), BF16),
        part_in=pltpu.VMEM((LAYERS, GROUPS, WIDE, ROWS), BF16),
        lse_out=pltpu.VMEM((LAYERS, GROUPS, 8, ROWS), F32),
        lse_in=pltpu.VMEM((LAYERS, GROUPS, 8, ROWS), F32),
        mixed=pltpu.VMEM((LAYERS, GROUPS, WIDE, ROWS), BF16),
        stats=pltpu.VMEM((LAYERS, GROUPS, 8, ROWS), F32),
        query_out=pltpu.VMEM((LAYERS, GROUPS, WIDE, ROWS), BF16),
        query_in=pltpu.VMEM((LAYERS, GROUPS, WIDE, ROWS), BF16),
        pair=pltpu.VMEM((HEADS, 128, 2 * ROWS), BF16),
        terms=pltpu.VMEM((KEYS, 2 * WIDE), F32),
        low_terms=pltpu.VMEM((LAYERS, KEYS, 2 * WIDE), BF16),
        term_slots=pltpu.VMEM((LAYERS, RING - 1, ROWS, 2 * WIDE), BF16),
        query=pltpu.VMEM((WIDE, ROWS), F32),
        merged_t=pltpu.VMEM((QKV, ROWS), BF16),
        ff=pltpu.VMEM((LAYERS, FF_ROWS, D), BF16),
        at=pltpu.VMEM((LAYERS, AT_ROWS, D), BF16),
        tp_mine=pltpu.VMEM((ROWS, D), F32),
        tp_out=pltpu.VMEM((ROWS, D), BF16),
        tp_slots=pltpu.VMEM((PHASES, TP - 1, QUARTER, D), BF16),
        tp_gathered=pltpu.VMEM((PHASES, ROWS, D), BF16),
        small=pltpu.VMEM((4, 16, D), F32),
        small_slots=pltpu.VMEM((4, 4, 16, D), F32),
    )
    for name, shape in dict(
        load=(LAYERS, 4),
        kv_send=(LAYERS, 3),
        kv_recv=(LAYERS, 3),
        term_send=(LAYERS, 3),
        term_recv=(LAYERS, 3),
        tp_send=(PHASES, 2 * TP - 2),
        tp_recv=(PHASES, 2 * TP - 2),
        small_send=(4, 3),
        small_recv=(4, 3),
    ).items():
        named[name] = sems(shape)[0]
    for name in ("q", "part", "lse", "mixed", "stat", "query"):
        named[name + "_go"] = sems((LAYERS, GROUPS))[0]
        named[name + "_come"] = sems((LAYERS, GROUPS))[0]
    return named


class Names:
    def __init__(self, named):
        self.__dict__.update(named)


def rotated(values, rot_ref, sign):
    cosine, sine = rot_ref[0], rot_ref[1] * sign
    rows = []
    for head in range(HEADS):
        start = HD * head
        one, two = values[start : start + 8, :], values[start + 8 : start + 16, :]
        rows.append(one * cosine - two * sine)
        rows.append(two * cosine + one * sine)
        rows.append(values[start + 16 : start + HD, :])
    return jnp.concatenate(rows, axis=0)


def step_kernel(
    x_ref,
    out_grad_ref,
    g1_ref,
    s1_ref,
    g2_ref,
    s2_ref,
    bqkv_ref,
    dense_bias_ref,
    bup_ref,
    down_bias_ref,
    rot_ref,
    wq_hbm,
    wo_hbm,
    wu_hbm,
    wd_hbm,
    out_ref,
    in_grad_ref,
    ff_out,
    at_out,
    g1_out,
    s1_out,
    g2_out,
    s2_out,
    bias_out,
    bqkv_out,
    bup_out,
    *refs,
):
    names = list(scratch())
    s = Names(zip(names, refs))
    flow_refs = refs[len(names) :]
    me = lax.axis_index("ctx")
    my_tp = lax.axis_index("tp")
    z, group = lax.rem(me, RING), me // RING
    weights = ((wq_hbm, s.wq), (wu_hbm, s.wu), (wd_hbm, s.wd), (wo_hbm, s.wo))

    def load(layer, index):
        src, dst = weights[index]
        return pltpu.make_async_copy(src.at[layer], dst.at[layer], s.load.at[layer, index])

    for layer in range(LAYERS):
        for index in range(4):
            load(layer, index).start()
    ring_peers = [group * RING + lax.rem(z + step, RING) for step in range(1, RING)]
    column_peers = [lax.rem(group + step, GROUPS) * RING + z for step in range(1, GROUPS)]
    tp_peers = [lax.rem(my_tp + step, TP) for step in range(1, TP)]
    barrier, greeted = greet(ring_peers + column_peers, tp_peers)

    def vector(ref, layer):
        return ref[...].astype(F32)[layer : layer + 1, :]

    def ring_part(step):
        place = lax.rem(z + step + RING, RING)
        return pl.ds(pl.multiple_of(place * ROWS, ROWS), ROWS)

    def to_group(src, dst, send, recv, target):
        return remote(src, dst, send, recv, ctx=target * RING + z)

    def allowed_pairs():
        key_pos = lax.broadcasted_iota(jnp.int32, (KEYS, ROWS), 0)
        query_pos = z * ROWS + lax.broadcasted_iota(jnp.int32, (KEYS, ROWS), 1)
        return key_pos <= query_pos

    def kv_copy(layer, step, place):
        lanes = ring_part(place)
        return remote(
            s.kv_t.at[layer, :, lanes],
            s.kv_t.at[layer, :, lanes],
            s.kv_send.at[layer, step - 1],
            s.kv_recv.at[layer, step - 1],
            ctx=group * RING + lax.rem(z + step, RING),
        )

    def q_copy(layer, target, source):
        return to_group(
            s.q.at[layer, source],
            s.q.at[layer, source],
            s.q_go.at[layer, target],
            s.q_come.at[layer, source],
            target,
        )

    def part_copies(layer, here, there, target):
        return (
            to_group(
                s.part_out.at[layer, here],
                s.part_in.at[layer, there],
                s.part_go.at[layer, target],
                s.part_come.at[layer, there],
                target,
            ),
            to_group(
                s.lse_out.at[layer, here],
                s.lse_in.at[layer, there],
                s.lse_go.at[layer, target],
                s.lse_come.at[layer, there],
                target,
            ),
        )

    def mixed_copies(layer, entry, target):
        return (
            to_group(
                s.mixed.at[layer, entry],
                s.mixed.at[layer, entry],
                s.mixed_go.at[layer, target],
                s.mixed_come.at[layer, entry],
                target,
            ),
            to_group(
                s.stats.at[layer, entry],
                s.stats.at[layer, entry],
                s.stat_go.at[layer, target],
                s.stat_come.at[layer, entry],
                target,
            ),
        )

    def query_copy(layer, here, there, target):
        return to_group(
            s.query_out.at[layer, here],
            s.query_in.at[layer, there],
            s.query_go.at[layer, target],
            s.query_come.at[layer, there],
            target,
        )

    def term_copy(layer, step):
        return remote(
            s.low_terms.at[layer, ring_part(step)],
            s.term_slots.at[layer, step - 1],
            s.term_send.at[layer, step - 1],
            s.term_recv.at[layer, step - 1],
            ctx=group * RING + lax.rem(z + step, RING),
        )

    def attend(layer, of_query, own):
        for head in range(HEADS):
            rows = slice(HD * head, HD * head + HD)
            keys = s.kv[layer, :, 128 * head : 128 * head + HD]
            scores = dot(keys, s.q[layer, of_query, rows, :]) * SCALE
            if own:
                scores = jnp.where(allowed_pairs(), scores, MASKED)
            highest = jnp.max(scores, axis=0, keepdims=True)
            weights_of = jnp.exp(scores - highest)
            total = jnp.sum(weights_of, axis=0, keepdims=True)
            values_t = s.kv_t[layer, 128 * head + HD : 128 * head + 128, :]
            attended = dot(values_t, weights_of.astype(BF16)) / total
            log_total = highest + jnp.log(total)
            if own:
                s.att[layer, rows, :] = attended
                s.lse[layer, head : head + 1, :] = log_total
            else:
                s.part_out[layer, of_query, rows, :] = attended.astype(BF16)
                s.lse_out[layer, of_query, head : head + 1, :] = log_total

    def forward(layer):
        hat, _ = centre(s.resid[layer])
        normed = (hat * vector(g1_ref, layer) + vector(s1_ref, layer)).astype(BF16)
        load(layer, 0).wait()
        own = ring_part(0)
        for slot in range(3):
            rows = slice(WIDE * slot, WIDE * slot + WIDE)
            bias = bqkv_ref[slot].astype(F32)[layer : layer + 1, :]
            values = (dot(normed, s.wq[layer, rows, :], NT) + bias).T
            if slot < 2:
                values = rotated(values, rot_ref, 1.0)
            values = values.astype(BF16)
            if slot == 0:
                s.q[layer, group] = values
            else:
                for head in range(HEADS):
                    start = 128 * head + HD * (slot - 1)
                    s.kv_t[layer, start : start + HD, own] = values[HD * head : HD * head + HD, :]
        if layer == 0:
            pl.semaphore_wait(barrier, greeted)
        for step in range(1, RING):
            kv_copy(layer, step, 0).start()

        @pl.loop(0, group)
        def _(target):
            q_copy(layer, target, group).start()

        normed = (hat * vector(g2_ref, layer) + vector(s2_ref, layer)).astype(BF16)
        load(layer, 1).wait()
        pre = dot(normed, s.wu[layer]) + vector(bup_ref, layer)
        s.pre[layer] = pre
        hidden = (pre * (1.0 + lax.erf(pre * math.sqrt(0.5))) * 0.5).astype(BF16)
        s.hid[layer] = hidden
        load(layer, 2).wait()
        s.branch[...] = dot(hidden, s.wd[layer])
        for step in range(1, RING):
            kv_copy(layer, step, -step).wait_recv()
        s.kv[layer] = s.kv_t[layer].T
        s.lse[layer] = jnp.zeros((8, ROWS), F32)

        @pl.loop(group + 1, GROUPS)
        def _(of_query):
            q_copy(layer, of_query, of_query).wait_recv()
            s.lse_out[layer, of_query] = jnp.zeros((8, ROWS), F32)
            attend(layer, of_query, False)
            for copy in part_copies(layer, of_query, group, of_query):
                copy.start()

        attend(layer, group, True)

        @pl.loop(0, group)
        def _(source):
            for copy in part_copies(layer, source, source, source):
                copy.wait_recv()
            old, new = s.lse[layer], s.lse_in[layer, source]
            highest = jnp.maximum(old, new)
            old_part, new_part = jnp.exp(old - highest), jnp.exp(new - highest)
            total = old_part + new_part
            s.lse[layer] = highest + jnp.log(total)
            old_part, new_part = old_part / total, new_part / total
            for head in range(HEADS):
                rows = slice(HD * head, HD * head + HD)
                s.att[layer, rows, :] = s.att[layer, rows, :] * old_part[head : head + 1, :] + (
                    s.part_in[layer, source, rows, :].astype(F32) * new_part[head : head + 1, :]
                )

        load(layer, 3).wait()
        branch = s.branch[...] + dot(s.att[layer].astype(BF16), s.wo[layer], TN)
        branch = tp_sum(branch, my_tp, layer, s)
        bias = vector(dense_bias_ref, layer) + vector(down_bias_ref, layer)
        residual = s.resid[layer] + branch + bias
        if layer + 1 < LAYERS:
            s.resid[layer + 1] = residual
        else:
            out_ref[...] = residual.astype(BF16)

    def attend_back(layer, of_query, own):
        for head in range(HEADS):
            rows = slice(HD * head, HD * head + HD)
            lanes = slice(128 * head, 128 * head + 128)
            s.pair[head, :HD, :ROWS] = s.q[layer, of_query, rows, :]
            s.pair[head, HD:, ROWS:] = s.mixed[layer, of_query, rows, :]
            both = dot(s.kv[layer, :, lanes], s.pair[head])
            stats = s.stats[layer, of_query]
            probs = jnp.exp(both[:, :ROWS] * SCALE - stats[head : head + 1, :])
            if own:
                probs = jnp.where(allowed_pairs(), probs, 0.0)
            scores = probs * (both[:, ROWS:] - stats[HEADS + head : HEADS + head + 1, :])
            scores = (scores * SCALE).astype(BF16)
            s.terms[:, lanes] += dot(
                jnp.concatenate([scores, probs.astype(BF16)], axis=1), s.pair[head], NT
            )
            back = dot(s.kv_t[layer, 128 * head : 128 * head + HD, :], scores)
            if own:
                s.query[rows, :] = back
            else:
                s.query_out[layer, of_query, rows, :] = back.astype(BF16)

    def backward(layer, between):
        low = s.grad[...].astype(BF16)
        own_mixed = dot(s.wo[layer], low, NT).astype(BF16)
        s.mixed[layer, group] = own_mixed
        s.stats[layer, group] = jnp.zeros((8, ROWS), F32)
        for head in range(HEADS):
            rows = slice(HD * head, HD * head + HD)
            delta = own_mixed[rows, :].astype(F32) * s.att[layer, rows, :]
            s.stats[layer, group, head : head + 1, :] = s.lse[layer, head : head + 1, :]
            s.stats[layer, group, HEADS + head : HEADS + head + 1, :] = jnp.sum(
                delta, axis=0, keepdims=True
            )

        @pl.loop(0, group)
        def _(target):
            for copy in mixed_copies(layer, group, target):
                copy.start()

        small = s.small.at[0]
        first = 8 * layer
        s.terms[...] = jnp.zeros_like(s.terms)
        small[first + 4 : first + 5, :] = jnp.sum(s.grad[...], axis=0, keepdims=True)
        hat, _ = centre(s.resid[layer])
        gain_one, gain_two = vector(g1_ref, layer), vector(g2_ref, layer)
        hidden_grad = dot(low, s.wd[layer], NT)
        pre = s.pre[layer]
        slope = 0.5 * (1.0 + lax.erf(pre * math.sqrt(0.5))) + pre * jnp.exp(
            -0.5 * pre * pre
        ) * (1.0 / math.sqrt(2.0 * math.pi))
        pre_grad = (hidden_grad * slope).astype(BF16)
        small[first + 6 : first + 7, :] = jnp.sum(pre_grad.astype(F32), axis=0, keepdims=True)
        normed_two = (hat * gain_two + vector(s2_ref, layer)).astype(BF16)
        s.ff[layer, :D, :] = dot(normed_two, pre_grad, TN).astype(BF16)
        s.ff[layer, D:, :] = dot(s.hid[layer], low, TN).astype(BF16)
        between(0)
        grad_two = dot(pre_grad, s.wu[layer], NT)
        small[first + 2 : first + 3, :] = jnp.sum(grad_two * hat, axis=0, keepdims=True)
        small[first + 3 : first + 4, :] = jnp.sum(grad_two, axis=0, keepdims=True)
        s.norm_part[...] = grad_two * gain_two

        @pl.loop(group + 1, GROUPS)
        def _(of_query):
            for copy in mixed_copies(layer, of_query, of_query):
                copy.wait_recv()
            attend_back(layer, of_query, False)
            query_copy(layer, of_query, group, of_query).start()

        attend_back(layer, group, True)
        s.low_terms[layer] = s.terms[...].astype(BF16)
        for step in range(1, RING):
            term_copy(layer, step).start()
        s.at[layer, QKV:, :] = dot(s.att[layer].astype(BF16), s.grad[...].astype(BF16)).astype(BF16)
        between(1)

        keys_values = s.terms[ring_part(0), :]
        for step in range(1, RING):
            term_copy(layer, step).wait_recv()
            keys_values = keys_values + s.term_slots[layer, step - 1].astype(F32)

        @pl.loop(0, group)
        def _(source):
            query_copy(layer, source, source, source).wait_recv()
            s.query[...] += s.query_in[layer, source].astype(F32)

        across = keys_values.T
        keys = jnp.concatenate(
            [across[128 * head : 128 * head + HD, :] for head in range(HEADS)], axis=0
        )
        s.merged_t[:WIDE, :] = rotated(s.query[...], rot_ref, -1.0).astype(BF16)
        s.merged_t[WIDE : 2 * WIDE, :] = rotated(keys, rot_ref, -1.0).astype(BF16)
        for head in range(HEADS):
            start = 2 * WIDE + HD * head
            s.merged_t[start : start + HD, :] = across[
                128 * head + HD : 128 * head + 128, :
            ].astype(BF16)
        merged = s.merged_t[...].T
        grad_one = dot(merged, s.wq[layer])
        hat, inverse = centre(s.resid[layer])

        def attention_weights():
            normed_one = (hat * gain_one + vector(s1_ref, layer)).astype(BF16)
            s.at[layer, :QKV, :] = dot(s.merged_t[...], normed_one).astype(BF16)
            between(2)

        if layer == 0:
            attention_weights()
        small[first : first + 1, :] = jnp.sum(grad_one * hat, axis=0, keepdims=True)
        small[first + 1 : first + 2, :] = jnp.sum(grad_one, axis=0, keepdims=True)
        small[first + 5 : first + 6, :] = jnp.zeros((1, D), F32)
        small[first + 5 : first + 6, :QKV] = jnp.sum(merged.astype(F32), axis=0, keepdims=True)
        small[first + 7 : first + 8, :] = jnp.zeros((1, D), F32)
        total = tp_sum(s.norm_part[...] + grad_one * gain_one, my_tp, LAYERS + layer, s)
        along = jnp.mean(total * hat, axis=-1, keepdims=True)
        level = jnp.mean(total, axis=-1, keepdims=True)
        grad = s.grad[...] + inverse * (total - level - hat * along)
        if layer > 0:
            s.grad[...] = grad
            attention_weights()
        else:
            in_grad_ref[...] = grad

    x, y = lax.rem(me // 4, 2), me // 8
    opposite = me + 4 - 8 * x
    z_axis = Axis(z, lambda place: me - z + place)
    y_axis = Axis(y, lambda place: me + (place - y) * 8)
    flows = {}
    per = len(flow_buffers(FF_ROWS))
    for layer in range(LAYERS):
        for kind, src, out in (("ff", s.ff, ff_out), ("at", s.at, at_out)):
            made = []
            for half in range(2):
                axes = (z_axis, y_axis) if half == 0 else (y_axis, z_axis)
                mine, flow_refs = flow_refs[:per], flow_refs[per:]
                made.append(Flow(axes, opposite, src.at[layer], out.at[layer], half, mine))
            flows[kind, layer] = made

    def advance(*which):
        for key in which:
            for one in flows[key]:
                one.advance()

    def between_last(point):
        if point == 0:
            advance(("ff", 1))
        elif point == 1:
            advance(("ff", 1))
        else:
            advance(("ff", 1), ("at", 1))

    def between_first(point):
        if point == 0:
            advance(("ff", 1), ("at", 1), ("ff", 0))
        elif point == 1:
            advance(("ff", 1), ("at", 1), ("ff", 0))
        else:
            advance(("at", 0), ("ff", 1), ("at", 1), ("ff", 0))

    s.resid[0] = x_ref[...].astype(F32)
    s.pair[...] = jnp.zeros_like(s.pair)
    for layer in range(LAYERS):
        forward(layer)
    s.grad[...] = out_grad_ref[...].astype(F32)
    backward(1, between_last)
    backward(0, between_first)

    z_peers = [z_axis.of_place(z_axis.at(step)) for step in (1, 2, 3)]
    y_peers = [y_axis.of_place(y_axis.at(step)) for step in (1, 2, 3)]
    stage_peers = (z_peers, y_peers, [opposite], tp_peers)
    places = (z, y, x, my_tp)

    def small_copies(stage):
        return [
            remote(
                s.small.at[stage],
                s.small_slots.at[stage, places[stage]],
                s.small_send.at[stage, step],
                s.small_recv.at[stage, step],
                **({"tp": peer} if stage == 3 else {"ctx": peer}),
            )
            for step, peer in enumerate(stage_peers[stage])
        ]

    def small_total(stage):
        for copy in small_copies(stage):
            copy.wait_recv()
        s.small_slots[stage, places[stage]] = s.small[stage]
        total = s.small_slots[stage, 0]
        for place in range(1, 2 if stage == 2 else 4):
            total = total + s.small_slots[stage, place]
        return total

    def small_step(number):
        if 0 < number < 4:
            s.small[number] = small_total(number - 1)
        if number < 4:
            for copy in small_copies(number):
                copy.start()
        elif number == 4:
            total, part = small_total(3), s.small[3]
            for row, ref in enumerate((g1_out, s1_out, g2_out, s2_out)):
                for layer in range(LAYERS):
                    ref[layer : layer + 1, :] = total[8 * layer + row : 8 * layer + row + 1, :]
            for layer in range(LAYERS):
                bias_out[layer : layer + 1, :] = part[8 * layer + 4 : 8 * layer + 5, :]
                bup_out[layer : layer + 1, :] = part[8 * layer + 6 : 8 * layer + 7, :]
                for slot in range(3):
                    bqkv_out[slot, layer : layer + 1, :] = part[
                        8 * layer + 5 : 8 * layer + 6, WIDE * slot : WIDE * slot + WIDE
                    ]

    order = (("ff", 1), ("at", 1), ("ff", 0), ("at", 0))
    for number in range(STEPS):
        small_step(number)
        advance(*order)

    for layer in range(LAYERS):
        for step in range(1, RING):
            kv_copy(layer, step, 0).wait_send()
            term_copy(layer, step).wait_send()

        @pl.loop(0, group)
        def _(target):
            q_copy(layer, target, group).wait_send()
            for copy in mixed_copies(layer, group, target):
                copy.wait_send()

        @pl.loop(group + 1, GROUPS)
        def _(of_query):
            query_copy(layer, of_query, group, of_query).wait_send()
            for copy in part_copies(layer, of_query, group, of_query):
                copy.wait_send()

    for key in order:
        for one in flows[key]:
            one.drain()
    for stage in range(4):
        for copy in small_copies(stage):
            copy.wait_send()


def vmem(count):
    return [pl.BlockSpec(memory_space=pltpu.VMEM)] * count


def hbm(count):
    return [pl.BlockSpec(memory_space=pl.ANY)] * count


def whole_step(*arrays):
    pair = jax.ShapeDtypeStruct((LAYERS, D), F32)
    buffers = []
    for _ in range(LAYERS):
        for rows in (FF_ROWS, AT_ROWS):
            buffers += flow_buffers(rows) * 2
    return pl.pallas_call(
        step_kernel,
        name="training_step",
        out_shape=[
            jax.ShapeDtypeStruct((ROWS, D), BF16),
            jax.ShapeDtypeStruct((ROWS, D), F32),
            jax.ShapeDtypeStruct((LAYERS, FF_ROWS, D), BF16),
            jax.ShapeDtypeStruct((LAYERS, AT_ROWS, D), BF16),
            pair,
            pair,
            pair,
            pair,
            pair,
            jax.ShapeDtypeStruct((3, LAYERS, WIDE), F32),
            pair,
        ],
        in_specs=vmem(11) + hbm(4),
        out_specs=vmem(11),
        scratch_shapes=[*scratch().values(), *buffers],
        compiler_params=pltpu.CompilerParams(
            collective_id=0, has_side_effects=True, vmem_limit_bytes=60 << 20
        ),
    )(*arrays)


def on_device(
    layer_input,
    attention_gain,
    attention_shift,
    feedforward_gain,
    feedforward_shift,
    query_key_value_weight,
    query_key_value_bias,
    attention_out_weight,
    dense_bias,
    expand_weight,
    expand_bias,
    down_weight,
    down_bias,
    output_grad,
):
    me = lax.axis_index("ctx")
    positions = (me * ROWS + jnp.arange(ROWS, dtype=jnp.int32)).astype(F32)
    inverse = jnp.power(10000.0, -2.0 * jnp.arange(ROT // 2, dtype=F32) / ROT)
    angles = inverse[:, None] * positions[None, :]
    rot = jnp.stack([jnp.cos(angles), jnp.sin(angles)])
    output, grad, ff, at, g1, s1, g2, s2, bias, bqkv, bup = whole_step(
        layer_input[0],
        output_grad[0],
        attention_gain,
        attention_shift,
        feedforward_gain,
        feedforward_shift,
        query_key_value_bias.transpose(1, 0, 2),
        dense_bias,
        expand_bias,
        down_bias,
        rot,
        query_key_value_weight.transpose(0, 2, 3, 1).reshape(LAYERS, QKV, D),
        attention_out_weight,
        expand_weight,
        down_weight,
    )
    return (
        output[None],
        grad[None],
        g1,
        s1,
        g2,
        s2,
        at[:, :QKV].astype(F32).reshape(LAYERS, 3, WIDE, D).transpose(0, 3, 1, 2),
        bqkv.transpose(1, 0, 2),
        at[:, QKV:].astype(F32),
        bias,
        ff[:, :D].astype(F32),
        bup,
        ff[:, D:].astype(F32),
        bias,
    )


def solution(mesh):
    in_specs = (
        P(None, "ctx", None),
        P(),
        P(),
        P(),
        P(),
        P(None, None, None, "tp"),
        P(None, None, "tp"),
        P(None, "tp", None),
        P(),
        P(None, None, "tp"),
        P(None, "tp"),
        P(None, "tp", None),
        P(),
        P(None, "ctx", None),
    )
    out_specs = (
        P(None, "ctx", None),
        P(None, "ctx", None),
        P(),
        P(),
        P(),
        P(),
        P(None, None, None, "tp"),
        P(None, None, "tp"),
        P(None, "tp", None),
        P(),
        P(None, None, "tp"),
        P(None, "tp"),
        P(None, "tp", None),
        P(),
    )
    return jax.shard_map(
        on_device, mesh=mesh, in_specs=in_specs, out_specs=out_specs, check_vma=False
    )
```

```python
import functools
import math

import jax
import jax.numpy as jnp
from jax import lax
from jax.experimental import pallas as pl
from jax.experimental.pallas import tpu as pltpu
from jax.sharding import PartitionSpec as P

HD = 64
ROT = 16
LAYERS = 2
NORM_EPSILON = 1e-05
MASKED = -1e30
F32 = jnp.float32
BF16 = jnp.bfloat16
ROWS = 128
D = 768
HEADS = 3
CTX = 32
TP = 4
RING = 4
GROUPS = CTX // RING
KEYS = RING * ROWS
WIDE = HEADS * HD
QUARTER = ROWS // TP
SCALE = HD**-0.5
QKV = 3 * WIDE
HALF = D // 2
FF_ROWS, AT_ROWS = 2 * D, QKV + WIDE
PHASES = 2 * LAYERS

NN = (((1,), (0,)), ((), ()))
NT = (((1,), (1,)), ((), ()))
TN = (((0,), (0,)), ((), ()))


def dot(a, b, dims=NN):
    return lax.dot_general(a, b, dims, preferred_element_type=F32)


def remote(src, dst, send, recv, ctx=None, tp=None):
    where = {}
    if ctx is not None:
        where["ctx"] = ctx
    if tp is not None:
        where["tp"] = tp
    return pltpu.make_async_remote_copy(
        src_ref=src,
        dst_ref=dst,
        send_sem=send,
        recv_sem=recv,
        device_id=where,
        device_id_type=pl.DeviceIdType.MESH,
    )


def greet(ctx_peers, tp_peers):
    barrier = pltpu.get_barrier_semaphore()
    for peer in ctx_peers:
        pl.semaphore_signal(
            barrier, inc=1, device_id={"ctx": peer}, device_id_type=pl.DeviceIdType.MESH
        )
    for peer in tp_peers:
        pl.semaphore_signal(
            barrier, inc=1, device_id={"tp": peer}, device_id_type=pl.DeviceIdType.MESH
        )
    return barrier, len(ctx_peers) + len(tp_peers)


def centre(residual):
    mean_value = jnp.mean(residual, axis=-1, keepdims=True)
    centred = residual - mean_value
    variance = jnp.mean(centred * centred, axis=-1, keepdims=True)
    inverse = lax.rsqrt(variance + NORM_EPSILON)
    return centred * inverse, inverse


def tp_sum(part, my_tp, phase, s, between=lambda point: None):
    s.tp_mine[...] = part
    s.tp_out[...] = part.astype(BF16)
    slots, gathered = s.tp_slots.at[phase], s.tp_gathered.at[phase]
    send, recv = s.tp_send.at[phase], s.tp_recv.at[phase]

    def quarter(place):
        return pl.ds(pl.multiple_of(place * QUARTER, QUARTER), QUARTER)

    def spread(step):
        peer = lax.rem(my_tp + step, TP)
        return remote(
            s.tp_out.at[quarter(peer)], slots.at[step - 1], send.at[step - 1], recv.at[step - 1], tp=peer
        )

    def collect(step, place):
        return remote(
            gathered.at[quarter(place)],
            gathered.at[quarter(place)],
            send.at[TP - 2 + step],
            recv.at[TP - 2 + step],
            tp=lax.rem(my_tp + step, TP),
        )

    for step in range(1, TP):
        spread(step).start()
    between(6)
    total = s.tp_mine[quarter(my_tp), :]
    for step in range(1, TP):
        spread(step).wait_recv()
        total = total + slots[step - 1].astype(F32)
    gathered[quarter(my_tp), :] = total.astype(BF16)
    for step in range(1, TP):
        collect(step, my_tp).start()
    between(7)
    for step in range(1, TP):
        collect(step, lax.rem(my_tp + TP - step, TP)).wait_recv()
    for step in range(1, TP):
        spread(step).wait_send()
        collect(step, my_tp).wait_send()
    return gathered[...].astype(F32)


RS_MESSAGES, AG_MESSAGES = 6, 6
FLOW_SEMS = 2 * RS_MESSAGES + 1 + 2 * AG_MESSAGES


def rows_at(start, count):
    return pl.ds(pl.multiple_of(start, 16), count)


class Axis:
    def __init__(self, place, of_place):
        self.place = place
        self.of_place = of_place
        self.right = of_place(lax.rem(place + 1, RING))
        self.left = of_place(lax.rem(place + 3, RING))

    def at(self, step):
        return lax.rem(self.place + step + RING, RING)


class ReduceScatter:
    def __init__(self, axis, src, size, cut, first, second, from_left, from_right, sems):
        self.axis, self.src, self.size, self.cut = axis, src, size, cut
        self.first, self.second = first, second
        self.from_left, self.from_right = from_left, from_right
        self.send, self.recv, self.base = sems

    def copy(self, index, src, dst, ctx):
        return remote(
            src, dst, self.send.at[self.base + index], self.recv.at[self.base + index], ctx=ctx
        )

    def copies(self):
        axis, size, cut = self.axis, self.size, self.cut
        rest = size - cut
        far, near_right, near_left = axis.at(2) * size, axis.at(1) * size, axis.at(3) * size
        return [
            self.copy(0, self.src(far, cut), self.first[0].at[pl.ds(0, cut)], axis.right),
            self.copy(1, self.src(far + cut, rest), self.second[0].at[pl.ds(0, rest)], axis.left),
            self.copy(
                2, self.src(near_right + cut, rest), self.from_left.at[pl.ds(cut, rest)], axis.right
            ),
            self.copy(3, self.src(near_left, cut), self.from_right.at[pl.ds(0, cut)], axis.left),
            self.copy(
                4, self.first[1].at[pl.ds(0, cut)], self.from_left.at[pl.ds(0, cut)], axis.right
            ),
            self.copy(
                5, self.second[1].at[pl.ds(0, rest)], self.from_right.at[pl.ds(cut, rest)], axis.left
            ),
        ]

    def start(self):
        for copy in self.copies()[:4]:
            copy.start()

    def middle(self):
        axis, size, cut = self.axis, self.size, self.cut
        rest = size - cut
        copies = self.copies()
        copies[0].wait_recv()
        self.first[1][0:cut, :] = (
            self.first[0][0:cut, :].astype(F32) + self.src(axis.at(1) * size, cut)[...].astype(F32)
        ).astype(BF16)
        copies[4].start()
        copies[1].wait_recv()
        self.second[1][0:rest, :] = (
            self.second[0][0:rest, :].astype(F32)
            + self.src(axis.at(3) * size + cut, rest)[...].astype(F32)
        ).astype(BF16)
        copies[5].start()

    def finish(self, out):
        for copy in self.copies()[2:]:
            copy.wait_recv()
        size = self.size
        out[0:size, :] = (
            self.src(self.axis.place * size, size)[...].astype(F32)
            + self.from_left[0:size, :].astype(F32)
            + self.from_right[0:size, :].astype(F32)
        ).astype(BF16)

    def drain(self):
        for copy in self.copies():
            copy.wait_send()


class AllGather:
    def __init__(self, axis, view, size, cut, sems):
        self.axis, self.view, self.size, self.cut = axis, view, size, cut
        self.send, self.recv, self.base = sems

    def copy(self, index, start, count, ctx):
        part = self.view(start, count)
        return remote(
            part, part, self.send.at[self.base + index], self.recv.at[self.base + index], ctx=ctx
        )

    def copies(self, shift):
        axis, size, cut = self.axis, self.size, self.cut
        rest = size - cut
        if shift == 0:
            own, from_left, from_right = axis.place * size, axis.at(3) * size, axis.at(1) * size
            return [
                self.copy(0, own, cut, axis.right),
                self.copy(1, own + cut, rest, axis.left),
                self.copy(2, own + cut, rest, axis.right),
                self.copy(3, own, cut, axis.left),
                self.copy(4, from_left, cut, axis.right),
                self.copy(5, from_right + cut, rest, axis.left),
            ]
        from_left, from_right, far = axis.at(3) * size, axis.at(1) * size, axis.at(2) * size
        return [
            self.copy(0, from_left, cut, axis.right),
            self.copy(1, from_right + cut, rest, axis.left),
            self.copy(2, from_left + cut, rest, axis.right),
            self.copy(3, from_right, cut, axis.left),
            self.copy(4, far, cut, axis.right),
            self.copy(5, far + cut, rest, axis.left),
        ]

    def start(self):
        for copy in self.copies(0)[:4]:
            copy.start()

    def middle(self):
        come, go = self.copies(1), self.copies(0)
        come[0].wait_recv()
        go[4].start()
        come[1].wait_recv()
        go[5].start()

    def finish(self):
        for copy in self.copies(1)[2:]:
            copy.wait_recv()

    def drain(self):
        for copy in self.copies(0):
            copy.wait_send()


STEPS = 10


def cuts(rows):
    big, sub = rows // RING, rows // RING // RING
    return big // 32 * 16, sub // 32 * 16


def flow_buffers(rows):
    big, sub = rows // RING, rows // RING // RING
    big_cut, sub_cut = cuts(rows)
    counts = [big_cut, big - big_cut, big, big]
    counts += [sub_cut, sub - sub_cut, sub, sub, sub]
    return [pltpu.VMEM((count, HALF), BF16) for count in counts] + dma_sems(FLOW_SEMS, FLOW_SEMS)


class Flow:
    def __init__(self, axes, across, src_ref, out_ref, half, scratch):
        self.at = 0
        rows = src_ref.shape[0]
        big, sub = rows // RING, rows // RING // RING
        big_cut, sub_cut = cuts(rows)
        one, two = axes
        a, b, left, right, c, d, left2, right2, self.other = scratch[:9]
        self.big, self.sub = left, left2
        self.send, self.recv = scratch[9:]
        lanes = pl.ds(half * HALF, HALF)

        def src(start, count):
            return src_ref.at[rows_at(start, count), lanes]

        def middle_src(start, count):
            return self.big.at[rows_at(start, count)]

        def out(start, count):
            return out_ref.at[rows_at(start, count), lanes]

        corner = one.place * big

        def out_sub(start, count):
            return out_ref.at[rows_at(corner + start, count), lanes]

        self.out_piece = out_sub(two.place * sub, sub)
        self.across = across

        def sems(base):
            return (self.send, self.recv, base)

        self.one = ReduceScatter(one, src, big, big_cut, (a, a), (b, b), left, right, sems(0))
        self.two = ReduceScatter(
            two, middle_src, sub, sub_cut, (c, c), (d, d), left2, right2, sems(6)
        )
        self.three = AllGather(two, out_sub, sub, sub_cut, sems(13))
        self.four = AllGather(one, out, big, big_cut, sems(19))

    def swap(self):
        return remote(self.sub, self.other, self.send.at[12], self.recv.at[12], ctx=self.across)

    def advance(self):
        if self.at < STEPS:
            self.step(self.at)
            self.at += 1

    def step(self, number):
        if number == 0:
            self.one.start()
        elif number == 1:
            self.one.middle()
        elif number == 2:
            self.one.finish(self.big)
            self.two.start()
        elif number == 3:
            self.two.middle()
        elif number == 4:
            self.two.finish(self.sub)
            self.swap().start()
        elif number == 5:
            self.swap().wait_recv()
            self.out_piece[...] = (
                self.sub[...].astype(F32) + self.other[...].astype(F32)
            ).astype(BF16)
            self.three.start()
        elif number == 6:
            self.three.middle()
        elif number == 7:
            self.three.finish()
            self.four.start()
        elif number == 8:
            self.four.middle()
        elif number == 9:
            self.four.finish()

    def drain(self):
        self.one.drain()
        self.two.drain()
        self.swap().wait_send()
        self.three.drain()
        self.four.drain()


def dma_sems(*counts):
    return [
        pltpu.SemaphoreType.DMA(count if isinstance(count, tuple) else (count,)) for count in counts
    ]


def scratch():
    sems = dma_sems
    named = dict(
        wq=pltpu.VMEM((LAYERS, QKV, D), BF16),
        wo=pltpu.VMEM((LAYERS, WIDE, D), BF16),
        wu=pltpu.VMEM((LAYERS, D, D), BF16),
        wd=pltpu.VMEM((LAYERS, D, D), BF16),
        resid=pltpu.VMEM((LAYERS, ROWS, D), F32),
        branch=pltpu.VMEM((ROWS, D), F32),
        grad=pltpu.VMEM((ROWS, D), F32),
        pre=pltpu.VMEM((LAYERS, ROWS, D), F32),
        hid=pltpu.VMEM((LAYERS, ROWS, D), BF16),
        kv_t=pltpu.VMEM((LAYERS, 2 * WIDE, KEYS), BF16),
        kv=pltpu.VMEM((LAYERS, KEYS, 2 * WIDE), BF16),
        q=pltpu.VMEM((LAYERS, GROUPS, WIDE, ROWS), BF16),
        att=pltpu.VMEM((LAYERS, WIDE, ROWS), F32),
        lse=pltpu.VMEM((LAYERS, 8, ROWS), F32),
        part_out=pltpu.VMEM((LAYERS, GROUPS, WIDE, ROWS), BF16),
        part_in=pltpu.VMEM((LAYERS, GROUPS, WIDE, ROWS), BF16),
        lse_out=pltpu.VMEM((LAYERS, GROUPS, 8, ROWS), F32),
        lse_in=pltpu.VMEM((LAYERS, GROUPS, 8, ROWS), F32),
        mixed=pltpu.VMEM((LAYERS, GROUPS, WIDE, ROWS), BF16),
        stats=pltpu.VMEM((LAYERS, GROUPS, 8, ROWS), F32),
        query_out=pltpu.VMEM((LAYERS, GROUPS, WIDE, ROWS), BF16),
        query_in=pltpu.VMEM((LAYERS, GROUPS, WIDE, ROWS), BF16),
        pair=pltpu.VMEM((HEADS, 128, 2 * ROWS), BF16),
        terms=pltpu.VMEM((KEYS, 2 * WIDE), F32),
        low_terms=pltpu.VMEM((LAYERS, KEYS, 2 * WIDE), BF16),
        term_slots=pltpu.VMEM((LAYERS, RING - 1, ROWS, 2 * WIDE), BF16),
        query=pltpu.VMEM((WIDE, ROWS), F32),
        merged_t=pltpu.VMEM((QKV, ROWS), BF16),
        ff=pltpu.VMEM((LAYERS, FF_ROWS, D), BF16),
        at=pltpu.VMEM((LAYERS, AT_ROWS, D), BF16),
        tp_mine=pltpu.VMEM((ROWS, D), F32),
        tp_out=pltpu.VMEM((ROWS, D), BF16),
        tp_slots=pltpu.VMEM((PHASES, TP - 1, QUARTER, D), BF16),
        tp_gathered=pltpu.VMEM((PHASES, ROWS, D), BF16),
        small=pltpu.VMEM((4, 16, D), F32),
        small_slots=pltpu.VMEM((4, 4, 16, D), F32),
    )
    for name, shape in dict(
        load=(LAYERS, 4),
        kv_send=(LAYERS, 3),
        kv_recv=(LAYERS, 3),
        term_send=(LAYERS, 3),
        term_recv=(LAYERS, 3),
        tp_send=(PHASES, 2 * TP - 2),
        tp_recv=(PHASES, 2 * TP - 2),
        small_send=(4, 3),
        small_recv=(4, 3),
    ).items():
        named[name] = sems(shape)[0]
    for name in ("q", "part", "lse", "mixed", "stat", "query"):
        named[name + "_go"] = sems((LAYERS, GROUPS))[0]
        named[name + "_come"] = sems((LAYERS, GROUPS))[0]
    return named


class Names:
    def __init__(self, named):
        self.__dict__.update(named)


def rotated(values, rot_ref, sign):
    cosine, sine = rot_ref[0], rot_ref[1] * sign
    rows = []
    for head in range(HEADS):
        start = HD * head
        one, two = values[start : start + 8, :], values[start + 8 : start + 16, :]
        rows.append(one * cosine - two * sine)
        rows.append(two * cosine + one * sine)
        rows.append(values[start + 16 : start + HD, :])
    return jnp.concatenate(rows, axis=0)


FF1, AT1, FF0, AT0 = ("ff", 1), ("at", 1), ("ff", 0), ("at", 0)
PLAN = {1: {1: (FF1,), 4: (FF1,), 7: (FF1,), 8: (AT1,)}, 0: {0: (FF1,), 1: (AT1, FF0), 4: (FF1, AT1, FF0), 5: (AT0,), 7: (FF1, AT1, FF0)}}


def step_kernel(
    x_ref,
    out_grad_ref,
    g1_ref,
    s1_ref,
    g2_ref,
    s2_ref,
    bqkv_ref,
    dense_bias_ref,
    bup_ref,
    down_bias_ref,
    rot_ref,
    wq_hbm,
    wo_hbm,
    wu_hbm,
    wd_hbm,
    out_ref,
    in_grad_ref,
    ff_out,
    at_out,
    small_out,
    bqkv_out,
    *refs,
):
    names = list(scratch())
    s = Names(zip(names, refs))
    flow_refs = refs[len(names) :]
    me = lax.axis_index("ctx")
    my_tp = lax.axis_index("tp")
    z, group = lax.rem(me, RING), me // RING
    weights = ((wq_hbm, s.wq), (wu_hbm, s.wu), (wd_hbm, s.wd), (wo_hbm, s.wo))

    def load(layer, index):
        src, dst = weights[index]
        return pltpu.make_async_copy(src.at[layer], dst.at[layer], s.load.at[layer, index])

    for layer in range(LAYERS):
        for index in range(4):
            load(layer, index).start()
    ring_peers = [group * RING + lax.rem(z + step, RING) for step in range(1, RING)]
    column_peers = [lax.rem(group + step, GROUPS) * RING + z for step in range(1, GROUPS)]
    tp_peers = [lax.rem(my_tp + step, TP) for step in range(1, TP)]
    barrier, greeted = greet(ring_peers + column_peers, tp_peers)

    def vector(ref, layer):
        return ref[...].astype(F32)[layer : layer + 1, :]

    def ring_part(step):
        place = lax.rem(z + step + RING, RING)
        return pl.ds(pl.multiple_of(place * ROWS, ROWS), ROWS)

    def to_group(src, dst, send, recv, target):
        return remote(src, dst, send, recv, ctx=target * RING + z)

    def allowed_pairs():
        key_pos = lax.broadcasted_iota(jnp.int32, (KEYS, ROWS), 0)
        query_pos = z * ROWS + lax.broadcasted_iota(jnp.int32, (KEYS, ROWS), 1)
        return key_pos <= query_pos

    def kv_copy(layer, step, place):
        lanes = ring_part(place)
        return remote(
            s.kv_t.at[layer, :, lanes],
            s.kv_t.at[layer, :, lanes],
            s.kv_send.at[layer, step - 1],
            s.kv_recv.at[layer, step - 1],
            ctx=group * RING + lax.rem(z + step, RING),
        )

    def q_copy(layer, target, source):
        return to_group(
            s.q.at[layer, source],
            s.q.at[layer, source],
            s.q_go.at[layer, target],
            s.q_come.at[layer, source],
            target,
        )

    def part_copies(layer, here, there, target):
        return (
            to_group(
                s.part_out.at[layer, here],
                s.part_in.at[layer, there],
                s.part_go.at[layer, target],
                s.part_come.at[layer, there],
                target,
            ),
            to_group(
                s.lse_out.at[layer, here],
                s.lse_in.at[layer, there],
                s.lse_go.at[layer, target],
                s.lse_come.at[layer, there],
                target,
            ),
        )

    def mixed_copies(layer, entry, target):
        return (
            to_group(
                s.mixed.at[layer, entry],
                s.mixed.at[layer, entry],
                s.mixed_go.at[layer, target],
                s.mixed_come.at[layer, entry],
                target,
            ),
            to_group(
                s.stats.at[layer, entry],
                s.stats.at[layer, entry],
                s.stat_go.at[layer, target],
                s.stat_come.at[layer, entry],
                target,
            ),
        )

    def query_copy(layer, here, there, target):
        return to_group(
            s.query_out.at[layer, here],
            s.query_in.at[layer, there],
            s.query_go.at[layer, target],
            s.query_come.at[layer, there],
            target,
        )

    def term_copy(layer, step):
        return remote(
            s.low_terms.at[layer, ring_part(step)],
            s.term_slots.at[layer, step - 1],
            s.term_send.at[layer, step - 1],
            s.term_recv.at[layer, step - 1],
            ctx=group * RING + lax.rem(z + step, RING),
        )

    def attend(layer, of_query, own):
        for head in range(HEADS):
            rows = slice(HD * head, HD * head + HD)
            keys = s.kv[layer, :, 128 * head : 128 * head + HD]
            scores = dot(keys, s.q[layer, of_query, rows, :]) * SCALE
            if own:
                scores = jnp.where(allowed_pairs(), scores, MASKED)
            highest = jnp.max(scores, axis=0, keepdims=True)
            weights_of = jnp.exp(scores - highest)
            total = jnp.sum(weights_of, axis=0, keepdims=True)
            values_t = s.kv_t[layer, 128 * head + HD : 128 * head + 128, :]
            attended = dot(values_t, weights_of.astype(BF16)) / total
            log_total = highest + jnp.log(total)
            if own:
                s.att[layer, rows, :] = attended
                s.lse[layer, head : head + 1, :] = log_total
            else:
                s.part_out[layer, of_query, rows, :] = attended.astype(BF16)
                s.lse_out[layer, of_query, head : head + 1, :] = log_total

    def forward(layer):
        hat, _ = centre(s.resid[layer])
        normed = (hat * vector(g1_ref, layer) + vector(s1_ref, layer)).astype(BF16)
        load(layer, 0).wait()
        own = ring_part(0)
        for slot in range(3):
            rows = slice(WIDE * slot, WIDE * slot + WIDE)
            bias = bqkv_ref[slot].astype(F32)[layer : layer + 1, :]
            values = (dot(normed, s.wq[layer, rows, :], NT) + bias).T
            if slot < 2:
                values = rotated(values, rot_ref, 1.0)
            values = values.astype(BF16)
            if slot == 0:
                s.q[layer, group] = values
            else:
                for head in range(HEADS):
                    start = 128 * head + HD * (slot - 1)
                    s.kv_t[layer, start : start + HD, own] = values[HD * head : HD * head + HD, :]
        if layer == 0:
            pl.semaphore_wait(barrier, greeted)
        for step in range(1, RING):
            kv_copy(layer, step, 0).start()

        @pl.loop(0, group)
        def _(target):
            q_copy(layer, target, group).start()

        normed = (hat * vector(g2_ref, layer) + vector(s2_ref, layer)).astype(BF16)
        load(layer, 1).wait()
        pre = dot(normed, s.wu[layer]) + vector(bup_ref, layer)
        s.pre[layer] = pre
        hidden = (pre * (1.0 + lax.erf(pre * math.sqrt(0.5))) * 0.5).astype(BF16)
        s.hid[layer] = hidden
        load(layer, 2).wait()
        s.branch[...] = dot(hidden, s.wd[layer])
        for step in range(1, RING):
            kv_copy(layer, step, -step).wait_recv()
        s.kv[layer] = s.kv_t[layer].T
        s.lse[layer] = jnp.zeros((8, ROWS), F32)

        @pl.loop(group + 1, GROUPS)
        def _(of_query):
            q_copy(layer, of_query, of_query).wait_recv()
            s.lse_out[layer, of_query] = jnp.zeros((8, ROWS), F32)
            attend(layer, of_query, False)
            for copy in part_copies(layer, of_query, group, of_query):
                copy.start()

        attend(layer, group, True)

        @pl.loop(0, group)
        def _(source):
            for copy in part_copies(layer, source, source, source):
                copy.wait_recv()
            old, new = s.lse[layer], s.lse_in[layer, source]
            highest = jnp.maximum(old, new)
            old_part, new_part = jnp.exp(old - highest), jnp.exp(new - highest)
            total = old_part + new_part
            s.lse[layer] = highest + jnp.log(total)
            old_part, new_part = old_part / total, new_part / total
            for head in range(HEADS):
                rows = slice(HD * head, HD * head + HD)
                s.att[layer, rows, :] = s.att[layer, rows, :] * old_part[head : head + 1, :] + (
                    s.part_in[layer, source, rows, :].astype(F32) * new_part[head : head + 1, :]
                )

        load(layer, 3).wait()
        branch = s.branch[...] + dot(s.att[layer].astype(BF16), s.wo[layer], TN)
        branch = tp_sum(branch, my_tp, layer, s)
        bias = vector(dense_bias_ref, layer) + vector(down_bias_ref, layer)
        residual = s.resid[layer] + branch + bias
        if layer + 1 < LAYERS:
            s.resid[layer + 1] = residual
        else:
            out_ref[...] = residual.astype(BF16)

    def attend_back(layer, of_query, own):
        for head in range(HEADS):
            rows = slice(HD * head, HD * head + HD)
            lanes = slice(128 * head, 128 * head + 128)
            s.pair[head, :HD, :ROWS] = s.q[layer, of_query, rows, :]
            s.pair[head, HD:, ROWS:] = s.mixed[layer, of_query, rows, :]
            both = dot(s.kv[layer, :, lanes], s.pair[head])
            stats = s.stats[layer, of_query]
            probs = jnp.exp(both[:, :ROWS] * SCALE - stats[head : head + 1, :])
            if own:
                probs = jnp.where(allowed_pairs(), probs, 0.0)
            scores = probs * (both[:, ROWS:] - stats[HEADS + head : HEADS + head + 1, :])
            scores = (scores * SCALE).astype(BF16)
            s.terms[:, lanes] += dot(
                jnp.concatenate([scores, probs.astype(BF16)], axis=1), s.pair[head], NT
            )
            back = dot(s.kv_t[layer, 128 * head : 128 * head + HD, :], scores)
            if own:
                s.query[rows, :] = back
            else:
                s.query_out[layer, of_query, rows, :] = back.astype(BF16)

    def backward(layer, between):
        low = s.grad[...].astype(BF16)
        own_mixed = dot(s.wo[layer], low, NT).astype(BF16)
        s.mixed[layer, group] = own_mixed
        s.stats[layer, group] = jnp.zeros((8, ROWS), F32)
        for head in range(HEADS):
            rows = slice(HD * head, HD * head + HD)
            delta = own_mixed[rows, :].astype(F32) * s.att[layer, rows, :]
            s.stats[layer, group, head : head + 1, :] = s.lse[layer, head : head + 1, :]
            s.stats[layer, group, HEADS + head : HEADS + head + 1, :] = jnp.sum(
                delta, axis=0, keepdims=True
            )

        @pl.loop(0, group)
        def _(target):
            for copy in mixed_copies(layer, group, target):
                copy.start()

        between(0)
        small = s.small.at[0]
        first = 8 * layer
        s.terms[...] = jnp.zeros_like(s.terms)
        small[first + 4 : first + 5, :] = jnp.sum(s.grad[...], axis=0, keepdims=True)
        hat, _ = centre(s.resid[layer])
        gain_one, gain_two = vector(g1_ref, layer), vector(g2_ref, layer)
        hidden_grad = dot(low, s.wd[layer], NT)
        pre = s.pre[layer]
        slope = 0.5 * (1.0 + lax.erf(pre * math.sqrt(0.5))) + pre * jnp.exp(
            -0.5 * pre * pre
        ) * (1.0 / math.sqrt(2.0 * math.pi))
        pre_grad = (hidden_grad * slope).astype(BF16)
        small[first + 6 : first + 7, :] = jnp.sum(pre_grad.astype(F32), axis=0, keepdims=True)
        normed_two = (hat * gain_two + vector(s2_ref, layer)).astype(BF16)
        s.ff[layer, :D, :] = dot(normed_two, pre_grad, TN).astype(BF16)
        s.ff[layer, D:, :] = dot(s.hid[layer], low, TN).astype(BF16)
        between(1)
        grad_two = dot(pre_grad, s.wu[layer], NT)
        small[first + 2 : first + 3, :] = jnp.sum(grad_two * hat, axis=0, keepdims=True)
        small[first + 3 : first + 4, :] = jnp.sum(grad_two, axis=0, keepdims=True)
        s.branch[...] = grad_two * gain_two
        between(2)

        @pl.loop(group + 1, GROUPS)
        def _(of_query):
            for copy in mixed_copies(layer, of_query, of_query):
                copy.wait_recv()
            attend_back(layer, of_query, False)
            query_copy(layer, of_query, group, of_query).start()

        between(3)
        attend_back(layer, group, True)
        s.low_terms[layer] = s.terms[...].astype(BF16)
        for step in range(1, RING):
            term_copy(layer, step).start()
        s.at[layer, QKV:, :] = dot(s.att[layer].astype(BF16), s.grad[...].astype(BF16)).astype(BF16)
        between(4)

        keys_values = s.terms[ring_part(0), :]
        for step in range(1, RING):
            term_copy(layer, step).wait_recv()
            keys_values = keys_values + s.term_slots[layer, step - 1].astype(F32)

        @pl.loop(0, group)
        def _(source):
            query_copy(layer, source, source, source).wait_recv()
            s.query[...] += s.query_in[layer, source].astype(F32)

        across = keys_values.T
        keys = jnp.concatenate(
            [across[128 * head : 128 * head + HD, :] for head in range(HEADS)], axis=0
        )
        s.merged_t[:WIDE, :] = rotated(s.query[...], rot_ref, -1.0).astype(BF16)
        s.merged_t[WIDE : 2 * WIDE, :] = rotated(keys, rot_ref, -1.0).astype(BF16)
        for head in range(HEADS):
            start = 2 * WIDE + HD * head
            s.merged_t[start : start + HD, :] = across[
                128 * head + HD : 128 * head + 128, :
            ].astype(BF16)
        merged = s.merged_t[...].T
        grad_one = dot(merged, s.wq[layer])
        hat, inverse = centre(s.resid[layer])

        def attention_weights():
            normed_one = (hat * gain_one + vector(s1_ref, layer)).astype(BF16)
            s.at[layer, :QKV, :] = dot(s.merged_t[...], normed_one).astype(BF16)

        if layer == 0:
            attention_weights()
        between(5)
        small[first : first + 1, :] = jnp.sum(grad_one * hat, axis=0, keepdims=True)
        small[first + 1 : first + 2, :] = jnp.sum(grad_one, axis=0, keepdims=True)
        small[first + 5 : first + 6, :] = jnp.zeros((1, D), F32)
        small[first + 5 : first + 6, :QKV] = jnp.sum(merged.astype(F32), axis=0, keepdims=True)
        small[first + 7 : first + 8, :] = jnp.zeros((1, D), F32)
        total = tp_sum(s.branch[...] + grad_one * gain_one, my_tp, LAYERS + layer, s, between)
        along = jnp.mean(total * hat, axis=-1, keepdims=True)
        level = jnp.mean(total, axis=-1, keepdims=True)
        grad = s.grad[...] + inverse * (total - level - hat * along)
        if layer > 0:
            s.grad[...] = grad
            attention_weights()
        else:
            in_grad_ref[...] = grad
        between(8)

    x, y = lax.rem(me // 4, 2), me // 8
    opposite = me + 4 - 8 * x
    z_axis = Axis(z, lambda place: me - z + place)
    y_axis = Axis(y, lambda place: me + (place - y) * 8)
    flows = {}
    per = len(flow_buffers(FF_ROWS))
    for layer in range(LAYERS):
        for kind, src, out in (("ff", s.ff, ff_out), ("at", s.at, at_out)):
            made = []
            for half in range(2):
                axes = (z_axis, y_axis) if half == 0 else (y_axis, z_axis)
                mine, flow_refs = flow_refs[:per], flow_refs[per:]
                made.append(Flow(axes, opposite, src.at[layer], out.at[layer], half, mine))
            flows[kind, layer] = made

    def advance(*which):
        for key in which:
            for one in flows[key]:
                one.advance()

    def between(layer):
        return lambda point: advance(*PLAN[layer].get(point, ()))

    s.resid[0] = x_ref[...].astype(F32)
    s.pair[...] = jnp.zeros_like(s.pair)
    for layer in range(LAYERS):
        forward(layer)
    s.grad[...] = out_grad_ref[...].astype(F32)
    backward(1, between(1))
    backward(0, between(0))

    z_peers = [z_axis.of_place(z_axis.at(step)) for step in (1, 2, 3)]
    y_peers = [y_axis.of_place(y_axis.at(step)) for step in (1, 2, 3)]
    stage_peers = (z_peers, y_peers, [opposite], tp_peers)
    places = (z, y, x, my_tp)

    def small_copies(stage):
        return [
            remote(
                s.small.at[stage],
                s.small_slots.at[stage, places[stage]],
                s.small_send.at[stage, step],
                s.small_recv.at[stage, step],
                **({"tp": peer} if stage == 3 else {"ctx": peer}),
            )
            for step, peer in enumerate(stage_peers[stage])
        ]

    def small_total(stage):
        for copy in small_copies(stage):
            copy.wait_recv()
        s.small_slots[stage, places[stage]] = s.small[stage]
        total = s.small_slots[stage, 0]
        for place in range(1, 2 if stage == 2 else 4):
            total = total + s.small_slots[stage, place]
        return total

    def small_step(number):
        if 0 < number < 4:
            s.small[number] = small_total(number - 1)
        if number < 4:
            for copy in small_copies(number):
                copy.start()
        elif number == 4:
            total, part = small_total(3), s.small[3]
            for layer in range(LAYERS):
                for row in range(4):
                    small_out[row, layer : layer + 1, :] = total[8 * layer + row : 8 * layer + row + 1, :]
                for row in (4, 6):
                    small_out[row, layer : layer + 1, :] = part[8 * layer + row : 8 * layer + row + 1, :]
                for row in (5, 7):
                    small_out[row, layer : layer + 1, :] = jnp.zeros((1, D), F32)
                for slot in range(3):
                    bqkv_out[slot, layer : layer + 1, :] = part[
                        8 * layer + 5 : 8 * layer + 6, WIDE * slot : WIDE * slot + WIDE
                    ]

    order = (AT0, FF0, AT1, FF1)
    for number in range(STEPS):
        small_step(number)
        advance(*order)

    for layer in range(LAYERS):
        for step in range(1, RING):
            kv_copy(layer, step, 0).wait_send()
            term_copy(layer, step).wait_send()

        @pl.loop(0, group)
        def _(target):
            q_copy(layer, target, group).wait_send()
            for copy in mixed_copies(layer, group, target):
                copy.wait_send()

        @pl.loop(group + 1, GROUPS)
        def _(of_query):
            query_copy(layer, of_query, group, of_query).wait_send()
            for copy in part_copies(layer, of_query, group, of_query):
                copy.wait_send()

    for key in order:
        for one in flows[key]:
            one.drain()
    for stage in range(4):
        for copy in small_copies(stage):
            copy.wait_send()


def vmem(count):
    return [pl.BlockSpec(memory_space=pltpu.VMEM)] * count


def hbm(count):
    return [pl.BlockSpec(memory_space=pl.ANY)] * count


def whole_step(*arrays):
    buffers = []
    for _ in range(LAYERS):
        for rows in (FF_ROWS, AT_ROWS):
            buffers += flow_buffers(rows) * 2
    return pl.pallas_call(
        step_kernel,
        name="training_step",
        out_shape=[
            jax.ShapeDtypeStruct((ROWS, D), BF16),
            jax.ShapeDtypeStruct((ROWS, D), F32),
            jax.ShapeDtypeStruct((LAYERS, FF_ROWS, D), BF16),
            jax.ShapeDtypeStruct((LAYERS, AT_ROWS, D), BF16),
            jax.ShapeDtypeStruct((8, LAYERS, D), F32),
            jax.ShapeDtypeStruct((3, LAYERS, WIDE), F32),
        ],
        in_specs=vmem(11) + hbm(4),
        out_specs=vmem(6),
        scratch_shapes=[*scratch().values(), *buffers],
        compiler_params=pltpu.CompilerParams(
            collective_id=0, has_side_effects=True, vmem_limit_bytes=60 << 20
        ),
    )(*arrays)


def on_device(
    layer_input,
    attention_gain,
    attention_shift,
    feedforward_gain,
    feedforward_shift,
    query_key_value_weight,
    query_key_value_bias,
    attention_out_weight,
    dense_bias,
    expand_weight,
    expand_bias,
    down_weight,
    down_bias,
    output_grad,
):
    me = lax.axis_index("ctx")
    positions = (me * ROWS + jnp.arange(ROWS, dtype=jnp.int32)).astype(F32)
    inverse = jnp.power(10000.0, -2.0 * jnp.arange(ROT // 2, dtype=F32) / ROT)
    angles = inverse[:, None] * positions[None, :]
    rot = jnp.stack([jnp.cos(angles), jnp.sin(angles)])
    output, grad, ff, at, small, bqkv = whole_step(
        layer_input[0],
        output_grad[0],
        attention_gain,
        attention_shift,
        feedforward_gain,
        feedforward_shift,
        query_key_value_bias.transpose(1, 0, 2),
        dense_bias,
        expand_bias,
        down_bias,
        rot,
        query_key_value_weight.transpose(0, 2, 3, 1).reshape(LAYERS, QKV, D),
        attention_out_weight,
        expand_weight,
        down_weight,
    )
    return (
        output[None],
        grad[None],
        small[0],
        small[1],
        small[2],
        small[3],
        at[:, :QKV].astype(F32).reshape(LAYERS, 3, WIDE, D).transpose(0, 3, 1, 2),
        bqkv.transpose(1, 0, 2),
        at[:, QKV:].astype(F32),
        small[4],
        ff[:, :D].astype(F32),
        small[6],
        ff[:, D:].astype(F32),
        small[4],
    )


def solution(mesh):
    in_specs = (
        P(None, "ctx", None),
        P(),
        P(),
        P(),
        P(),
        P(None, None, None, "tp"),
        P(None, None, "tp"),
        P(None, "tp", None),
        P(),
        P(None, None, "tp"),
        P(None, "tp"),
        P(None, "tp", None),
        P(),
        P(None, "ctx", None),
    )
    out_specs = (
        P(None, "ctx", None),
        P(None, "ctx", None),
        P(),
        P(),
        P(),
        P(),
        P(None, None, None, "tp"),
        P(None, None, "tp"),
        P(None, "tp", None),
        P(),
        P(None, None, "tp"),
        P(None, "tp"),
        P(None, "tp", None),
        P(),
    )
    return jax.shard_map(
        on_device, mesh=mesh, in_specs=in_specs, out_specs=out_specs, check_vma=False
    )
```

```python
import functools
import math

import jax
import jax.numpy as jnp
from jax import lax
from jax.experimental import pallas as pl
from jax.experimental.pallas import tpu as pltpu
from jax.sharding import PartitionSpec as P

HD = 64
ROT = 16
LAYERS = 2
NORM_EPSILON = 1e-05
MASKED = -1e30
F32 = jnp.float32
BF16 = jnp.bfloat16
ROWS = 128
D = 768
HEADS = 3
CTX = 32
TP = 4
RING = 4
GROUPS = CTX // RING
KEYS = RING * ROWS
WIDE = HEADS * HD
QUARTER = ROWS // TP
SCALE = HD**-0.5
QKV = 3 * WIDE
HALF = D // 2
FF_ROWS, AT_ROWS = 2 * D, QKV + WIDE
PHASES = 2 * LAYERS

NN = (((1,), (0,)), ((), ()))
NT = (((1,), (1,)), ((), ()))
TN = (((0,), (0,)), ((), ()))


def dot(a, b, dims=NN):
    return lax.dot_general(a, b, dims, preferred_element_type=F32)


def remote(src, dst, send, recv, ctx=None, tp=None):
    where = {}
    if ctx is not None:
        where["ctx"] = ctx
    if tp is not None:
        where["tp"] = tp
    return pltpu.make_async_remote_copy(
        src_ref=src,
        dst_ref=dst,
        send_sem=send,
        recv_sem=recv,
        device_id=where,
        device_id_type=pl.DeviceIdType.MESH,
    )


def greet(ctx_peers, tp_peers):
    barrier = pltpu.get_barrier_semaphore()
    for peer in ctx_peers:
        pl.semaphore_signal(
            barrier, inc=1, device_id={"ctx": peer}, device_id_type=pl.DeviceIdType.MESH
        )
    for peer in tp_peers:
        pl.semaphore_signal(
            barrier, inc=1, device_id={"tp": peer}, device_id_type=pl.DeviceIdType.MESH
        )
    return barrier, len(ctx_peers) + len(tp_peers)


def centre(residual):
    mean_value = jnp.mean(residual, axis=-1, keepdims=True)
    centred = residual - mean_value
    variance = jnp.mean(centred * centred, axis=-1, keepdims=True)
    inverse = lax.rsqrt(variance + NORM_EPSILON)
    return centred * inverse, inverse


def tp_sum(part, my_tp, phase, s, between=lambda point: None):
    s.tp_mine[...] = part
    s.tp_out[...] = part.astype(BF16)
    slots, gathered = s.tp_slots.at[phase], s.tp_gathered.at[phase]
    send, recv = s.tp_send.at[phase], s.tp_recv.at[phase]

    def quarter(place):
        return pl.ds(pl.multiple_of(place * QUARTER, QUARTER), QUARTER)

    def spread(step):
        peer = lax.rem(my_tp + step, TP)
        return remote(
            s.tp_out.at[quarter(peer)], slots.at[step - 1], send.at[step - 1], recv.at[step - 1], tp=peer
        )

    def collect(step, place):
        return remote(
            gathered.at[quarter(place)],
            gathered.at[quarter(place)],
            send.at[TP - 2 + step],
            recv.at[TP - 2 + step],
            tp=lax.rem(my_tp + step, TP),
        )

    for step in range(1, TP):
        spread(step).start()
    between(6)
    total = s.tp_mine[quarter(my_tp), :]
    for step in range(1, TP):
        spread(step).wait_recv()
        total = total + slots[step - 1].astype(F32)
    gathered[quarter(my_tp), :] = total.astype(BF16)
    for step in range(1, TP):
        collect(step, my_tp).start()
    between(7)
    for step in range(1, TP):
        collect(step, lax.rem(my_tp + TP - step, TP)).wait_recv()
    for step in range(1, TP):
        spread(step).wait_send()
        collect(step, my_tp).wait_send()
    return gathered[...].astype(F32)


RS_MESSAGES, AG_MESSAGES = 6, 6
FLOW_SEMS = 2 * RS_MESSAGES + 1 + 2 * AG_MESSAGES


def rows_at(start, count):
    return pl.ds(pl.multiple_of(start, 16), count)


class Axis:
    def __init__(self, place, of_place):
        self.place = place
        self.of_place = of_place
        self.right = of_place(lax.rem(place + 1, RING))
        self.left = of_place(lax.rem(place + 3, RING))

    def at(self, step):
        return lax.rem(self.place + step + RING, RING)


class ReduceScatter:
    def __init__(self, axis, src, size, cut, first, second, from_left, from_right, sems):
        self.axis, self.src, self.size, self.cut = axis, src, size, cut
        self.first, self.second = first, second
        self.from_left, self.from_right = from_left, from_right
        self.send, self.recv, self.base = sems

    def copy(self, index, src, dst, ctx):
        return remote(
            src, dst, self.send.at[self.base + index], self.recv.at[self.base + index], ctx=ctx
        )

    def copies(self):
        axis, size, cut = self.axis, self.size, self.cut
        rest = size - cut
        far, near_right, near_left = axis.at(2) * size, axis.at(1) * size, axis.at(3) * size
        return [
            self.copy(0, self.src(far, cut), self.first[0].at[pl.ds(0, cut)], axis.right),
            self.copy(1, self.src(far + cut, rest), self.second[0].at[pl.ds(0, rest)], axis.left),
            self.copy(
                2, self.src(near_right + cut, rest), self.from_left.at[pl.ds(cut, rest)], axis.right
            ),
            self.copy(3, self.src(near_left, cut), self.from_right.at[pl.ds(0, cut)], axis.left),
            self.copy(
                4, self.first[1].at[pl.ds(0, cut)], self.from_left.at[pl.ds(0, cut)], axis.right
            ),
            self.copy(
                5, self.second[1].at[pl.ds(0, rest)], self.from_right.at[pl.ds(cut, rest)], axis.left
            ),
        ]

    def start(self):
        for copy in self.copies()[:4]:
            copy.start()

    def middle(self):
        axis, size, cut = self.axis, self.size, self.cut
        rest = size - cut
        copies = self.copies()
        copies[0].wait_recv()
        self.first[1][0:cut, :] = (
            self.first[0][0:cut, :].astype(F32) + self.src(axis.at(1) * size, cut)[...].astype(F32)
        ).astype(BF16)
        copies[4].start()
        copies[1].wait_recv()
        self.second[1][0:rest, :] = (
            self.second[0][0:rest, :].astype(F32)
            + self.src(axis.at(3) * size + cut, rest)[...].astype(F32)
        ).astype(BF16)
        copies[5].start()

    def finish(self, out):
        for copy in self.copies()[2:]:
            copy.wait_recv()
        size = self.size
        out[0:size, :] = (
            self.src(self.axis.place * size, size)[...].astype(F32)
            + self.from_left[0:size, :].astype(F32)
            + self.from_right[0:size, :].astype(F32)
        ).astype(BF16)

    def drain(self):
        for copy in self.copies():
            copy.wait_send()


class AllGather:
    def __init__(self, axis, view, size, cut, sems):
        self.axis, self.view, self.size, self.cut = axis, view, size, cut
        self.send, self.recv, self.base = sems

    def copy(self, index, start, count, ctx):
        part = self.view(start, count)
        return remote(
            part, part, self.send.at[self.base + index], self.recv.at[self.base + index], ctx=ctx
        )

    def copies(self, shift):
        axis, size, cut = self.axis, self.size, self.cut
        rest = size - cut
        if shift == 0:
            own, from_left, from_right = axis.place * size, axis.at(3) * size, axis.at(1) * size
            return [
                self.copy(0, own, cut, axis.right),
                self.copy(1, own + cut, rest, axis.left),
                self.copy(2, own + cut, rest, axis.right),
                self.copy(3, own, cut, axis.left),
                self.copy(4, from_left, cut, axis.right),
                self.copy(5, from_right + cut, rest, axis.left),
            ]
        from_left, from_right, far = axis.at(3) * size, axis.at(1) * size, axis.at(2) * size
        return [
            self.copy(0, from_left, cut, axis.right),
            self.copy(1, from_right + cut, rest, axis.left),
            self.copy(2, from_left + cut, rest, axis.right),
            self.copy(3, from_right, cut, axis.left),
            self.copy(4, far, cut, axis.right),
            self.copy(5, far + cut, rest, axis.left),
        ]

    def start(self):
        for copy in self.copies(0)[:4]:
            copy.start()

    def middle(self):
        come, go = self.copies(1), self.copies(0)
        come[0].wait_recv()
        go[4].start()
        come[1].wait_recv()
        go[5].start()

    def finish(self):
        for copy in self.copies(1)[2:]:
            copy.wait_recv()

    def drain(self):
        for copy in self.copies(0):
            copy.wait_send()


STEPS = 10


def cuts(rows):
    big, sub = rows // RING, rows // RING // RING
    return big // 32 * 16, sub // 32 * 16


def flow_buffers(rows):
    big, sub = rows // RING, rows // RING // RING
    big_cut, sub_cut = cuts(rows)
    counts = [big_cut, big - big_cut, big, big]
    counts += [sub_cut, sub - sub_cut, sub, sub, sub]
    return [pltpu.VMEM((count, HALF), BF16) for count in counts] + dma_sems(FLOW_SEMS, FLOW_SEMS)


class Flow:
    def __init__(self, axes, across, src_ref, out_ref, half, scratch):
        self.at = 0
        rows = src_ref.shape[0]
        big, sub = rows // RING, rows // RING // RING
        big_cut, sub_cut = cuts(rows)
        one, two = axes
        a, b, left, right, c, d, left2, right2, self.other = scratch[:9]
        self.big, self.sub = left, left2
        self.send, self.recv = scratch[9:]
        lanes = pl.ds(half * HALF, HALF)

        def src(start, count):
            return src_ref.at[rows_at(start, count), lanes]

        def middle_src(start, count):
            return self.big.at[rows_at(start, count)]

        def out(start, count):
            return out_ref.at[rows_at(start, count), lanes]

        corner = one.place * big

        def out_sub(start, count):
            return out_ref.at[rows_at(corner + start, count), lanes]

        self.out_piece = out_sub(two.place * sub, sub)
        self.across = across

        def sems(base):
            return (self.send, self.recv, base)

        self.one = ReduceScatter(one, src, big, big_cut, (a, a), (b, b), left, right, sems(0))
        self.two = ReduceScatter(
            two, middle_src, sub, sub_cut, (c, c), (d, d), left2, right2, sems(6)
        )
        self.three = AllGather(two, out_sub, sub, sub_cut, sems(13))
        self.four = AllGather(one, out, big, big_cut, sems(19))

    def swap(self):
        return remote(self.sub, self.other, self.send.at[12], self.recv.at[12], ctx=self.across)

    def advance(self):
        if self.at < STEPS:
            self.step(self.at)
            self.at += 1

    def step(self, number):
        if number == 0:
            self.one.start()
        elif number == 1:
            self.one.middle()
        elif number == 2:
            self.one.finish(self.big)
            self.two.start()
        elif number == 3:
            self.two.middle()
        elif number == 4:
            self.two.finish(self.sub)
            self.swap().start()
        elif number == 5:
            self.swap().wait_recv()
            self.out_piece[...] = (
                self.sub[...].astype(F32) + self.other[...].astype(F32)
            ).astype(BF16)
            self.three.start()
        elif number == 6:
            self.three.middle()
        elif number == 7:
            self.three.finish()
            self.four.start()
        elif number == 8:
            self.four.middle()
        elif number == 9:
            self.four.finish()

    def drain(self):
        self.one.drain()
        self.two.drain()
        self.swap().wait_send()
        self.three.drain()
        self.four.drain()


def dma_sems(*counts):
    return [
        pltpu.SemaphoreType.DMA(count if isinstance(count, tuple) else (count,)) for count in counts
    ]


def scratch():
    sems = dma_sems
    named = dict(
        wq=pltpu.VMEM((LAYERS, QKV, D), BF16),
        wo=pltpu.VMEM((LAYERS, WIDE, D), BF16),
        wu=pltpu.VMEM((LAYERS, D, D), BF16),
        wd=pltpu.VMEM((LAYERS, D, D), BF16),
        resid=pltpu.VMEM((LAYERS, ROWS, D), F32),
        branch=pltpu.VMEM((ROWS, D), F32),
        grad=pltpu.VMEM((ROWS, D), F32),
        pre=pltpu.VMEM((LAYERS, ROWS, D), F32),
        hid=pltpu.VMEM((LAYERS, ROWS, D), BF16),
        kv_t=pltpu.VMEM((LAYERS, 2 * WIDE, KEYS), BF16),
        kv=pltpu.VMEM((LAYERS, KEYS, 2 * WIDE), BF16),
        q=pltpu.VMEM((LAYERS, GROUPS, WIDE, ROWS), BF16),
        att=pltpu.VMEM((LAYERS, WIDE, ROWS), F32),
        lse=pltpu.VMEM((LAYERS, 8, ROWS), F32),
        part_out=pltpu.VMEM((LAYERS, GROUPS, WIDE, ROWS), BF16),
        part_in=pltpu.VMEM((LAYERS, GROUPS, WIDE, ROWS), BF16),
        lse_out=pltpu.VMEM((LAYERS, GROUPS, 8, ROWS), F32),
        lse_in=pltpu.VMEM((LAYERS, GROUPS, 8, ROWS), F32),
        mixed=pltpu.VMEM((LAYERS, GROUPS, WIDE, ROWS), BF16),
        stats=pltpu.VMEM((LAYERS, GROUPS, 8, ROWS), F32),
        query_out=pltpu.VMEM((LAYERS, GROUPS, WIDE, ROWS), BF16),
        query_in=pltpu.VMEM((LAYERS, GROUPS, WIDE, ROWS), BF16),
        pair=pltpu.VMEM((HEADS, 128, 2 * ROWS), BF16),
        terms=pltpu.VMEM((KEYS, 2 * WIDE), F32),
        low_terms=pltpu.VMEM((LAYERS, KEYS, 2 * WIDE), BF16),
        term_slots=pltpu.VMEM((LAYERS, RING - 1, ROWS, 2 * WIDE), BF16),
        query=pltpu.VMEM((WIDE, ROWS), F32),
        merged_t=pltpu.VMEM((QKV, ROWS), BF16),
        ff=pltpu.VMEM((LAYERS, FF_ROWS, D), BF16),
        at=pltpu.VMEM((LAYERS, AT_ROWS, D), BF16),
        tp_mine=pltpu.VMEM((ROWS, D), F32),
        tp_out=pltpu.VMEM((ROWS, D), BF16),
        tp_slots=pltpu.VMEM((PHASES, TP - 1, QUARTER, D), BF16),
        tp_gathered=pltpu.VMEM((PHASES, ROWS, D), BF16),
        small=pltpu.VMEM((4, 16, D), F32),
        small_slots=pltpu.VMEM((4, 4, 16, D), F32),
    )
    for name, shape in dict(
        load=(LAYERS, 4),
        kv_send=(LAYERS, 3),
        kv_recv=(LAYERS, 3),
        term_send=(LAYERS, 3),
        term_recv=(LAYERS, 3),
        tp_send=(PHASES, 2 * TP - 2),
        tp_recv=(PHASES, 2 * TP - 2),
        small_send=(4, 3),
        small_recv=(4, 3),
    ).items():
        named[name] = sems(shape)[0]
    for name in ("q", "part", "lse", "mixed", "stat", "query"):
        named[name + "_go"] = sems((LAYERS, GROUPS))[0]
        named[name + "_come"] = sems((LAYERS, GROUPS))[0]
    return named


class Names:
    def __init__(self, named):
        self.__dict__.update(named)


def rotated(values, rot_ref, sign):
    cosine, sine = rot_ref[0], rot_ref[1] * sign
    rows = []
    for head in range(HEADS):
        start = HD * head
        one, two = values[start : start + 8, :], values[start + 8 : start + 16, :]
        rows.append(one * cosine - two * sine)
        rows.append(two * cosine + one * sine)
        rows.append(values[start + 16 : start + HD, :])
    return jnp.concatenate(rows, axis=0)


FF1, AT1, FF0, AT0 = ("ff", 1), ("at", 1), ("ff", 0), ("at", 0)
PLAN = {
    1: {1: (FF1,), 4: (FF1,), 7: (FF1,), 8: (AT1,)},
    0: {0: (FF1,), 1: (AT1, FF0), 4: (FF1, AT1, FF0), 5: (AT0,), 7: (AT0, FF1, AT1, FF0)},
}


def step_kernel(
    x_ref,
    out_grad_ref,
    g1_ref,
    s1_ref,
    g2_ref,
    s2_ref,
    bqkv_ref,
    dense_bias_ref,
    bup_ref,
    down_bias_ref,
    rot_ref,
    wq_hbm,
    wo_hbm,
    wu_hbm,
    wd_hbm,
    out_ref,
    in_grad_ref,
    ff_out,
    at_out,
    small_out,
    bqkv_out,
    *refs,
):
    names = list(scratch())
    s = Names(zip(names, refs))
    flow_refs = refs[len(names) :]
    me = lax.axis_index("ctx")
    my_tp = lax.axis_index("tp")
    z, group = lax.rem(me, RING), me // RING
    weights = ((wq_hbm, s.wq), (wu_hbm, s.wu), (wd_hbm, s.wd), (wo_hbm, s.wo))

    def load(layer, index):
        src, dst = weights[index]
        return pltpu.make_async_copy(src.at[layer], dst.at[layer], s.load.at[layer, index])

    for layer in range(LAYERS):
        for index in range(4):
            load(layer, index).start()
    ring_peers = [group * RING + lax.rem(z + step, RING) for step in range(1, RING)]
    column_peers = [lax.rem(group + step, GROUPS) * RING + z for step in range(1, GROUPS)]
    tp_peers = [lax.rem(my_tp + step, TP) for step in range(1, TP)]
    barrier, greeted = greet(ring_peers + column_peers, tp_peers)

    def vector(ref, layer):
        return ref[...].astype(F32)[layer : layer + 1, :]

    def ring_part(step):
        place = lax.rem(z + step + RING, RING)
        return pl.ds(pl.multiple_of(place * ROWS, ROWS), ROWS)

    def to_group(src, dst, send, recv, target):
        return remote(src, dst, send, recv, ctx=target * RING + z)

    def allowed_pairs():
        key_pos = lax.broadcasted_iota(jnp.int32, (KEYS, ROWS), 0)
        query_pos = z * ROWS + lax.broadcasted_iota(jnp.int32, (KEYS, ROWS), 1)
        return key_pos <= query_pos

    def kv_copy(layer, step, place):
        lanes = ring_part(place)
        return remote(
            s.kv_t.at[layer, :, lanes],
            s.kv_t.at[layer, :, lanes],
            s.kv_send.at[layer, step - 1],
            s.kv_recv.at[layer, step - 1],
            ctx=group * RING + lax.rem(z + step, RING),
        )

    def q_copy(layer, target, source):
        return to_group(
            s.q.at[layer, source],
            s.q.at[layer, source],
            s.q_go.at[layer, target],
            s.q_come.at[layer, source],
            target,
        )

    def part_copies(layer, here, there, target):
        return (
            to_group(
                s.part_out.at[layer, here],
                s.part_in.at[layer, there],
                s.part_go.at[layer, target],
                s.part_come.at[layer, there],
                target,
            ),
            to_group(
                s.lse_out.at[layer, here],
                s.lse_in.at[layer, there],
                s.lse_go.at[layer, target],
                s.lse_come.at[layer, there],
                target,
            ),
        )

    def mixed_copies(layer, entry, target):
        return (
            to_group(
                s.mixed.at[layer, entry],
                s.mixed.at[layer, entry],
                s.mixed_go.at[layer, target],
                s.mixed_come.at[layer, entry],
                target,
            ),
            to_group(
                s.stats.at[layer, entry],
                s.stats.at[layer, entry],
                s.stat_go.at[layer, target],
                s.stat_come.at[layer, entry],
                target,
            ),
        )

    def query_copy(layer, here, there, target):
        return to_group(
            s.query_out.at[layer, here],
            s.query_in.at[layer, there],
            s.query_go.at[layer, target],
            s.query_come.at[layer, there],
            target,
        )

    def term_copy(layer, step):
        return remote(
            s.low_terms.at[layer, ring_part(step)],
            s.term_slots.at[layer, step - 1],
            s.term_send.at[layer, step - 1],
            s.term_recv.at[layer, step - 1],
            ctx=group * RING + lax.rem(z + step, RING),
        )

    def attend(layer, of_query, own):
        for head in range(HEADS):
            rows = slice(HD * head, HD * head + HD)
            keys = s.kv[layer, :, 128 * head : 128 * head + HD]
            scores = dot(keys, s.q[layer, of_query, rows, :]) * SCALE
            if own:
                scores = jnp.where(allowed_pairs(), scores, MASKED)
            highest = jnp.max(scores, axis=0, keepdims=True)
            weights_of = jnp.exp(scores - highest)
            total = jnp.sum(weights_of, axis=0, keepdims=True)
            values_t = s.kv_t[layer, 128 * head + HD : 128 * head + 128, :]
            attended = dot(values_t, weights_of.astype(BF16)) / total
            log_total = highest + jnp.log(total)
            if own:
                s.att[layer, rows, :] = attended
                s.lse[layer, head : head + 1, :] = log_total
            else:
                s.part_out[layer, of_query, rows, :] = attended.astype(BF16)
                s.lse_out[layer, of_query, head : head + 1, :] = log_total

    def forward(layer):
        hat, _ = centre(s.resid[layer])
        normed = (hat * vector(g1_ref, layer) + vector(s1_ref, layer)).astype(BF16)
        load(layer, 0).wait()
        own = ring_part(0)
        for slot in range(3):
            rows = slice(WIDE * slot, WIDE * slot + WIDE)
            bias = bqkv_ref[slot].astype(F32)[layer : layer + 1, :]
            values = (dot(normed, s.wq[layer, rows, :], NT) + bias).T
            if slot < 2:
                values = rotated(values, rot_ref, 1.0)
            values = values.astype(BF16)
            if slot == 0:
                s.q[layer, group] = values
            else:
                for head in range(HEADS):
                    start = 128 * head + HD * (slot - 1)
                    s.kv_t[layer, start : start + HD, own] = values[HD * head : HD * head + HD, :]
        if layer == 0:
            pl.semaphore_wait(barrier, greeted)
        for step in range(1, RING):
            kv_copy(layer, step, 0).start()

        @pl.loop(0, group)
        def _(target):
            q_copy(layer, target, group).start()

        normed = (hat * vector(g2_ref, layer) + vector(s2_ref, layer)).astype(BF16)
        load(layer, 1).wait()
        pre = dot(normed, s.wu[layer]) + vector(bup_ref, layer)
        s.pre[layer] = pre
        hidden = (pre * (1.0 + lax.erf(pre * math.sqrt(0.5))) * 0.5).astype(BF16)
        s.hid[layer] = hidden
        load(layer, 2).wait()
        s.branch[...] = dot(hidden, s.wd[layer])
        for step in range(1, RING):
            kv_copy(layer, step, -step).wait_recv()
        s.kv[layer] = s.kv_t[layer].T
        s.lse[layer] = jnp.zeros((8, ROWS), F32)

        @pl.loop(group + 1, GROUPS)
        def _(of_query):
            q_copy(layer, of_query, of_query).wait_recv()
            s.lse_out[layer, of_query] = jnp.zeros((8, ROWS), F32)
            attend(layer, of_query, False)
            for copy in part_copies(layer, of_query, group, of_query):
                copy.start()

        attend(layer, group, True)

        @pl.loop(0, group)
        def _(source):
            for copy in part_copies(layer, source, source, source):
                copy.wait_recv()
            old, new = s.lse[layer], s.lse_in[layer, source]
            highest = jnp.maximum(old, new)
            old_part, new_part = jnp.exp(old - highest), jnp.exp(new - highest)
            total = old_part + new_part
            s.lse[layer] = highest + jnp.log(total)
            old_part, new_part = old_part / total, new_part / total
            for head in range(HEADS):
                rows = slice(HD * head, HD * head + HD)
                s.att[layer, rows, :] = s.att[layer, rows, :] * old_part[head : head + 1, :] + (
                    s.part_in[layer, source, rows, :].astype(F32) * new_part[head : head + 1, :]
                )

        load(layer, 3).wait()
        branch = s.branch[...] + dot(s.att[layer].astype(BF16), s.wo[layer], TN)
        branch = tp_sum(branch, my_tp, layer, s)
        bias = vector(dense_bias_ref, layer) + vector(down_bias_ref, layer)
        residual = s.resid[layer] + branch + bias
        if layer + 1 < LAYERS:
            s.resid[layer + 1] = residual
        else:
            out_ref[...] = residual.astype(BF16)

    def attend_back(layer, of_query, own):
        for head in range(HEADS):
            rows = slice(HD * head, HD * head + HD)
            lanes = slice(128 * head, 128 * head + 128)
            s.pair[head, :HD, :ROWS] = s.q[layer, of_query, rows, :]
            s.pair[head, HD:, ROWS:] = s.mixed[layer, of_query, rows, :]
            both = dot(s.kv[layer, :, lanes], s.pair[head])
            stats = s.stats[layer, of_query]
            probs = jnp.exp(both[:, :ROWS] * SCALE - stats[head : head + 1, :])
            if own:
                probs = jnp.where(allowed_pairs(), probs, 0.0)
            scores = probs * (both[:, ROWS:] - stats[HEADS + head : HEADS + head + 1, :])
            scores = (scores * SCALE).astype(BF16)
            s.terms[:, lanes] += dot(
                jnp.concatenate([scores, probs.astype(BF16)], axis=1), s.pair[head], NT
            )
            back = dot(s.kv_t[layer, 128 * head : 128 * head + HD, :], scores)
            if own:
                s.query[rows, :] = back
            else:
                s.query_out[layer, of_query, rows, :] = back.astype(BF16)

    def backward(layer, between):
        low = s.grad[...].astype(BF16)
        own_mixed = dot(s.wo[layer], low, NT).astype(BF16)
        s.mixed[layer, group] = own_mixed
        s.stats[layer, group] = jnp.zeros((8, ROWS), F32)
        for head in range(HEADS):
            rows = slice(HD * head, HD * head + HD)
            delta = own_mixed[rows, :].astype(F32) * s.att[layer, rows, :]
            s.stats[layer, group, head : head + 1, :] = s.lse[layer, head : head + 1, :]
            s.stats[layer, group, HEADS + head : HEADS + head + 1, :] = jnp.sum(
                delta, axis=0, keepdims=True
            )

        @pl.loop(0, group)
        def _(target):
            for copy in mixed_copies(layer, group, target):
                copy.start()

        between(0)
        small = s.small.at[0]
        first = 8 * layer
        s.terms[...] = jnp.zeros_like(s.terms)
        small[first + 4 : first + 5, :] = jnp.sum(s.grad[...], axis=0, keepdims=True)
        hat, _ = centre(s.resid[layer])
        gain_one, gain_two = vector(g1_ref, layer), vector(g2_ref, layer)
        hidden_grad = dot(low, s.wd[layer], NT)
        pre = s.pre[layer]
        slope = 0.5 * (1.0 + lax.erf(pre * math.sqrt(0.5))) + pre * jnp.exp(
            -0.5 * pre * pre
        ) * (1.0 / math.sqrt(2.0 * math.pi))
        pre_grad = (hidden_grad * slope).astype(BF16)
        small[first + 6 : first + 7, :] = jnp.sum(pre_grad.astype(F32), axis=0, keepdims=True)
        normed_two = (hat * gain_two + vector(s2_ref, layer)).astype(BF16)
        s.ff[layer, :D, :] = dot(normed_two, pre_grad, TN).astype(BF16)
        s.ff[layer, D:, :] = dot(s.hid[layer], low, TN).astype(BF16)
        between(1)
        grad_two = dot(pre_grad, s.wu[layer], NT)
        small[first + 2 : first + 3, :] = jnp.sum(grad_two * hat, axis=0, keepdims=True)
        small[first + 3 : first + 4, :] = jnp.sum(grad_two, axis=0, keepdims=True)
        s.branch[...] = grad_two * gain_two
        between(2)

        @pl.loop(group + 1, GROUPS)
        def _(of_query):
            for copy in mixed_copies(layer, of_query, of_query):
                copy.wait_recv()
            attend_back(layer, of_query, False)
            query_copy(layer, of_query, group, of_query).start()

        between(3)
        attend_back(layer, group, True)
        s.low_terms[layer] = s.terms[...].astype(BF16)
        for step in range(1, RING):
            term_copy(layer, step).start()
        s.at[layer, QKV:, :] = dot(s.att[layer].astype(BF16), s.grad[...].astype(BF16)).astype(BF16)
        between(4)

        keys_values = s.terms[ring_part(0), :]
        for step in range(1, RING):
            term_copy(layer, step).wait_recv()
            keys_values = keys_values + s.term_slots[layer, step - 1].astype(F32)

        @pl.loop(0, group)
        def _(source):
            query_copy(layer, source, source, source).wait_recv()
            s.query[...] += s.query_in[layer, source].astype(F32)

        across = keys_values.T
        keys = jnp.concatenate(
            [across[128 * head : 128 * head + HD, :] for head in range(HEADS)], axis=0
        )
        s.merged_t[:WIDE, :] = rotated(s.query[...], rot_ref, -1.0).astype(BF16)
        s.merged_t[WIDE : 2 * WIDE, :] = rotated(keys, rot_ref, -1.0).astype(BF16)
        for head in range(HEADS):
            start = 2 * WIDE + HD * head
            s.merged_t[start : start + HD, :] = across[
                128 * head + HD : 128 * head + 128, :
            ].astype(BF16)
        merged = s.merged_t[...].T
        grad_one = dot(merged, s.wq[layer])
        hat, inverse = centre(s.resid[layer])

        def attention_weights():
            normed_one = (hat * gain_one + vector(s1_ref, layer)).astype(BF16)
            s.at[layer, :QKV, :] = dot(s.merged_t[...], normed_one).astype(BF16)

        if layer == 0:
            attention_weights()
        between(5)
        small[first : first + 1, :] = jnp.sum(grad_one * hat, axis=0, keepdims=True)
        small[first + 1 : first + 2, :] = jnp.sum(grad_one, axis=0, keepdims=True)
        small[first + 5 : first + 6, :] = jnp.zeros((1, D), F32)
        small[first + 5 : first + 6, :QKV] = jnp.sum(merged.astype(F32), axis=0, keepdims=True)
        small[first + 7 : first + 8, :] = jnp.zeros((1, D), F32)
        total = tp_sum(s.branch[...] + grad_one * gain_one, my_tp, LAYERS + layer, s, between)
        along = jnp.mean(total * hat, axis=-1, keepdims=True)
        level = jnp.mean(total, axis=-1, keepdims=True)
        grad = s.grad[...] + inverse * (total - level - hat * along)
        if layer > 0:
            s.grad[...] = grad
            attention_weights()
        else:
            in_grad_ref[...] = grad
        between(8)

    x, y = lax.rem(me // 4, 2), me // 8
    opposite = me + 4 - 8 * x
    z_axis = Axis(z, lambda place: me - z + place)
    y_axis = Axis(y, lambda place: me + (place - y) * 8)
    flows = {}
    per = len(flow_buffers(FF_ROWS))
    for layer in range(LAYERS):
        for kind, src, out in (("ff", s.ff, ff_out), ("at", s.at, at_out)):
            made = []
            for half in range(2):
                axes = (z_axis, y_axis) if half == 0 else (y_axis, z_axis)
                mine, flow_refs = flow_refs[:per], flow_refs[per:]
                made.append(Flow(axes, opposite, src.at[layer], out.at[layer], half, mine))
            flows[kind, layer] = made

    def advance(*which):
        for key in which:
            for one in flows[key]:
                one.advance()

    def between(layer):
        return lambda point: advance(*PLAN[layer].get(point, ()))

    s.resid[0] = x_ref[...].astype(F32)
    s.pair[...] = jnp.zeros_like(s.pair)
    for layer in range(LAYERS):
        forward(layer)
    s.grad[...] = out_grad_ref[...].astype(F32)
    backward(1, between(1))
    backward(0, between(0))

    z_peers = [z_axis.of_place(z_axis.at(step)) for step in (1, 2, 3)]
    y_peers = [y_axis.of_place(y_axis.at(step)) for step in (1, 2, 3)]
    stage_peers = (z_peers, y_peers, [opposite], tp_peers)
    places = (z, y, x, my_tp)

    def small_copies(stage):
        return [
            remote(
                s.small.at[stage],
                s.small_slots.at[stage, places[stage]],
                s.small_send.at[stage, step],
                s.small_recv.at[stage, step],
                **({"tp": peer} if stage == 3 else {"ctx": peer}),
            )
            for step, peer in enumerate(stage_peers[stage])
        ]

    def small_total(stage):
        for copy in small_copies(stage):
            copy.wait_recv()
        s.small_slots[stage, places[stage]] = s.small[stage]
        total = s.small_slots[stage, 0]
        for place in range(1, 2 if stage == 2 else 4):
            total = total + s.small_slots[stage, place]
        return total

    def small_step(number):
        if 0 < number < 4:
            s.small[number] = small_total(number - 1)
        if number < 4:
            for copy in small_copies(number):
                copy.start()
        elif number == 4:
            total, part = small_total(3), s.small[3]
            for layer in range(LAYERS):
                for row in range(4):
                    small_out[row, layer : layer + 1, :] = total[8 * layer + row : 8 * layer + row + 1, :]
                for row in (4, 6):
                    small_out[row, layer : layer + 1, :] = part[8 * layer + row : 8 * layer + row + 1, :]
                for row in (5, 7):
                    small_out[row, layer : layer + 1, :] = jnp.zeros((1, D), F32)
                for slot in range(3):
                    bqkv_out[slot, layer : layer + 1, :] = part[
                        8 * layer + 5 : 8 * layer + 6, WIDE * slot : WIDE * slot + WIDE
                    ]

    order = (AT0, FF0, AT1, FF1)
    for number in range(STEPS):
        small_step(number)
        advance(*order)

    for layer in range(LAYERS):
        for step in range(1, RING):
            kv_copy(layer, step, 0).wait_send()
            term_copy(layer, step).wait_send()

        @pl.loop(0, group)
        def _(target):
            q_copy(layer, target, group).wait_send()
            for copy in mixed_copies(layer, group, target):
                copy.wait_send()

        @pl.loop(group + 1, GROUPS)
        def _(of_query):
            query_copy(layer, of_query, group, of_query).wait_send()
            for copy in part_copies(layer, of_query, group, of_query):
                copy.wait_send()

    for key in order:
        for one in flows[key]:
            one.drain()
    for stage in range(4):
        for copy in small_copies(stage):
            copy.wait_send()


def vmem(count):
    return [pl.BlockSpec(memory_space=pltpu.VMEM)] * count


def hbm(count):
    return [pl.BlockSpec(memory_space=pl.ANY)] * count


def whole_step(*arrays):
    buffers = []
    for _ in range(LAYERS):
        for rows in (FF_ROWS, AT_ROWS):
            buffers += flow_buffers(rows) * 2
    return pl.pallas_call(
        step_kernel,
        name="training_step",
        out_shape=[
            jax.ShapeDtypeStruct((ROWS, D), BF16),
            jax.ShapeDtypeStruct((ROWS, D), F32),
            jax.ShapeDtypeStruct((LAYERS, FF_ROWS, D), BF16),
            jax.ShapeDtypeStruct((LAYERS, AT_ROWS, D), BF16),
            jax.ShapeDtypeStruct((8, LAYERS, D), F32),
            jax.ShapeDtypeStruct((3, LAYERS, WIDE), F32),
        ],
        in_specs=vmem(11) + hbm(4),
        out_specs=vmem(6),
        scratch_shapes=[*scratch().values(), *buffers],
        compiler_params=pltpu.CompilerParams(
            collective_id=0, has_side_effects=True, vmem_limit_bytes=60 << 20
        ),
    )(*arrays)


def on_device(
    layer_input,
    attention_gain,
    attention_shift,
    feedforward_gain,
    feedforward_shift,
    query_key_value_weight,
    query_key_value_bias,
    attention_out_weight,
    dense_bias,
    expand_weight,
    expand_bias,
    down_weight,
    down_bias,
    output_grad,
):
    me = lax.axis_index("ctx")
    positions = (me * ROWS + jnp.arange(ROWS, dtype=jnp.int32)).astype(F32)
    inverse = jnp.power(10000.0, -2.0 * jnp.arange(ROT // 2, dtype=F32) / ROT)
    angles = inverse[:, None] * positions[None, :]
    rot = jnp.stack([jnp.cos(angles), jnp.sin(angles)])
    output, grad, ff, at, small, bqkv = whole_step(
        layer_input[0],
        output_grad[0],
        attention_gain,
        attention_shift,
        feedforward_gain,
        feedforward_shift,
        query_key_value_bias.transpose(1, 0, 2),
        dense_bias,
        expand_bias,
        down_bias,
        rot,
        query_key_value_weight.transpose(0, 2, 3, 1).reshape(LAYERS, QKV, D),
        attention_out_weight,
        expand_weight,
        down_weight,
    )
    return (
        output[None],
        grad[None],
        small[0],
        small[1],
        small[2],
        small[3],
        at[:, :QKV].astype(F32).reshape(LAYERS, 3, WIDE, D).transpose(0, 3, 1, 2),
        bqkv.transpose(1, 0, 2),
        at[:, QKV:].astype(F32),
        small[4],
        ff[:, :D].astype(F32),
        small[6],
        ff[:, D:].astype(F32),
        small[4],
    )


def solution(mesh):
    in_specs = (
        P(None, "ctx", None),
        P(),
        P(),
        P(),
        P(),
        P(None, None, None, "tp"),
        P(None, None, "tp"),
        P(None, "tp", None),
        P(),
        P(None, None, "tp"),
        P(None, "tp"),
        P(None, "tp", None),
        P(),
        P(None, "ctx", None),
    )
    out_specs = (
        P(None, "ctx", None),
        P(None, "ctx", None),
        P(),
        P(),
        P(),
        P(),
        P(None, None, None, "tp"),
        P(None, None, "tp"),
        P(None, "tp", None),
        P(),
        P(None, None, "tp"),
        P(None, "tp"),
        P(None, "tp", None),
        P(),
    )
    return jax.shard_map(
        on_device, mesh=mesh, in_specs=in_specs, out_specs=out_specs, check_vma=False
    )
```
